32 devices in a mesh: dp: 16 (over z, x, core), tensor: 2 (over y).
Axes of the slice: x: 2, y: 2, z: 4, core: 2. Of those that a mesh axis runs over, the one named last changes fastest.
Arguments:
- tokens: bfloat16 [8192, 1024], P(('dp', 'tensor')), may hold values from -6 to 6
- time_index: int32 [64], P(('dp', 'tensor')), may hold values from 0 to 255
- time_table: float32 [256, 1024], replicated, may hold values from -1 to 1
- norm_gain: float32 [2, 2, 1024], replicated, may hold values from 0.5 to 1.5
- norm_bias: float32 [2, 2, 1024], replicated, may hold values from -1 to 1
- w_qkv: bfloat16 [2, 1024, 3, 1024], P(None, None, None, 'tensor'), may hold values from -0.1875 to 0.1875
- w_out: bfloat16 [2, 1024, 1024], P(None, 'tensor'), may hold values from -1 to 1
- w_up: bfloat16 [2, 1024, 4096], P(None, None, 'tensor'), may hold values from -0.1875 to 0.1875
- w_down: bfloat16 [2, 4096, 1024], P(None, 'tensor'), may hold values from -0.09375 to 0.09375
- time_weight: float32 [2, 1024], replicated, may hold values from -0.5 to 0.5
- cotangent: bfloat16 [8192, 1024], P(('dp', 'tensor')), may hold values from -6 to 6
Outputs:
- result: float32 [8192, 1024], P(('dp', 'tensor'))
- grad_tokens: float32 [8192, 1024], P(('dp', 'tensor'))
- grad_norm_gain: float32 [2, 2, 1024], replicated
- grad_norm_bias: float32 [2, 2, 1024], replicated
- grad_w_qkv: float32 [2, 1024, 3, 1024], P(None, None, None, 'tensor')
- grad_w_out: float32 [2, 1024, 1024], P(None, 'tensor')
- grad_w_up: float32 [2, 1024, 4096], P(None, None, 'tensor')
- grad_w_down: float32 [2, 4096, 1024], P(None, 'tensor')
- grad_time_weight: float32 [2, 1024], replicated
- grad_mlp_norm: float32 [2, 1024], replicated
The draws below stay inside these ranges and needn't reach their ends.
All inputs are finite; a program needn't handle non-finite values.
Results may differ from the reference program's by a relative error of at most 0.028.
Values may be sent and summed in bfloat16 or wider, within the bound.
No kernel may reach another device: no remote copies, remote signals or barrier semaphores. Data moves between devices by JAX's collectives and lax.ppermute only.
A program may use at most 192 MiB of HBM per device.

```python
import math
import jax
import jax.numpy as jnp
from jax import lax

D = 1024
HEADS = 16
HD = 64
FF = 4096
LAYERS = 2
SEQ_LEN = 128
NT = 256
SEQS = 64
TOKENS = 8192


def with_ends(array, key, low, high):
    shape = array.shape
    spot = [jax.random.randint(jax.random.fold_in(key, axis), (), 0, shape[axis]) for axis in range(len(shape))]
    array = array.at[tuple(spot)].set(low)
    longest = shape.index(max(shape))
    spot[longest] = (spot[longest] + 1) % shape[longest]
    return array.at[tuple(spot)].set(high)


def shard_levels(key, shape, split, least, top_value):
    factor_of, own = 1.0, jax.random.fold_in(key, 6)
    for dim, parts in split:
        heights = jnp.exp(jax.random.uniform(jax.random.fold_in(own, dim), (parts,), jnp.float32, least / len(split), top_value / len(split)))
        factor_of = factor_of * jnp.repeat(heights, shape[dim] // parts).reshape([-1 if axis == dim else 1 for axis in range(len(shape))])
    return factor_of


def gaussian(rng, extent, spread, most, cuts=(), held_as=jnp.bfloat16):
    level = shard_levels(rng, extent, cuts, -0.22, 0.18) if cuts else 1.0
    entries = jax.random.normal(rng, extent, jnp.float32) * spread * level
    return jnp.minimum(jnp.maximum(entries, -most), most).astype(held_as)


def setup_inputs(seed: int = 0) -> dict:
    streams_of = jax.random.split(jax.random.key(seed), 12)
    tokens = gaussian(streams_of[0], (TOKENS, D), 1.0, 6.0, ((0, 32),))
    time_index = with_ends(jax.random.randint(streams_of[1], (SEQS,), 0, NT), jax.random.fold_in(streams_of[1], 1), 0, NT - 1).astype(jnp.int32)
    time_table = jnp.clip(jax.random.uniform(streams_of[2], (NT, D), jnp.float32, -1.0, 1.0), -1.0, 1.0)
    norm_gain = jnp.clip(1.0 + 0.1 * jax.random.normal(streams_of[3], (LAYERS, 2, D), jnp.float32), 0.5, 1.5)
    norm_bias = gaussian(streams_of[4], (LAYERS, 2, D), 0.2, 1.0, (), jnp.float32)
    w_qkv = gaussian(streams_of[5], (LAYERS, D, 3, D), D ** -0.5, 0.1875, ((3, 2),))
    w_out = gaussian(streams_of[6], (LAYERS, D, D), (D // 32) ** -0.5, 1.0, ((1, 2),))
    w_up = gaussian(streams_of[7], (LAYERS, D, FF), D ** -0.5, 0.1875, ((2, 2),))
    w_down = gaussian(streams_of[8], (LAYERS, FF, D), FF ** -0.5, 0.09375, ((1, 2),))
    time_weight = jnp.clip(jax.random.uniform(streams_of[9], (LAYERS, D), jnp.float32, -0.5, 0.5), -0.5, 0.5)
    cotangent = gaussian(streams_of[10], (TOKENS, D), 1.0, 6.0, ((0, 32),))
    return {"tokens": tokens, "time_index": time_index, "time_table": time_table, "norm_gain": norm_gain, "norm_bias": norm_bias, "w_qkv": w_qkv, "w_out": w_out, "w_up": w_up, "w_down": w_down, "time_weight": time_weight, "cotangent": cotangent}


@jax.custom_vjp
def low(v):
    return lax.optimization_barrier(v.astype(jnp.bfloat16)).astype(jnp.float32)

@jax.custom_vjp
def low_back(v):
    return v

def low_keep(v):
    return (low(v), None)

def low_pass(kept, incoming_gradient):
    return (incoming_gradient,)

def back_keep(v):
    return (v, None)

def back_low(kept, incoming_gradient):
    return (low(incoming_gradient),)
low.defvjp(low_keep, low_pass)
low_back.defvjp(back_keep, back_low)

def gelu_tanh(u):
    return 0.5 * u * (1.0 + jnp.tanh(0.7978845608 * (u + 0.044715 * u * u * u)))

def layer_norm(v):
    centered = v - lax.optimization_barrier(jnp.mean(v, axis=-1, keepdims=True))
    return centered * lax.rsqrt(lax.optimization_barrier(jnp.mean(centered * centered, axis=-1, keepdims=True)) + 1e-05)

def rope_tables(length, head_size):
    half = head_size // 2
    freqs = jnp.exp(-math.log(10000.0) * jnp.arange(half, dtype=jnp.float32) * 2.0 / head_size)
    angles = jnp.arange(length, dtype=jnp.float32)[:, None] * freqs[None, :]
    angles = jnp.concatenate([angles, angles], axis=1)
    return (jnp.cos(angles), jnp.sin(angles))

def rotate_half(v):
    half = v.shape[-1] // 2
    return jnp.concatenate([-v[..., half:], v[..., :half]], axis=-1)

def rotate(v, cos_table, sin_table):
    return v * cos_table[None, :, None, :] + rotate_half(v) * sin_table[None, :, None, :]

def block_forward(x, time_seq, params):
    gains, biases, wqkv, wout, wup, wdown, tweight = params
    highest = lax.Precision.HIGHEST
    count = x.shape[0] // SEQ_LEN
    cos_table, sin_table = rope_tables(SEQ_LEN, HD)
    scale = HD ** (-0.5)
    time_rows = jnp.broadcast_to(time_seq[:, None, :], (count, SEQ_LEN, D)).reshape(count * SEQ_LEN, D)
    for layer in range(LAYERS):
        normed = low(layer_norm(x) * gains[layer, 0] + biases[layer, 0])
        proj = jnp.dot(normed, wqkv[layer].reshape(D, 3 * D), precision=highest)
        proj = proj.reshape(count, SEQ_LEN, 3, HEADS, HD)
        query = low(rotate(low_back(proj[:, :, 0]), cos_table, sin_table))
        keys = low(rotate(low_back(proj[:, :, 1]), cos_table, sin_table))
        values = low(low_back(proj[:, :, 2]))
        scores = low_back(jnp.einsum('sqhd,skhd->shqk', query, keys, precision=highest) * scale)
        top = lax.optimization_barrier(jnp.max(scores, axis=-1, keepdims=True))
        expo = jnp.exp(scores - top)
        probs = low(expo / lax.optimization_barrier(jnp.sum(expo, axis=-1, keepdims=True)))
        attended = jnp.einsum('shqk,skhd->sqhd', probs, values, precision=highest)
        attended = low(low_back(attended)).reshape(count * SEQ_LEN, D)
        x = x + low_back(jnp.dot(attended, wout[layer], precision=highest))
        normed = low(layer_norm(x) * gains[layer, 1] + biases[layer, 1])
        upper = low_back(jnp.dot(normed, wup[layer], precision=highest))
        hidden = low(gelu_tanh(upper))
        x = x + low_back(jnp.dot(hidden, wdown[layer], precision=highest))
        x = x * (1.0 + time_rows * tweight[layer])
    return x

def reference(tokens, time_index, time_table, norm_gain, norm_bias, w_qkv, w_out, w_up, w_down, time_weight, cotangent):
    block = math.gcd(SEQS, 32)
    blocks = SEQS // block
    params = (norm_gain, norm_bias, w_qkv.astype(jnp.float32), w_out.astype(jnp.float32), w_up.astype(jnp.float32), w_down.astype(jnp.float32), time_weight)
    time_seq = time_table[time_index.astype(jnp.int32)]

    def forward(x, weights):
        pieces = x.reshape(blocks, block * SEQ_LEN, D)
        times = time_seq.reshape(blocks, block, D)
        step = jax.checkpoint(lambda pair: block_forward(pair[0], pair[1], weights))
        return lax.map(step, (pieces, times)).reshape(TOKENS, D)
    result, pull = jax.vjp(forward, tokens.astype(jnp.float32), params)
    grad_tokens, grads = pull(cotangent.astype(jnp.float32))
    mlp_norm = jnp.stack([grads[0][LAYERS - 1, 1], grads[1][LAYERS - 1, 1]], axis=0)
    return (result, grad_tokens, grads[0], grads[1], grads[2], grads[3], grads[4], grads[5], grads[6], mlp_norm)
```

```python
import math

import jax
import jax.numpy as jnp
from jax import lax
from jax.experimental import pallas as pl
from jax.experimental.pallas import tpu as pltpu
from jax.sharding import PartitionSpec as P

HD = 64
bf16 = jnp.bfloat16
f32 = jnp.float32
epsilon = 1e-05


def mm(a, b):
    return jnp.dot(a, b, preferred_element_type=f32)


def mm_t(a, b):
    return lax.dot_general(a, b, (((1,), (1,)), ((), ())), preferred_element_type=f32)


def across(a, b):
    return lax.dot_general(a, b, (((0,), (0,)), ((), ())), preferred_element_type=f32)


def ein(spec, a, b):
    return jnp.einsum(spec, a, b, preferred_element_type=f32)


def gelu_parts(u):
    inner = 0.7978845608 * (u + 0.044715 * u * u * u)
    th = jnp.tanh(inner)
    half = 0.5 * (1.0 + th)
    slope = half + 0.5 * u * (1.0 - th * th) * (0.7978845608 + 3.0 * 0.7978845608 * 0.044715 * u * u)
    return u * half, slope


def standardize(v):
    centered = v - jnp.mean(v, axis=-1, keepdims=True)
    inverse = lax.rsqrt(jnp.mean(centered * centered, axis=-1, keepdims=True) + epsilon)
    return centered * inverse, inverse


def norm_backward(grad, xhat, inverse, gain):
    e = grad * gain
    return inverse * (
        e
        - jnp.mean(e, axis=-1, keepdims=True)
        - xhat * jnp.mean(e * xhat, axis=-1, keepdims=True)
    )


CHUNK = 32
BLOCK = 256


def rope_tables(length, width):
    half = HD // 2
    freqs = jnp.exp(-math.log(10000.0) * jnp.arange(half, dtype=f32) * 2.0 / HD)
    angles = jnp.arange(length, dtype=f32)[:, None] * freqs[None, :]
    heads = width // HD
    cos = jnp.tile(jnp.cos(angles), (1, 2 * heads))
    sin = jnp.tile(jnp.concatenate([-jnp.sin(angles), jnp.sin(angles)], axis=1), (1, heads))
    return cos, sin


def partner(u):
    width = u.shape[1]
    lane = lax.broadcasted_iota(jnp.int32, u.shape, 1)
    low = (lane & (HD - 1)) < HD // 2
    return jnp.where(low, pltpu.roll(u, width - HD // 2, 1), pltpu.roll(u, HD // 2, 1))


def chunks(rows, body, start=0):
    def step(i, carry):
        body(pl.multiple_of(i * CHUNK, CHUNK))
        return carry

    lax.fori_loop(start // CHUNK, rows // CHUNK, step, 0)


def rows_at(at):
    return pl.ds(at, CHUNK)


def other_rows(at, rows, swapped):
    if not swapped:
        return rows_at(at)
    half = rows // 2
    return rows_at(pl.multiple_of(jnp.where(at < half, at + half, at - half), CHUNK))


def fold(v):
    return jnp.sum(v.reshape(-1, 8, v.shape[-1]), axis=0)


LIMIT = 18 * 2**20


def call(kernel, ins, outs, scratch, flops, name, aliases={}):
    vmem = pl.BlockSpec(memory_space=pltpu.VMEM)
    far = pl.BlockSpec(memory_space=pltpu.HBM)
    smem = pl.BlockSpec(memory_space=pltpu.SMEM)
    spec = lambda a, away: smem if a.dtype == jnp.int32 else far if away else vmem
    return pl.pallas_call(
        kernel,
        out_shape=[jax.ShapeDtypeStruct(s, d) for s, d, _ in outs],
        in_specs=[spec(a, away) for a, away in ins],
        out_specs=[far if away else vmem for _, _, away in outs],
        scratch_shapes=scratch,
        input_output_aliases=aliases,
        compiler_params=pltpu.CompilerParams(vmem_limit_bytes=LIMIT),
        cost_estimate=pl.CostEstimate(flops=flops, bytes_accessed=2**20, transcendentals=0),
        name=name,
    )(*[a for a, _ in ins])


def masks():
    lane = lax.broadcasted_iota(jnp.int32, (1, 2 * HD), 1)
    return lane < HD


def both_heads(v, low):
    zero = jnp.zeros_like(v)
    return jnp.concatenate([jnp.where(low, v, zero), jnp.where(low, zero, v)], axis=0)


def softmax(scores):
    top = jnp.max(scores, axis=-1, keepdims=True)
    e = jnp.exp(scores - top)
    return e / jnp.sum(e, axis=-1, keepdims=True)


def forward_attention(layer, part_index, length, swapped, head, tau, time_weight, gain, bias, w_qkv, w_out, tables):
    first = layer == 0
    rows = sum(n for _, _, n in head) if first else head[0].shape[0]
    width = w_out.shape[2]
    local = w_out.shape[1]
    block = min(BLOCK, local)
    scale = HD ** (-0.5)
    seqs = rows // length
    parts = tau.shape[0] // seqs

    def kernel(*refs):
        it = iter(refs)
        take = lambda n: [next(it) for _ in range(n)]
        head_refs = take(len(head))
        tau_ref, tw_ref, gain_ref, bias_ref, wq_any, wo_any, cos_ref, sin_ref = take(8)
        if not first:
            x2_ref, = take(1)
        x_ref, n_ref, q_ref, k_ref, v_ref, att_ref, part_ref = take(7)
        wq, wo, sems = take(3)
        copies = [pltpu.make_async_copy(wq_any.at[layer, j], wq.at[j], sems.at[j]) for j in range(3)]
        copies.append(pltpu.make_async_copy(wo_any.at[layer], wo, sems.at[3]))
        for c in copies:
            c.start()

        def norm(at, x):
            x_ref[rows_at(at), :] = x
            xhat, _ = standardize(x)
            n_ref[rows_at(at), :] = (xhat * gain_ref[layer, 0:1, :] + bias_ref[layer, 0:1, :]).astype(bf16)

        if first:
            low = 0
            for ref, (_, begin, count) in zip(head_refs, head):
                chunks(
                    low + count,
                    lambda at, ref=ref, shift=begin - low: norm(
                        at, ref[rows_at(pl.multiple_of(at + shift, CHUNK)), :].astype(f32)
                    ),
                    low,
                )
                low += count
        else:
            x1, own, got = head_refs

            def scaled(at):
                here = rows_at(at)
                there = other_rows(at, rows, swapped)
                x2 = x1[here, :] + own[here, :].astype(f32) + got[there, :].astype(f32)
                x2_ref[here, :] = x2
                t = tau_ref[pl.ds(at // length * parts + part_index, 1), :]
                norm(at, x2 * (1.0 + t * tw_ref[layer - 1 : layer, :]))

            chunks(rows, scaled)
        for j, out in enumerate((q_ref, k_ref, v_ref)):
            copies[j].wait()
            for b in range(0, local, block):
                u = mm(n_ref[...], wq[j, :, b : b + block])
                if j < 2:
                    for s in range(0, rows, length):
                        us = u[s : s + length]
                        us = us * cos_ref[:, b : b + block] + partner(us) * sin_ref[:, b : b + block]
                        out[s : s + length, b : b + block] = us.astype(bf16)
                else:
                    out[:, b : b + block] = u.astype(bf16)
        low = masks()
        for s in range(0, rows, length):
            for b in range(0, local, 2 * HD):
                here = (slice(s, s + length), slice(b, b + 2 * HD))
                q2 = both_heads(q_ref[here], low)
                probs = softmax(mm_t(q2, k_ref[here]) * scale).astype(bf16)
                o = mm(probs, v_ref[here])
                att_ref[here] = jnp.where(low, o[:length], o[length:]).astype(bf16)
        copies[3].wait()
        for b in range(0, width, BLOCK):
            part_ref[:, b : b + BLOCK] = mm(att_ref[...], wo[:, b : b + BLOCK]).astype(bf16)

    ins = [(a[0] if first else a, False) for a in head]
    ins += [(a, False) for a in (tau, time_weight, gain, bias)] + [(w_qkv, True), (w_out, True)]
    ins += [(t, False) for t in tables]
    near = lambda n, d: ((rows, n), d, False)
    outs = [] if first else [near(width, f32)]
    outs += [near(width, f32), near(width, bf16)] + [near(local, bf16)] * 4 + [near(width, bf16)]
    scratch = [
        pltpu.VMEM((3, width, local), bf16),
        pltpu.VMEM((local, width), bf16),
        pltpu.SemaphoreType.DMA((4,)),
    ]
    return call(kernel, ins, outs, scratch, 4 * 10**9, "forward_attention")


def forward_mlp(layer, swapped, x, own, got, gain, bias, w_up, w_down):
    rows, width = x.shape
    hidden = w_up.shape[2]
    tiles = hidden // BLOCK

    def kernel(x_ref, own_ref, got_ref, gain_ref, bias_ref, wu_any, wd_any,
               x1_ref, n_ref, h_ref, slope_ref, part_ref, wu, wd, sems):
        ups = [
            pltpu.make_async_copy(
                wu_any.at[layer, :, pl.ds(t * BLOCK, BLOCK)], wu.at[t], sems.at[t]
            )
            for t in range(tiles)
        ]
        down = pltpu.make_async_copy(wd_any.at[layer], wd, sems.at[tiles])
        for c in ups:
            c.start()
        down.start()

        def norm(at):
            here = rows_at(at)
            there = other_rows(at, rows, swapped)
            x1 = x_ref[here, :] + own_ref[here, :].astype(f32) + got_ref[there, :].astype(f32)
            x1_ref[here, :] = x1
            xhat, _ = standardize(x1)
            n_ref[here, :] = (xhat * gain_ref[layer, 1:2, :] + bias_ref[layer, 1:2, :]).astype(bf16)

        chunks(rows, norm)
        for t in range(tiles):
            ups[t].wait()
            value, slope = gelu_parts(mm(n_ref[...], wu[t]))
            h_ref[:, t * BLOCK : (t + 1) * BLOCK] = value.astype(bf16)
            slope_ref[:, t * BLOCK : (t + 1) * BLOCK] = slope.astype(bf16)
        down.wait()
        for b in range(0, width, BLOCK):
            part_ref[:, b : b + BLOCK] = mm(h_ref[...], wd[:, b : b + BLOCK]).astype(bf16)

    ins = [(a, False) for a in (x, own, got, gain, bias)] + [(w_up, True), (w_down, True)]
    near = lambda n, d: ((rows, n), d, False)
    outs = [near(width, f32), near(width, bf16), near(hidden, bf16), near(hidden, bf16), near(width, bf16)]
    scratch = [
        pltpu.VMEM((tiles, width, BLOCK), bf16),
        pltpu.VMEM((hidden, width), bf16),
        pltpu.SemaphoreType.DMA((tiles + 1,)),
    ]
    return call(kernel, ins, outs, scratch, 6 * 10**9, "forward_mlp")


def backward_mlp(layer, part_index, length, swapped, head, x2, tau, time_weight, gain, slope, w_up, w_down):
    last = layer == gain.shape[0] - 1
    rows, width = x2.shape
    hidden = w_up.shape[2]
    tiles = hidden // BLOCK
    seqs = rows // length
    parts = tau.shape[0] // seqs

    def kernel(*refs):
        it = iter(refs)
        take = lambda n: [next(it) for _ in range(n)]
        head_refs = take(len(head))
        x2_ref, tau_ref, tw_ref, gain_ref, slope_ref, wu_any, wd_any = take(7)
        g2_ref, gm_ref, du_ref, part_ref, sums_ref = take(5)
        wu, wd, sems = take(3)
        downs = [
            pltpu.make_async_copy(
                wd_any.at[layer, pl.ds(t * BLOCK, BLOCK), :], wd.at[t], sems.at[t]
            )
            for t in range(tiles)
        ]
        up = pltpu.make_async_copy(wu_any.at[layer], wu, sems.at[tiles])
        for c in downs:
            c.start()
        up.start()
        sums_ref[...] = jnp.zeros_like(sums_ref)

        def begin(at, g):
            here = rows_at(at)
            t = tau_ref[pl.ds(at // length * parts + part_index, 1), :]
            sums_ref[16:24, :] += fold(g * x2_ref[here, :]) * t
            g2 = g * (1.0 + t * tw_ref[layer : layer + 1, :])
            g2_ref[here, :] = g2
            gm_ref[here, :] = g2.astype(bf16)

        if last:
            low = 0
            for ref, (_, start, count) in zip(head_refs, head):
                chunks(
                    low + count,
                    lambda at, ref=ref, shift=start - low: begin(
                        at, ref[rows_at(pl.multiple_of(at + shift, CHUNK)), :].astype(f32)
                    ),
                    low,
                )
                low += count
        else:
            g1, x, own, got = head_refs

            def through_norm(at):
                here = rows_at(at)
                dn = own[here, :].astype(f32) + got[other_rows(at, rows, swapped), :].astype(f32)
                xhat, inverse = standardize(x[here, :])
                sums_ref[0:8, :] += fold(dn * xhat)
                sums_ref[8:16, :] += fold(dn)
                begin(at, g1[here, :] + norm_backward(dn, xhat, inverse, gain_ref[layer + 1, 0:1, :]))

            chunks(rows, through_norm)
        for t in range(tiles):
            downs[t].wait()
            at = slice(t * BLOCK, (t + 1) * BLOCK)
            dh = mm_t(gm_ref[...], wd[t])
            du_ref[:, at] = (dh * slope_ref[:, at].astype(f32)).astype(bf16)
        up.wait()
        for b in range(0, width, BLOCK):
            part_ref[:, b : b + BLOCK] = mm_t(du_ref[...], wu[b : b + BLOCK, :]).astype(bf16)

    ins = [(a[0] if last else a, False) for a in head]
    ins += [(a, False) for a in (x2, tau, time_weight, gain, slope)]
    ins += [(w_up, True), (w_down, True)]
    near = lambda n, d: ((rows, n), d, False)
    outs = [near(width, f32), near(width, bf16), near(hidden, bf16), near(width, bf16)]
    outs += [((24, width), f32, False)]
    scratch = [
        pltpu.VMEM((width, hidden), bf16),
        pltpu.VMEM((tiles, BLOCK, width), bf16),
        pltpu.SemaphoreType.DMA((tiles + 1,)),
    ]
    return call(kernel, ins, outs, scratch, 6 * 10**9, "backward_mlp")


def backward_attention(layer, length, swapped, g2, x1, own, got, gain, q, k, v, w_qkv, w_out, tables):
    rows, width = x1.shape
    local = w_out.shape[1]
    block = min(BLOCK, local)
    scale = HD ** (-0.5)

    def kernel(g2_ref, x1_ref, own_ref, got_ref, gain_ref, q_ref, k_ref, v_ref, wq_any, wo_any, cos_ref, sin_ref,
               g1_ref, ga_ref, dq_ref, dk_ref, dv_ref, part_ref, sums_ref, wq, wo, do_ref, sems):
        copies = [pltpu.make_async_copy(wo_any.at[layer], wo, sems.at[3])]
        copies += [pltpu.make_async_copy(wq_any.at[layer, j], wq.at[j], sems.at[j]) for j in range(3)]
        for c in copies:
            c.start()
        sums_ref[...] = jnp.zeros_like(sums_ref)

        def begin(at):
            here = rows_at(at)
            dn = own_ref[here, :].astype(f32) + got_ref[other_rows(at, rows, swapped), :].astype(f32)
            xhat, inverse = standardize(x1_ref[here, :])
            sums_ref[0:8, :] += fold(dn * xhat)
            sums_ref[8:16, :] += fold(dn)
            g1 = g2_ref[here, :] + norm_backward(dn, xhat, inverse, gain_ref[layer, 1:2, :])
            g1_ref[here, :] = g1
            ga_ref[here, :] = g1.astype(bf16)

        chunks(rows, begin)
        copies[0].wait()
        for b in range(0, local, block):
            do_ref[:, b : b + block] = mm_t(ga_ref[...], wo[b : b + block, :]).astype(bf16)
        low = masks()
        for s in range(0, rows, length):
            for b in range(0, local, 2 * HD):
                here = (slice(s, s + length), slice(b, b + 2 * HD))
                lanes = slice(b, b + 2 * HD)
                keys = k_ref[here]
                q2 = both_heads(q_ref[here], low)
                do2 = both_heads(do_ref[here], low)
                probs = softmax(mm_t(q2, keys) * scale)
                dp = mm_t(do2, v_ref[here])
                ds = probs * (dp - jnp.sum(probs * dp, axis=-1, keepdims=True))
                ds = ds.astype(bf16)
                dv_ref[here] = across(probs.astype(bf16), do2).astype(bf16)
                dq = mm(ds, keys) * scale
                dq = jnp.where(low, dq[:length], dq[length:])
                dk = across(ds, q2) * scale
                for d, out in ((dq, dq_ref), (dk, dk_ref)):
                    out[here] = (d * cos_ref[:, lanes] + partner(d * sin_ref[:, lanes])).astype(bf16)
        for c in copies[1:]:
            c.wait()
        for b in range(0, width, BLOCK):
            at = slice(b, b + BLOCK)
            part = mm_t(dq_ref[...], wq[0, at, :]) + mm_t(dk_ref[...], wq[1, at, :])
            part_ref[:, at] = (part + mm_t(dv_ref[...], wq[2, at, :])).astype(bf16)

    ins = [(a, False) for a in (g2, x1, own, got, gain, q, k, v)] + [(w_qkv, True), (w_out, True)]
    ins += [(t, False) for t in tables]
    near = lambda n, d: ((rows, n), d, False)
    outs = [near(width, f32), near(width, bf16)] + [near(local, bf16)] * 3
    outs += [near(width, bf16), ((16, width), f32, False)]
    scratch = [
        pltpu.VMEM((3, width, local), bf16),
        pltpu.VMEM((local, width), bf16),
        pltpu.VMEM((rows, local), bf16),
        pltpu.SemaphoreType.DMA((4,)),
    ]
    return call(kernel, ins, outs, scratch, 7 * 10**9, "backward_attention")


class Links:
    def __init__(self, dp, tensor):
        self.dp, self.tensor = dp, tensor
        self.chips = dp // 2
        self.ring = dp == 16
        self.walk = [0, 2, 4, 6, 7, 5, 3, 1]
        place = [self.walk.index(i) for i in range(8)]
        self.place = place
        self.ring_pairs = []
        for k in range(8):
            here, there = self.walk[k], self.walk[(k + 1) % 8]
            self.ring_pairs.append((2 * here, 2 * there))
            self.ring_pairs.append((2 * there + 1, 2 * here + 1))
        self.core_pairs = [(i, i ^ 1) for i in range(dp)]

    def ring_place(self):
        i = lax.axis_index("dp")
        p = jnp.asarray(self.place, jnp.int32)[i >> 1]
        return jnp.where(i & 1 == 0, p, (8 - p) % 8)

    def swap_tensor(self, v):
        return lax.ppermute(v, "tensor", [(0, 1), (1, 0)])

    def gather_tensor(self, v):
        if self.tensor != 2:
            return lax.all_gather(v, "tensor", axis=0, tiled=True)
        other = self.swap_tensor(v)
        first = lax.axis_index("tensor") == 0
        return jnp.concatenate([jnp.where(first, v, other), jnp.where(first, other, v)])

    def start_sum(self, part):
        part = part.astype(bf16)
        if self.tensor != 2:
            summed = lax.psum(part, "tensor")
            return (summed, jnp.zeros_like(summed))
        return (part, self.swap_tensor(part))

    def sum_small(self, v):
        if self.dp & (self.dp - 1):
            return lax.psum(v, "dp")
        mask = 1
        while mask < self.dp:
            v = v + lax.ppermute(v, "dp", [(i, i ^ mask) for i in range(self.dp)])
            mask *= 2
        return v


def total(parts):
    out = parts[0].astype(f32)
    for p in parts[1:]:
        out = out + p.astype(f32)
    return out


def over_rows(lefts, rights):
    out = across(lefts[0], rights[0])
    for a, b in zip(lefts[1:], rights[1:]):
        out = out + across(a, b)
    return out


def mlp_gradients(h, gm, n2, du, core, place):
    n = len(h)
    hidden, width = h[0].shape[1], gm[0].shape[1]
    half_hidden = hidden // 2
    tall = half_hidden // 8
    wide = width // 8

    def kernel(s_ref, *refs):
        hs, gms, ns, dus = [refs[n * j : n * j + n] for j in range(4)]
        for target, half, p in (
            (refs[4 * n], 1 - s_ref[0], lax.rem(8 - s_ref[1], 8)),
            (refs[4 * n + 1], s_ref[0], s_ref[1]),
        ):
            for j in range(4):
                first = pl.multiple_of(half * half_hidden + j * 2 * tall, 2 * tall)
                down = over_rows([r[:, pl.ds(first, 2 * tall)] for r in hs], [r[...] for r in gms])
                columns = pl.ds(pl.multiple_of(half * half_hidden, half_hidden), half_hidden)
                up = over_rows(
                    [r[:, j * 2 * wide : (j + 1) * 2 * wide] for r in ns], [r[:, columns] for r in dus]
                )
                for i in range(2):
                    slot = lax.rem(p - (2 * j + i) + 8, 8)
                    target[slot, 0:tall, :] = down[i * tall : (i + 1) * tall].astype(bf16)
                    target[slot, tall : tall + wide, :] = up[i * wide : (i + 1) * wide].astype(bf16)

    ins = [(jnp.stack([core, place]).astype(jnp.int32), False)]
    ins += [(v, False) for group in (h, gm, n2, du) for v in group]
    out = ((8, tall + wide, width), bf16, False)
    return call(kernel, ins, [out, out], [], 9 * 10**9, "mlp_gradients")


def attention_gradients(att, ga, n1, dq, dk, dv, core, place):
    n = len(att)
    local, width = att[0].shape[1], ga[0].shape[1]
    heads, wide = local // 2, width // 2

    def kernel(s_ref, *refs):
        atts, gas, ns = [refs[n * j : n * j + n] for j in range(3)]
        dps = [refs[n * j : n * j + n] for j in range(3, 6)]
        for target, half, p in (
            (refs[6 * n], 1 - s_ref[0], lax.rem(8 - s_ref[1], 8)),
            (refs[6 * n + 1], s_ref[0], s_ref[1]),
        ):

            def put(value, low, size):
                for b in range(8):
                    slot = lax.rem(p - b + 8, 8)
                    target[slot, low : low + size, :] = value[b * size : (b + 1) * size].astype(bf16)

            lefts = [r[:, pl.ds(pl.multiple_of(half * heads, heads), heads)] for r in atts]
            for j in range(2):
                put(over_rows(lefts, [r[:, j * wide : (j + 1) * wide] for r in gas]), heads // 8 * j, heads // 8)
            lefts = [r[:, pl.ds(pl.multiple_of(half * wide, wide), wide)] for r in ns]
            for j in range(3):
                put(over_rows(lefts, [r[...] for r in dps[j]]), heads // 4 + wide // 8 * j, wide // 8)

    ins = [(jnp.stack([core, place]).astype(jnp.int32), False)]
    ins += [(v, False) for group in (att, ga, n1, dq, dk, dv) for v in group]
    out = ((8, heads // 4 + 3 * wide // 8, local), bf16, False)
    return call(kernel, ins, [out, out], [], 5 * 10**9, "attention_gradients")


def pack(blocks):
    def kernel(*refs):
        for i, r in enumerate(refs[:-1]):
            refs[-1][i] = r[...]

    out = ((len(blocks),) + blocks[0].shape, bf16, False)
    return call(kernel, [(v, False) for v in blocks], [out], [], 10**9, "pack")[0]


DEEP = 4


def spread(pieces, shapes, mine, peer, core, place, before):
    depth, width = mine.shape[1:]

    def kernel(s_ref, mine_ref, peer_ref, *refs):
        held, sems = refs[-2:]
        outs = refs[len(refs) - 2 - len(shapes) : -2]

        def copies(i):
            half, p = (s_ref[0], s_ref[1]) if i < 8 else (1 - s_ref[0], lax.rem(8 - s_ref[1], 8))
            b = lax.rem(p + 1 - i % 8 + 8, 8)
            return [
                pltpu.make_async_copy(
                    held.at[(i % DEEP,) + source], outs[o].at[place], sems.at[i % DEEP, j]
                )
                for j, (source, o, place) in enumerate(pieces(half, b))
            ]

        for i in range(16):
            if i >= DEEP:
                for c in copies(i - DEEP):
                    c.wait()
            held[i % DEEP] = (mine_ref if i < 8 else peer_ref)[i % 8].astype(f32)
            for c in copies(i):
                c.start()
        for i in range(16 - DEEP, 16):
            for c in copies(i):
                c.wait()

    ins = [(jnp.stack([core, place]).astype(jnp.int32), False), (mine, False), (peer, False)]
    aliases = {}
    if before is not None:
        for j, v in enumerate(before):
            aliases[len(ins)] = j
            ins.append((v, True))
    scratch = [
        pltpu.VMEM((DEEP, depth, width), f32),
        pltpu.SemaphoreType.DMA((DEEP, len(pieces(0, 0)))),
    ]
    outs = [(s, f32, True) for s in shapes]
    return call(kernel, ins, outs, scratch, 5 * 10**9, "spread", aliases)


def mlp_pieces(layer, layers, hidden, width):
    tall, wide = hidden // 16, width // 8

    def pieces(half, b):
        rows = pl.ds(pl.multiple_of(half * (hidden // 2) + b * tall, tall), tall)
        across_rows = pl.ds(pl.multiple_of(b * wide, wide), wide)
        columns = pl.ds(pl.multiple_of(half * (hidden // 2), hidden // 2), hidden // 2)
        return [
            ((slice(0, tall), slice(None)), 0, (layer, rows, slice(None))),
            ((slice(tall, tall + wide), slice(None)), 1, (layer, across_rows, columns)),
        ]

    return pieces, [(layers, hidden, width), (layers, width, hidden)]


def attention_pieces(layer, layers, local, width):
    tall, wide = local // 16, width // 16

    def pieces(half, b):
        rows = pl.ds(pl.multiple_of(half * (local // 2) + b * tall, tall), tall)
        deep = pl.ds(pl.multiple_of(half * (width // 2) + b * wide, wide), wide)
        out = []
        for j in range(2):
            columns = slice(j * width // 2, (j + 1) * width // 2)
            out.append(((slice(tall * j, tall * (j + 1)), slice(None)), 0, (layer, rows, columns)))
        for j in range(3):
            low = 2 * tall + wide * j
            out.append(((slice(low, low + wide), slice(None)), 1, (layer, j, deep, slice(None))))
        return out

    return pieces, [(layers, local, width), (layers, 3, width, local)]


class Stream:
    def __init__(self, links, kind, layer, layers, groups):
        self.links = links
        self.steps = 0
        self.core = lax.axis_index("dp") & 1
        self.p = links.ring_place()
        if kind == "mlp":
            send, self.keep = mlp_gradients(*groups, self.core, self.p)
            self.layout = mlp_pieces(layer, layers, groups[0][0].shape[1], groups[1][0].shape[1])
        else:
            send, self.keep = attention_gradients(*groups, self.core, self.p)
            self.layout = attention_pieces(layer, layers, groups[0][0].shape[1], groups[1][0].shape[1])
        self.got = lax.ppermute(send, "dp", links.core_pairs)
        self.cur = None
        self.done = []

    def step(self):
        if self.steps >= 14:
            return
        if self.cur is None:
            self.cur = (self.keep[0].astype(f32) + self.got[0].astype(f32)).astype(bf16)
        got = lax.ppermute(self.cur, "dp", self.links.ring_pairs)
        self.steps += 1
        if self.steps < 8:
            i = self.steps
            got = got.astype(f32) + self.keep[i].astype(f32) + self.got[i].astype(f32)
            got = got.astype(bf16)
        self.cur = got
        if self.steps >= 7:
            self.done.append(got)

    def state(self):
        return (self.keep, self.got) if self.cur is None else (self.cur,)

    def set_state(self, st):
        if self.cur is None:
            self.keep, self.got = st
        else:
            self.cur, = st
            if self.done:
                self.done[-1] = self.cur

    def finish(self, before):
        while self.steps < 14:
            self.step()
        mine = pack(self.done)
        peer = lax.ppermute(mine, "dp", self.links.core_pairs)
        return spread(*self.layout, mine, peer, self.core, self.p, before)


class Plain:
    def __init__(self, links, kind, layer, layers, groups):
        self.layer, self.layers, self.steps = layer, layers, 14
        left, right, deep, *dps = [jnp.concatenate(g) for g in groups]
        out = [ein("ra,rb->ab", left, right)]
        if kind == "mlp":
            out.append(ein("ra,rb->ab", deep, dps[0]))
        else:
            out.append(jnp.stack([ein("ra,rb->ab", deep, d) for d in dps]))
        self.out = [lax.psum(v.astype(bf16), "dp").astype(f32) for v in out]

    def step(self):
        pass

    def state(self):
        return ()

    def set_state(self, st):
        pass

    def finish(self, before):
        if before is None:
            before = [jnp.zeros((self.layers,) + v.shape, f32) for v in self.out]
        return [b.at[self.layer].set(v) for b, v in zip(before, self.out)]


def make_local(links):
    def local(
        tokens,
        time_index,
        time_table,
        norm_gain,
        norm_bias,
        w_qkv,
        w_out,
        w_up,
        w_down,
        time_weight,
        cotangent,
    ):
        rows, width = tokens.shape
        seq_here = time_index.shape[0]
        length = rows // seq_here
        layers = norm_gain.shape[0]
        local_width = w_out.shape[1]
        tables = rope_tables(length, local_width)
        parts = 2 if seq_here % 2 == 0 else 1
        own = rows // parts
        paired = links.tensor == 2
        wq = jnp.transpose(w_qkv, (0, 2, 1, 3))

        def group_rows(v, m):
            if paired:
                got = links.swap_tensor(v[m * own : (m + 1) * own])
                return [(v, m * own, own), (got, 0, own)]
            v = links.gather_tensor(v[m * own : (m + 1) * own])
            return [(v, 0, v.shape[0])]

        heads = [group_rows(tokens, m) for m in range(parts)]
        if paired:
            index = jnp.concatenate([time_index, links.swap_tensor(time_index)])
        else:
            index = links.gather_tensor(time_index)
        onehot = (index[:, None] == jnp.arange(time_table.shape[0], dtype=jnp.int32)[None, :]).astype(f32)
        tau = jnp.dot(onehot, time_table, precision=lax.Precision.HIGHEST)
        saved = [[None] * parts for _ in range(layers)]
        after = [[None] * parts for _ in range(layers)]
        for l in range(layers):
            for m in range(parts):
                out = forward_attention(
                    l, m, length, paired, heads[m], tau, time_weight, norm_gain, norm_bias, wq, w_out, tables
                )
                if l > 0:
                    after[l - 1][m], out = out[0], out[1:]
                x, n1, q, k, v, att, part = out
                saved[l][m] = [x, n1, q, k, v, att, links.start_sum(part)]
            for m in range(parts):
                x, n1, q, k, v, att, summed = saved[l][m]
                x1, n2, h, slope, part = forward_mlp(
                    l, paired, x, *summed, norm_gain, norm_bias, w_up, w_down
                )
                saved[l][m] = (x, n1, q, k, v, att, x1, n2, h, slope)
                heads[m] = (x1, *links.start_sum(part))
        gs = [group_rows(cotangent, m) for m in range(parts)]

        def meet(v):
            return jnp.roll(v, v.shape[0] // 2, axis=0) if paired else v

        result = []
        for m in range(parts):
            x1, mine_part, got = heads[m]
            x2 = x1 + mine_part.astype(f32) + meet(got).astype(f32)
            after[layers - 1][m] = x2
            t = tau.reshape(-1, parts, 1, width)[:, m]
            scaled = x2.reshape(-1, length, width) * (1.0 + t * time_weight[layers - 1])
            result.append(scaled.reshape(x2.shape))
        kind = Stream if links.ring else Plain
        small = [[0.0] * 5 for _ in range(layers)]
        streams = []

        def add_sums(l, first, sums):
            for j in range(sums.shape[0] // 8):
                small[l][first[j]] += jnp.sum(sums[8 * j : 8 * j + 8], axis=0)

        keep = lambda l, i: [s[i] for s in saved[l]]

        def sync(live):
            going = [s for s in streams if s.steps < 14]
            for s in going:
                s.step()
            leaves, tree = jax.tree.flatten(live)
            arrays = [i for i, v in enumerate(leaves) if not isinstance(v, int)]
            held, states = lax.optimization_barrier(([leaves[i] for i in arrays], [s.state() for s in going]))
            for s, st in zip(going, states):
                s.set_state(st)
            for i, v in zip(arrays, held):
                leaves[i] = v
            return jax.tree.unflatten(tree, leaves)

        for l in reversed(range(layers)):
            g2s, gms, dus, sums = [None] * parts, [None] * parts, [None] * parts, [None] * parts
            for m in range(parts):
                g2, gm, du, part, s = backward_mlp(
                    l, m, length, paired, gs[m], after[l][m], tau, time_weight, norm_gain, saved[l][m][9], w_up, w_down
                )
                if l < layers - 1:
                    add_sums(l + 1, (0, 2), s[0:16])
                add_sums(l, (4,), s[16:24])
                if m == 0:
                    part, gs[1:] = sync((part, gs[1:]))
                else:
                    part, sums[:m] = sync((part, sums[:m]))
                g2s[m], gms[m], dus[m], sums[m] = g2, gm, du, links.start_sum(part)
            groups = [keep(l, 8), gms, keep(l, 7), dus]
            stream = kind(links, "mlp", l, layers, groups)
            if links.ring:
                (sums, stream.keep) = sync((sums, stream.keep))
            streams.append(stream)
            gas, dps = [None] * parts, [None] * parts
            for m in range(parts):
                x, n1, q, k, v, att, x1 = saved[l][m][:7]
                g1, gas[m], dq, dk, dv, part, s = backward_attention(
                    l, length, paired, g2s[m], x1, *sums[m], norm_gain, q, k, v, wq, w_out, tables
                )
                add_sums(l, (1, 3), s)
                dps[m] = (dq, dk, dv)
                if m == 0:
                    part, sums[1:] = sync((part, sums[1:]))
                else:
                    part, gs[:m] = sync((part, gs[:m]))
                gs[m] = (g1, x, *links.start_sum(part))
            groups = [keep(l, 5), gas, keep(l, 1)] + [[d[j] for d in dps] for j in range(3)]
            stream = kind(links, "attention", l, layers, groups)
            if links.ring:
                (gs, stream.keep) = sync((gs, stream.keep))
            streams.append(stream)
        inputs = []
        for m in range(parts):
            g1, x, mine_part, got = gs[m]
            dn1 = mine_part.astype(f32) + meet(got).astype(f32)
            xhat, inverse = standardize(x)
            small[0][0] += jnp.sum(dn1 * xhat, axis=0)
            small[0][2] += jnp.sum(dn1, axis=0)
            inputs.append((g1 + norm_backward(dn1, xhat, inverse, norm_gain[0, 0])))
        tiny = jnp.stack([jnp.stack(a) for a in small])
        tiny = links.sum_small(tiny)
        written = {}
        for j, s in enumerate(streams):
            written[j % 2] = s.finish(written.get(j % 2))
        if paired:
            mine = lambda vs: jnp.concatenate([v[:own] for v in vs])
        else:
            t = lax.axis_index("tensor")
            mine = lambda vs: jnp.concatenate([lax.dynamic_slice_in_dim(v, t * own, own) for v in vs])
        gains, biases = tiny[:, 0:2], tiny[:, 2:4]
        return (
            mine(result),
            mine(inputs),
            gains,
            biases,
            jnp.transpose(written[1][1], (0, 2, 1, 3)),
            written[1][0],
            written[0][1],
            written[0][0],
            tiny[:, 4],
            jnp.stack([gains[layers - 1, 1], biases[layers - 1, 1]]),
        )

    return local


def solution(mesh):
    links = Links(mesh.shape["dp"], mesh.shape["tensor"])
    token_spec = P(("dp", "tensor"), None)
    in_specs = (
        token_spec,
        P(("dp", "tensor")),
        P(),
        P(),
        P(),
        P(None, None, None, "tensor"),
        P(None, "tensor", None),
        P(None, None, "tensor"),
        P(None, "tensor", None),
        P(),
        token_spec,
    )
    out_specs = (
        token_spec,
        token_spec,
        P(),
        P(),
        P(None, None, None, "tensor"),
        P(None, "tensor", None),
        P(None, None, "tensor"),
        P(None, "tensor", None),
        P(),
        P(),
    )
    return jax.shard_map(
        make_local(links), mesh=mesh, in_specs=in_specs, out_specs=out_specs, check_vma=False
    )
```

```python
import functools
import math

import jax
import jax.numpy as jnp
import numpy as np
from jax import lax
from jax.experimental import pallas as pl
from jax.experimental.pallas import tpu as pltpu
from jax.sharding import PartitionSpec as P

HD = 64
bf16 = jnp.bfloat16
f32 = jnp.float32
epsilon = 1e-05


def mm(a, b):
    return jnp.dot(a, b, preferred_element_type=f32)


def mm_t(a, b):
    return lax.dot_general(a, b, (((1,), (1,)), ((), ())), preferred_element_type=f32)


def across(a, b):
    return lax.dot_general(a, b, (((0,), (0,)), ((), ())), preferred_element_type=f32)


def ein(spec, a, b):
    return jnp.einsum(spec, a, b, preferred_element_type=f32)


def gelu_parts(u):
    square = u * u
    s = 0.5 + 0.5 * jnp.tanh(u * (0.7978845608 + 0.7978845608 * 0.044715 * square))
    value = u * s
    slope = s + value * (1.0 - s) * (2.0 * 0.7978845608 + 6.0 * 0.7978845608 * 0.044715 * square)
    return value, slope


def standardize(v):
    centered = v - jnp.mean(v, axis=-1, keepdims=True)
    inverse = lax.rsqrt(jnp.mean(centered * centered, axis=-1, keepdims=True) + epsilon)
    return centered * inverse, inverse


def norm_backward(grad, xhat, inverse, gain):
    e = grad * gain
    return inverse * (
        e
        - jnp.mean(e, axis=-1, keepdims=True)
        - xhat * jnp.mean(e * xhat, axis=-1, keepdims=True)
    )


CHUNK = 32
BLOCK = 256


def rope_tables(length, width):
    half = HD // 2
    freqs = np.exp(-math.log(10000.0) * np.arange(half) * 2.0 / HD)
    angles = np.arange(length)[:, None] * freqs[None, :]
    heads = width // HD
    cos = np.tile(np.cos(angles), (1, 2 * heads))
    sin = np.tile(np.concatenate([-np.sin(angles), np.sin(angles)], axis=1), (1, heads))
    return jnp.asarray(cos, f32), jnp.asarray(sin, f32)


def partner(u):
    width = u.shape[1]
    lane = lax.broadcasted_iota(jnp.int32, u.shape, 1)
    low = (lane & (HD - 1)) < HD // 2
    return jnp.where(low, pltpu.roll(u, width - HD // 2, 1), pltpu.roll(u, HD // 2, 1))


GAIN, BIAS, TIME = 0, 1, 2


def vector(ref, group, row):
    at = group * (ref.shape[0] // 3) + row
    return ref[at : at + 1, :]


def chunks(rows, body, start=0):
    def step(i, carry):
        body(pl.multiple_of(i * CHUNK, CHUNK))
        return carry

    lax.fori_loop(start // CHUNK, rows // CHUNK, step, 0, unroll=4)


def rows_at(at):
    return pl.ds(at, CHUNK)


def other_rows(at, rows, swapped):
    if not swapped:
        return rows_at(at)
    half = rows // 2
    return rows_at(pl.multiple_of(jnp.where(at < half, at + half, at - half), CHUNK))


def fold(v):
    return jnp.sum(v.reshape(-1, 8, v.shape[-1]), axis=0)


LIMIT = 17 * 2**20
SMALL = 12 * 2**20


def call(kernel, ins, outs, scratch, flops, name, aliases={}, after=(), limit=LIMIT):
    count, late = len(ins), len(after)
    specs, args = [], []
    for a, away in ins:
        space = pltpu.SMEM if a.dtype == jnp.int32 else pltpu.HBM if away else pltpu.VMEM
        specs.append(pl.BlockSpec(memory_space=space))
        args.append(a if space == pltpu.SMEM else pltpu.with_memory_space_constraint(a, space))

    def run(*refs):
        kernel(*refs[:count], *refs[count + late :])

    return pl.pallas_call(
        run,
        out_shape=[(pltpu.HBM if away else pltpu.VMEM)(s, d) for s, d, away in outs],
        in_specs=specs + [pl.BlockSpec(memory_space=pl.ANY)] * late,
        out_specs=[pl.BlockSpec(memory_space=pltpu.HBM if away else pltpu.VMEM) for _, _, away in outs],
        scratch_shapes=scratch,
        input_output_aliases=aliases,
        compiler_params=pltpu.CompilerParams(vmem_limit_bytes=limit),
        cost_estimate=pl.CostEstimate(flops=20 * flops, bytes_accessed=2**20, transcendentals=0),
        name=name,
    )(*args, *after)


class Saver:
    def __init__(self, sems):
        self.sems, self.copies = sems, []

    def save(self, held, out):
        c = pltpu.make_async_copy(held, out, self.sems.at[len(self.copies)])
        c.start()
        self.copies.append(c)

    def wait(self):
        for c in self.copies:
            c.wait()


def masks():
    lane = lax.broadcasted_iota(jnp.int32, (1, 2 * HD), 1)
    return lane < HD


def both_heads(v, low):
    zero = jnp.zeros_like(v)
    return jnp.concatenate([jnp.where(low, v, zero), jnp.where(low, zero, v)], axis=0)


def halves(v):
    n = v.shape[1] // 2
    return v[:, :n], v[:, n:]


def softmax(scores):
    out = []
    for s in halves(scores):
        e = jnp.exp(s - jnp.max(s, axis=-1, keepdims=True))
        out.append(e * (1.0 / jnp.sum(e, axis=-1, keepdims=True)))
    return out


def beside(a, b):
    return jnp.concatenate([a, b], axis=1)


def forward_attention(layer, part_index, length, swapped, head, tau, vectors, w_qkv, w_out, tables):
    first = layer == 0
    rows = sum(n for _, _, n in head) if first else head[0].shape[0]
    width = w_out.shape[2]
    local = w_out.shape[1]
    block = min(BLOCK, local)
    scale = HD ** (-0.5)
    seqs = rows // length
    parts = tau.shape[0] // seqs

    def kernel(*refs):
        it = iter(refs)
        take = lambda n: [next(it) for _ in range(n)]
        head_refs = take(len(head))
        tau_ref, vec_ref, wq_any, wo_any, cos_any, sin_any = take(6)
        x_ref, part_ref = take(2)
        outs = take(6 if first else 7)
        wq, wo, cos_ref, sin_ref, sems, out_sems = take(6)
        n_ref, q_ref, k_ref, v_ref, att_ref = take(5)
        if first:
            held, = take(1)
        else:
            x2_ref, = take(1)
        saver = Saver(out_sems)
        if first:
            own = head_refs[0].at[pl.ds(head[0][1], head[0][2]), :]
            fetch = pltpu.make_async_copy(own, held, sems.at[4])
            fetch.start()
        ropes = [pltpu.make_async_copy(a, b, sems.at[5 + j]) for j, (a, b) in
                 enumerate(((cos_any, cos_ref), (sin_any, sin_ref)))]
        copies = [pltpu.make_async_copy(wq_any.at[layer, j], wq.at[j], sems.at[j]) for j in range(3)]
        copies.append(pltpu.make_async_copy(wo_any.at[layer], wo, sems.at[3]))
        for c in copies[:1] + ropes + copies[1:]:
            c.start()
        gain, bias = vector(vec_ref, GAIN, 2 * layer), vector(vec_ref, BIAS, 2 * layer)

        def norm(at, x):
            x_ref[rows_at(at), :] = x
            xhat, _ = standardize(x)
            n_ref[rows_at(at), :] = (xhat * gain + bias).astype(bf16)

        if first:
            count = head[0][2]
            if len(head) > 1:
                ref = head_refs[1]
                chunks(rows, lambda at: norm(at, ref[rows_at(at - count), :].astype(f32)), count)
            fetch.wait()
            chunks(count, lambda at: norm(at, held[rows_at(at), :].astype(f32)))
        else:
            x1, own, got = head_refs

            def scaled(at):
                here = rows_at(at)
                there = other_rows(at, rows, swapped)
                x2 = x1[here, :] + own[here, :].astype(f32) + got[there, :].astype(f32)
                x2_ref[here, :] = x2
                t = tau_ref[pl.ds(at // length * parts + part_index, 1), :]
                norm(at, x2 * (1.0 + t * vector(vec_ref, TIME, layer - 1)))

            chunks(rows, scaled)
            saver.save(x2_ref, outs[6])
        saver.save(x_ref, outs[0])
        saver.save(n_ref, outs[1])
        for c in ropes:
            c.wait()
        for j, out in enumerate((q_ref, k_ref, v_ref)):
            copies[j].wait()
            for b in range(0, local, block):
                u = mm(n_ref[...], wq[j, :, b : b + block])
                if j < 2:
                    for s in range(0, rows, length):
                        us = u[s : s + length]
                        us = us * cos_ref[:, b : b + block] + partner(us) * sin_ref[:, b : b + block]
                        out[s : s + length, b : b + block] = us.astype(bf16)
                else:
                    out[:, b : b + block] = u.astype(bf16)
            saver.save(out, outs[2 + j])
        low = masks()
        for s in range(0, rows, length):
            for b in range(0, local, 2 * HD):
                here = (slice(s, s + length), slice(b, b + 2 * HD))
                keys = both_heads(k_ref[here], low)
                probs = beside(*softmax(mm_t(q_ref[here], keys) * scale)).astype(bf16)
                att_ref[here] = mm(probs, both_heads(v_ref[here], low)).astype(bf16)
        saver.save(att_ref, outs[5])
        copies[3].wait()
        for b in range(0, width, BLOCK):
            part_ref[:, b : b + BLOCK] = mm(att_ref[...], wo[:, b : b + BLOCK]).astype(bf16)
        saver.wait()

    ins = [(a[0], j == 0) for j, a in enumerate(head)] if first else [(a, False) for a in head]
    ins += [(a, False) for a in (tau, vectors)] + [(w_qkv, True), (w_out, True)]
    ins += [(t, True) for t in tables]
    near = lambda n, d: ((rows, n), d, False)
    far = lambda n, d: ((rows, n), d, True)
    outs = [near(width, f32), near(width, bf16)]
    outs += [far(width, f32), far(width, bf16)] + [far(local, bf16)] * 4
    outs += [] if first else [far(width, f32)]
    scratch = [
        pltpu.VMEM((3, width, local), bf16),
        pltpu.VMEM((local, width), bf16),
        pltpu.VMEM((length, local), f32),
        pltpu.VMEM((length, local), f32),
        pltpu.SemaphoreType.DMA((7,)),
        pltpu.SemaphoreType.DMA((7,)),
        pltpu.VMEM((rows, width), bf16),
    ]
    scratch += [pltpu.VMEM((rows, local), bf16)] * 4
    scratch.append(pltpu.VMEM((head[0][2], width), bf16) if first else pltpu.VMEM((rows, width), f32))
    return call(kernel, ins, outs, scratch, 4 * 10**9, "forward_attention")


def forward_mlp(layer, swapped, split, x, own, got, vectors, w_up, w_down, after):
    rows, width = x.shape
    hidden = w_up.shape[2]
    tiles = hidden // BLOCK

    def kernel(x_ref, own_ref, got_ref, vec_ref, wu_any, wd_any, x1_ref, *refs):
        part_refs, refs = refs[: 1 + split], refs[1 + split :]
        x1_out, n_out, h_out, slope_out, n_ref, h_ref, slope_ref, wu, wd, sems, out_sems = refs
        saver = Saver(out_sems)
        gain, bias = vector(vec_ref, GAIN, 2 * layer + 1), vector(vec_ref, BIAS, 2 * layer + 1)
        ups = [
            pltpu.make_async_copy(
                wu_any.at[layer, :, pl.ds(t * BLOCK, BLOCK)], wu.at[t], sems.at[t]
            )
            for t in range(tiles)
        ]
        down = pltpu.make_async_copy(wd_any.at[layer], wd, sems.at[tiles])
        for c in ups:
            c.start()
        down.start()

        def norm(at):
            here = rows_at(at)
            there = other_rows(at, rows, swapped)
            x1 = x_ref[here, :] + own_ref[here, :].astype(f32) + got_ref[there, :].astype(f32)
            x1_ref[here, :] = x1
            xhat, _ = standardize(x1)
            n_ref[here, :] = (xhat * gain + bias).astype(bf16)

        chunks(rows, norm)
        saver.save(x1_ref, x1_out)
        saver.save(n_ref, n_out)
        for t in range(tiles):
            ups[t].wait()
            value, slope = gelu_parts(mm(n_ref[...], wu[t]))
            h_ref[:, t * BLOCK : (t + 1) * BLOCK] = value.astype(bf16)
            slope_ref[:, t * BLOCK : (t + 1) * BLOCK] = slope.astype(bf16)
        saver.save(h_ref, h_out)
        saver.save(slope_ref, slope_out)
        down.wait()
        for b in range(0, width, BLOCK):
            part = mm(h_ref[...], wd[:, b : b + BLOCK]).astype(bf16)
            for j, ref in enumerate(part_refs):
                ref[:, b : b + BLOCK] = part[j * ref.shape[0] : (j + 1) * ref.shape[0]]
        saver.wait()

    ins = [(a, False) for a in (x, own, got, vectors)] + [(w_up, True), (w_down, True)]
    near = lambda n, d: ((rows, n), d, False)
    far = lambda n, d: ((rows, n), d, True)
    outs = [near(width, f32)] + [((rows // (1 + split), width), bf16, False)] * (1 + split)
    outs += [far(width, f32), far(width, bf16), far(hidden, bf16), far(hidden, bf16)]
    scratch = [
        pltpu.VMEM((rows, width), bf16),
        pltpu.VMEM((rows, hidden), bf16),
        pltpu.VMEM((rows, hidden), bf16),
        pltpu.VMEM((tiles, width, BLOCK), bf16),
        pltpu.VMEM((hidden, width), bf16),
        pltpu.SemaphoreType.DMA((tiles + 1,)),
        pltpu.SemaphoreType.DMA((4,)),
    ]
    return call(kernel, ins, outs, scratch, 6 * 10**9, "forward_mlp", after=after)


def last_layer(layer, length, parts, tau, vectors, cotangent, rows_of, after):
    rows = cotangent.shape[0] // parts
    width = cotangent.shape[1]
    seqs = rows // length

    def kernel(tau_ref, vec_ref, cot_ref, *refs):
        result_ref, sums_ref = refs[-2:]
        sums_ref[...] = jnp.zeros_like(sums_ref)
        for m in range(parts):
            x1_ref, own_ref, got_ref = refs[3 * m : 3 * m + 3]

            def body(at):
                here, there = rows_at(at), rows_at(pl.multiple_of(at + m * rows, CHUNK))
                x2 = x1_ref[here, :] + own_ref[here, :].astype(f32) + got_ref[here, :].astype(f32)
                t = tau_ref[pl.ds(at // length * parts + m, 1), :]
                sums_ref[...] += fold(cot_ref[there, :].astype(f32) * x2) * t
                result_ref[there, :] = x2 * (1.0 + t * vector(vec_ref, TIME, layer))

            chunks(rows, body)

    ins = [(tau, False), (vectors, False), (cotangent, False)] + [(v, False) for part in rows_of for v in part]
    outs = [(cotangent.shape, f32, False), ((8, width), f32, False)]
    return call(kernel, ins, outs, [], 10**8, "last_layer", after=after)


def backward_mlp(layer, last, part_index, length, swapped, head, x2, tau, vectors, slope, w_up, w_down, after):
    rows = slope.shape[0]
    width = vectors.shape[1]
    hidden = w_up.shape[2]
    tiles = hidden // BLOCK
    seqs = rows // length
    parts = tau.shape[0] // seqs

    def kernel(*refs):
        it = iter(refs)
        take = lambda n: [next(it) for _ in range(n)]
        head_refs = take(len(head))
        x2_ref = None if last else take(1)[0]
        tau_ref, vec_ref, slope_ref, wu_any, wd_any = take(5)
        g2_ref, gm_ref, du_ref, part_ref, sums_ref = take(5)
        wu, wd, sems = take(3)
        downs = [
            pltpu.make_async_copy(
                wd_any.at[layer, pl.ds(t * BLOCK, BLOCK), :], wd.at[t], sems.at[t]
            )
            for t in range(tiles)
        ]
        up = pltpu.make_async_copy(wu_any.at[layer], wu, sems.at[tiles])
        for c in downs:
            c.start()
        up.start()
        sums_ref[...] = jnp.zeros_like(sums_ref)

        def begin(at, g):
            here = rows_at(at)
            t = tau_ref[pl.ds(at // length * parts + part_index, 1), :]
            if not last:
                sums_ref[16:24, :] += fold(g * x2_ref[here, :]) * t
            g2 = g * (1.0 + t * vector(vec_ref, TIME, layer))
            g2_ref[here, :] = g2
            gm_ref[here, :] = g2.astype(bf16)

        if last:
            low = 0
            for ref, (_, start, count) in zip(head_refs, head):
                chunks(
                    low + count,
                    lambda at, ref=ref, shift=start - low: begin(
                        at, ref[rows_at(pl.multiple_of(at + shift, CHUNK)), :].astype(f32)
                    ),
                    low,
                )
                low += count
        else:
            g1, x, own, got = head_refs

            def through_norm(at):
                here = rows_at(at)
                dn = own[here, :].astype(f32) + got[other_rows(at, rows, swapped), :].astype(f32)
                xhat, inverse = standardize(x[here, :])
                sums_ref[0:8, :] += fold(dn * xhat)
                sums_ref[8:16, :] += fold(dn)
                begin(at, g1[here, :] + norm_backward(dn, xhat, inverse, vector(vec_ref, GAIN, 2 * layer + 2)))

            chunks(rows, through_norm)
        for t in range(tiles):
            downs[t].wait()
            at = slice(t * BLOCK, (t + 1) * BLOCK)
            dh = mm_t(gm_ref[...], wd[t])
            du_ref[:, at] = (dh * slope_ref[:, at].astype(f32)).astype(bf16)
        up.wait()
        for b in range(0, width, BLOCK):
            part_ref[:, b : b + BLOCK] = mm_t(du_ref[...], wu[b : b + BLOCK, :]).astype(bf16)

    ins = [(a[0] if last else a, False) for a in head]
    ins += [] if last else [(x2, False)]
    ins += [(a, False) for a in (tau, vectors, slope)]
    ins += [(w_up, True), (w_down, True)]
    near = lambda n, d: ((rows, n), d, False)
    outs = [near(width, f32), near(width, bf16), near(hidden, bf16), near(width, bf16)]
    outs += [((24, width), f32, False)]
    scratch = [
        pltpu.VMEM((width, hidden), bf16),
        pltpu.VMEM((tiles, BLOCK, width), bf16),
        pltpu.SemaphoreType.DMA((tiles + 1,)),
    ]
    return call(kernel, ins, outs, scratch, 6 * 10**9, "backward_mlp", after=after)


def input_gradient(layer, swapped, own_rows, vectors, rows_of, after):
    rows, width = rows_of[0][1].shape

    def kernel(vec_ref, *refs):
        out_ref, sums_ref = refs[-2:]
        sums_ref[...] = jnp.zeros_like(sums_ref)
        for m in range(len(rows_of)):
            g1_ref, x_ref, own_ref, got_ref = refs[4 * m : 4 * m + 4]

            def body(at, mine):
                here = rows_at(at)
                dn = own_ref[here, :].astype(f32) + got_ref[other_rows(at, rows, swapped), :].astype(f32)
                xhat, inverse = standardize(x_ref[here, :])
                sums_ref[0:8, :] += fold(dn * xhat)
                sums_ref[8:16, :] += fold(dn)
                if mine:
                    out_ref[rows_at(pl.multiple_of(at + m * own_rows, CHUNK)), :] = g1_ref[here, :] + norm_backward(
                        dn, xhat, inverse, vector(vec_ref, GAIN, 2 * layer)
                    )

            chunks(own_rows, lambda at: body(at, True))
            chunks(rows, lambda at: body(at, False), own_rows)

    ins = [(vectors, False)] + [(v, False) for part in rows_of for v in part]
    outs = [((own_rows * len(rows_of), width), f32, False), ((16, width), f32, False)]
    return call(kernel, ins, outs, [], 10**8, "input_gradient", after=after)


def totals(sums, layers, width, after):
    def kernel(*refs):
        out = refs[-1]
        out[...] = jnp.zeros_like(out)
        for ref, (layer, rows, factor, _) in zip(refs, sums):
            for j, row in enumerate(rows):
                if row is not None:
                    out[layer, row : row + 1, :] += factor * jnp.sum(ref[8 * j : 8 * j + 8, :], axis=0, keepdims=True)

    ins = [(v, False) for _, _, _, v in sums]
    return call(kernel, ins, [((layers, 8, width), f32, False)], [], 10**8, "totals", after=after)[0]


def backward_attention(layer, length, swapped, g2, x1, own, got, vectors, q, k, v, w_qkv, w_out, tables, after):
    rows, width = x1.shape
    local = w_out.shape[1]
    block = min(BLOCK, local)
    scale = HD ** (-0.5)

    def kernel(g2_ref, x1_ref, own_ref, got_ref, vec_ref, q_ref, k_ref, v_ref, wq_any, wo_any, cos_any, sin_any,
               g1_ref, ga_ref, dq_ref, dk_ref, dv_ref, part_ref, sums_ref, wq, wo, do_ref, cos_ref, sin_ref, sems):
        copies = [pltpu.make_async_copy(wo_any.at[layer], wo, sems.at[3])]
        copies += [pltpu.make_async_copy(cos_any, cos_ref, sems.at[4])]
        copies += [pltpu.make_async_copy(sin_any, sin_ref, sems.at[5])]
        copies += [pltpu.make_async_copy(wq_any.at[layer, j], wq.at[j], sems.at[j]) for j in range(3)]
        for c in copies:
            c.start()
        sums_ref[...] = jnp.zeros_like(sums_ref)

        def begin(at):
            here = rows_at(at)
            dn = own_ref[here, :].astype(f32) + got_ref[other_rows(at, rows, swapped), :].astype(f32)
            xhat, inverse = standardize(x1_ref[here, :])
            sums_ref[0:8, :] += fold(dn * xhat)
            sums_ref[8:16, :] += fold(dn)
            g1 = g2_ref[here, :] + norm_backward(dn, xhat, inverse, vector(vec_ref, GAIN, 2 * layer + 1))
            g1_ref[here, :] = g1
            ga_ref[here, :] = g1.astype(bf16)

        chunks(rows, begin)
        for c in copies[:3]:
            c.wait()
        for b in range(0, local, block):
            do_ref[:, b : b + block] = mm_t(ga_ref[...], wo[b : b + block, :]).astype(bf16)
        low = masks()
        for s in range(0, rows, length):
            for b in range(0, local, 2 * HD):
                here = (slice(s, s + length), slice(b, b + 2 * HD))
                lanes = slice(b, b + 2 * HD)
                keys = both_heads(k_ref[here], low)
                grad = do_ref[here]
                probs = softmax(mm_t(q_ref[here], keys) * scale)
                dps = halves(mm_t(grad, both_heads(v_ref[here], low)))
                ds = [p * (d - jnp.sum(p * d, axis=-1, keepdims=True)) for p, d in zip(probs, dps)]
                across_heads = lambda v, w: mm(beside(v[0].T, v[1].T).astype(bf16), both_heads(w, low))
                dv_ref[here] = across_heads(probs, grad).astype(bf16)
                dq = mm(beside(*ds).astype(bf16), keys) * scale
                dk = across_heads(ds, q_ref[here]) * scale
                for d, out in ((dq, dq_ref), (dk, dk_ref)):
                    out[here] = (d * cos_ref[:, lanes] + partner(d * sin_ref[:, lanes])).astype(bf16)
        for c in copies[3:]:
            c.wait()
        for b in range(0, width, BLOCK):
            at = slice(b, b + BLOCK)
            part = mm_t(dq_ref[...], wq[0, at, :]) + mm_t(dk_ref[...], wq[1, at, :])
            part_ref[:, at] = (part + mm_t(dv_ref[...], wq[2, at, :])).astype(bf16)

    ins = [(a, False) for a in (g2, x1, own, got, vectors, q, k, v)] + [(w_qkv, True), (w_out, True)]
    ins += [(t, True) for t in tables]
    near = lambda n, d: ((rows, n), d, False)
    outs = [near(width, f32), near(width, bf16)] + [near(local, bf16)] * 3
    outs += [near(width, bf16), ((16, width), f32, False)]
    scratch = [
        pltpu.VMEM((3, width, local), bf16),
        pltpu.VMEM((local, width), bf16),
        pltpu.VMEM((rows, local), bf16),
        pltpu.VMEM((length, local), f32),
        pltpu.VMEM((length, local), f32),
        pltpu.SemaphoreType.DMA((6,)),
    ]
    return call(kernel, ins, outs, scratch, 7 * 10**9, "backward_attention", after=after)


class Links:
    def __init__(self, dp, tensor):
        self.dp, self.tensor = dp, tensor
        self.chips = dp // 2
        self.ring = dp == 16
        self.walk = [0, 2, 4, 6, 7, 5, 3, 1]
        place = [self.walk.index(i) for i in range(8)]
        self.place = place
        self.ring_pairs = []
        for k in range(8):
            here, there = self.walk[k], self.walk[(k + 1) % 8]
            self.ring_pairs.append((2 * here, 2 * there))
            self.ring_pairs.append((2 * there + 1, 2 * here + 1))
        self.core_pairs = [(i, i ^ 1) for i in range(dp)]

    def ring_place(self):
        i = lax.axis_index("dp")
        p = jnp.asarray(self.place, jnp.int32)[i >> 1]
        return jnp.where(i & 1 == 0, p, (8 - p) % 8)

    def swap_tensor(self, v):
        return lax.ppermute(v, "tensor", [(0, 1), (1, 0)])

    def gather_tensor(self, v):
        if self.tensor != 2:
            return lax.all_gather(v, "tensor", axis=0, tiled=True)
        other = self.swap_tensor(v)
        first = lax.axis_index("tensor") == 0
        return jnp.concatenate([jnp.where(first, v, other), jnp.where(first, other, v)])

    def start_sum(self, part):
        part = part.astype(bf16)
        if self.tensor != 2:
            summed = lax.psum(part, "tensor")
            return (summed, jnp.zeros_like(summed))
        return (part, self.swap_tensor(part))

def total(parts):
    out = parts[0].astype(f32)
    for p in parts[1:]:
        out = out + p.astype(f32)
    return out


def over_rows(lefts, rights):
    return across(jnp.concatenate(lefts), jnp.concatenate(rights))


def mlp_gradients(h, gm, n2, du, core, place, after):
    n = len(h)
    hidden, width = h[0].shape[1], gm[0].shape[1]
    half_hidden = hidden // 2
    tall = half_hidden // 8
    wide = width // 8

    def kernel(s_ref, *refs):
        hs, gms, ns, dus = [refs[n * j : n * j + n] for j in range(4)]

        def make(target, half, p):
            gm_all = jnp.concatenate([r[...] for r in gms])
            columns = slice(half * half_hidden, (half + 1) * half_hidden)
            du_all = jnp.concatenate([r[:, columns] for r in dus])
            for j in range(4):
                first = half * half_hidden + j * 2 * tall
                down = across(jnp.concatenate([r[:, first : first + 2 * tall] for r in hs]), gm_all)
                up = across(jnp.concatenate([r[:, j * 2 * wide : (j + 1) * 2 * wide] for r in ns]), du_all)
                for i in range(2):
                    slot = lax.rem(p - (2 * j + i) + 8, 8)
                    target[slot, 0:tall, :] = down[i * tall : (i + 1) * tall].astype(bf16)
                    target[slot, tall : tall + wide, :] = up[i * wide : (i + 1) * wide].astype(bf16)

        for c in range(2):

            @pl.when(s_ref[0] == c)
            def _():
                make(refs[4 * n], 1 - c, lax.rem(8 - s_ref[1], 8))
                make(refs[4 * n + 1], c, s_ref[1])

    ins = [(jnp.stack([core, place]).astype(jnp.int32), False)]
    ins += [(v, False) for group in (h, gm, n2, du) for v in group]
    out = ((8, tall + wide, width), bf16, False)
    return call(kernel, ins, [out, out], [], 9 * 10**9, "mlp_gradients", after=after, limit=SMALL)


def attention_gradients(att, ga, n1, dq, dk, dv, core, place, after):
    n = len(att)
    local, width = att[0].shape[1], ga[0].shape[1]
    heads, wide = local // 2, width // 2

    def kernel(s_ref, *refs):
        atts, gas, ns = [refs[n * j : n * j + n] for j in range(3)]
        dps = [refs[n * j : n * j + n] for j in range(3, 6)]

        def make(target, half, p):
            def put(value, low, size):
                for b in range(8):
                    slot = lax.rem(p - b + 8, 8)
                    target[slot, low : low + size, :] = value[b * size : (b + 1) * size].astype(bf16)

            lefts = [r[:, half * heads : (half + 1) * heads] for r in atts]
            for j in range(2):
                put(over_rows(lefts, [r[:, j * wide : (j + 1) * wide] for r in gas]), heads // 8 * j, heads // 8)
            lefts = [r[:, half * wide : (half + 1) * wide] for r in ns]
            for j in range(3):
                put(over_rows(lefts, [r[...] for r in dps[j]]), heads // 4 + wide // 8 * j, wide // 8)

        for c in range(2):

            @pl.when(s_ref[0] == c)
            def _():
                make(refs[6 * n], 1 - c, lax.rem(8 - s_ref[1], 8))
                make(refs[6 * n + 1], c, s_ref[1])

    ins = [(jnp.stack([core, place]).astype(jnp.int32), False)]
    ins += [(v, False) for group in (att, ga, n1, dq, dk, dv) for v in group]
    out = ((8, heads // 4 + 3 * wide // 8, local), bf16, False)
    return call(kernel, ins, [out, out], [], 5 * 10**9, "attention_gradients", after=after, limit=SMALL)


def pack(lanes, after):
    depths = [lane[0].shape[0] for lane in lanes]
    count, width = len(lanes[0]), lanes[0][0].shape[1]

    def kernel(*refs):
        low = 0
        for j, depth in enumerate(depths):
            for i in range(count):
                refs[-1][i, low : low + depth, :] = refs[j * count + i][...]
            low += depth

    out = ((count, sum(depths), width), bf16, False)
    ins = [(v, False) for lane in lanes for v in lane]
    return call(kernel, ins, [out], [], 10**8, "pack", after=after, limit=SMALL)[0]


def merge(a, b, lanes, after):
    count, depth, width = a.shape
    depth //= lanes

    def kernel(a_ref, b_ref, *outs):
        def total(i, j):
            at = slice(j * depth, (j + 1) * depth)
            return (a_ref[i, at, :].astype(f32) + b_ref[i, at, :].astype(f32)).astype(bf16)

        for j in range(lanes):
            outs[2 * j][...] = total(0, j)

        def body(i, carry):
            for j in range(lanes):
                outs[2 * j + 1][i] = total(i, j)
            return carry

        lax.fori_loop(1, count, body, 0)

    outs = [((depth, width), bf16, False), ((count, depth, width), bf16, False)] * lanes
    out = call(kernel, [(a, False), (b, False)], outs, [], 10**8, "merge", after=after, limit=SMALL)
    return out[0::2], out[1::2]


def add(a, blocks, i, after):
    def kernel(a_ref, b_ref, out_ref):
        out_ref[...] = (a_ref[...].astype(f32) + b_ref[i].astype(f32)).astype(bf16)

    outs = [(a.shape, bf16, False)]
    return call(kernel, [(a, False), (blocks, False)], outs, [], 10**8, "add", after=after, limit=SMALL)[0]


def hold(a, after):
    def kernel(a_ref, out_ref):
        out_ref[...] = a_ref[...]

    return call(kernel, [(a, False)], [(a.shape, bf16, False)], [], 10**8, "hold", after=after, limit=SMALL)[0]


DEEP = 4


def spread(pieces, shapes, mine, peer, core, place, before, after):
    depth, width = mine.shape[1:]

    def kernel(s_ref, mine_ref, peer_ref, *refs):
        token_ref, held, sems = refs[-3:]
        outs = refs[len(refs) - 3 - len(shapes) : -3]
        token_ref[...] = jnp.zeros_like(token_ref)

        def copies(i):
            half, p = (s_ref[0], s_ref[1]) if i < 8 else (1 - s_ref[0], lax.rem(8 - s_ref[1], 8))
            b = lax.rem(p + 1 - i % 8 + 8, 8)
            return [
                pltpu.make_async_copy(
                    held.at[(i % DEEP,) + source], outs[o].at[place], sems.at[i % DEEP, j]
                )
                for j, (source, o, place) in enumerate(pieces(half, b))
            ]

        for i in range(16):
            if i >= DEEP:
                for c in copies(i - DEEP):
                    c.wait()
            held[i % DEEP] = (mine_ref if i < 8 else peer_ref)[i % 8].astype(f32)
            for c in copies(i):
                c.start()
        for i in range(16 - DEEP, 16):
            for c in copies(i):
                c.wait()

    ins = [(jnp.stack([core, place]).astype(jnp.int32), False), (mine, False), (peer, False)]
    aliases = {}
    if before is not None:
        for j, v in enumerate(before):
            aliases[len(ins)] = j
            ins.append((v, True))
    scratch = [
        pltpu.VMEM((DEEP, depth, width), f32),
        pltpu.SemaphoreType.DMA((DEEP, len(pieces(0, 0)))),
    ]
    outs = [(s, f32, True) for s in shapes] + [((8, 128), f32, False)]
    *outs, token = call(kernel, ins, outs, scratch, 10**8, "spread", aliases, after=after, limit=SMALL)
    return outs, token


def mlp_pieces(layer, layers, hidden, width):
    tall, wide = hidden // 16, width // 8

    def pieces(half, b):
        rows = pl.ds(pl.multiple_of(half * (hidden // 2) + b * tall, tall), tall)
        across_rows = pl.ds(pl.multiple_of(b * wide, wide), wide)
        columns = pl.ds(pl.multiple_of(half * (hidden // 2), hidden // 2), hidden // 2)
        return [
            ((slice(0, tall), slice(None)), 0, (layer, rows, slice(None))),
            ((slice(tall, tall + wide), slice(None)), 1, (layer, across_rows, columns)),
        ]

    return pieces, [(layers, hidden, width), (layers, width, hidden)]


def attention_pieces(layer, layers, local, width):
    tall, wide = local // 16, width // 16

    def pieces(half, b):
        rows = pl.ds(pl.multiple_of(half * (local // 2) + b * tall, tall), tall)
        deep = pl.ds(pl.multiple_of(half * (width // 2) + b * wide, wide), wide)
        out = []
        for j in range(2):
            columns = slice(j * width // 2, (j + 1) * width // 2)
            out.append(((slice(tall * j, tall * (j + 1)), slice(None)), 0, (layer, rows, columns)))
        for j in range(3):
            low = 2 * tall + wide * j
            out.append(((slice(low, low + wide), slice(None)), 1, (layer, j, deep, slice(None))))
        return out

    return pieces, [(layers, local, width), (layers, 3, width, local)]


class Stream:
    def __init__(self, links, kind, layer, layers, groups, after, written):
        self.links, self.kind, self.written = links, kind, written
        self.steps = -2
        self.lanes = LANES[kind][min(layer, 1)]
        self.core = lax.axis_index("dp") & 1
        self.p = links.ring_place()
        if kind == "mlp":
            send, self.blocks = mlp_gradients(*groups, self.core, self.p, after)
            self.layout = mlp_pieces(layer, layers, groups[0][0].shape[1], groups[1][0].shape[1])
        else:
            send, self.blocks = attention_gradients(*groups, self.core, self.p, after)
            self.layout = attention_pieces(layer, layers, groups[0][0].shape[1], groups[1][0].shape[1])
        self.raw = lax.ppermute(send, "dp", links.core_pairs)
        self.done = [[] for _ in range(self.lanes)]
        self.token = self.blocks

    def step(self, after):
        self.steps += 1
        if self.steps < 0:
            return []
        if self.steps == 15:
            before = self.written.get(self.kind)
            self.written[self.kind], token = spread(
                *self.layout, self.mine, self.raw, self.core, self.p, before, after
            )
            return [token]
        if self.steps == 14:
            for lane, v in zip(self.done, self.raw):
                lane.append(v)
            self.mine = pack(self.done, after)
            self.raw = lax.ppermute(self.mine, "dp", self.links.core_pairs)
            return [self.mine]
        if self.steps == 0:
            now, self.blocks = merge(self.blocks, self.raw, self.lanes, after)
        elif self.steps < 8:
            now = [add(r, b, self.steps, after) for r, b in zip(self.raw, self.blocks)]
        else:
            now = [hold(r, after) for r in self.raw]
        if self.steps >= 7:
            for lane, v in zip(self.done, now):
                lane.append(v)
        self.raw = [lax.ppermute(v, "dp", self.links.ring_pairs) for v in now]
        return list(now)

    def going(self):
        return self.steps < 15


LANES = {"mlp": (2, 1), "attention": (1, 1)}


class Plain:
    def __init__(self, links, kind, layer, layers, groups, after, written):
        left, right, deep, *dps = [jnp.concatenate(g) for g in groups]
        out = [ein("ra,rb->ab", left, right)]
        if kind == "mlp":
            out.append(ein("ra,rb->ab", deep, dps[0]))
        else:
            out.append(jnp.stack([ein("ra,rb->ab", deep, d) for d in dps]))
        out = [lax.psum(v.astype(bf16), "dp").astype(f32) for v in out]
        if kind not in written:
            written[kind] = [jnp.zeros((layers,) + v.shape, f32) for v in out]
        written[kind] = [b.at[layer].set(v) for b, v in zip(written[kind], out)]
        self.token = after[0]

    def going(self):
        return False

def make_local(links):
    def local(
        tokens,
        time_index,
        time_table,
        norm_gain,
        norm_bias,
        w_qkv,
        w_out,
        w_up,
        w_down,
        time_weight,
        cotangent,
    ):
        rows, width = tokens.shape
        seq_here = time_index.shape[0]
        length = rows // seq_here
        layers = norm_gain.shape[0]
        local_width = w_out.shape[1]
        tables = rope_tables(length, local_width)
        parts = 2 if seq_here % 2 == 0 else 1
        own = rows // parts
        paired = links.tensor == 2
        wq = jnp.transpose(w_qkv, (0, 2, 1, 3))

        def group_rows(v, m):
            if paired:
                got = links.swap_tensor(v[m * own : (m + 1) * own])
                return [(v, m * own, own), (got, 0, own)]
            v = links.gather_tensor(v[m * own : (m + 1) * own])
            return [(v, 0, v.shape[0])]

        heads = [group_rows(tokens, m) for m in range(parts)]
        gs = [group_rows(cotangent, m) for m in range(parts)]
        arrived = [g[-1][0] for g in gs]
        vectors = [norm_gain.reshape(2 * layers, width), norm_bias.reshape(2 * layers, width)]
        vectors += [time_weight, jnp.zeros((layers, width), f32)]
        vectors = jnp.concatenate(vectors)
        if paired:
            index = jnp.concatenate([time_index, links.swap_tensor(time_index)])
        else:
            index = links.gather_tensor(time_index)
        onehot = (index[:, None] == jnp.arange(time_table.shape[0], dtype=jnp.int32)[None, :]).astype(f32)
        tau = jnp.dot(onehot, time_table, precision=lax.Precision.HIGHEST)
        saved = [[None] * parts for _ in range(layers)]
        after = [[None] * parts for _ in range(layers)]
        for l in range(layers):
            for m in range(parts):
                x_near, part, *out = forward_attention(
                    l, m, length, paired, heads[m], tau, vectors, wq, w_out, tables
                )
                if l > 0:
                    after[l - 1][m] = out.pop()
                saved[l][m] = out
                heads[m] = (x_near, *links.start_sum(part))
            for m in range(parts):
                split = paired and l == layers - 1
                x1, *out = forward_mlp(l, paired, split, *heads[m], vectors, w_up, w_down, arrived)
                if split:
                    heads[m] = (x1, *out[:2])
                else:
                    heads[m] = (x1, *links.start_sum(out[0]))
                saved[l][m] += out[1 + split :]
                arrived = []

        kind = Stream if links.ring else Plain
        streams = []
        small = []
        share = 0.5 if paired else 1.0
        keep = lambda l, i: [s[i] for s in saved[l]]

        last, written = [], {}

        def step(also=()):
            before = list(also)
            for s in streams:
                if s.going():
                    before += s.step(list(last))
            return before

        def ran(out):
            last[:] = [out]

        gs_first = gs
        gs = list(gs)
        for l in reversed(range(layers)):
            g2s, gms, dus, sums = [None] * parts, [None] * parts, [None] * parts, [None] * parts
            for m in range(parts):
                g2s[m], gms[m], dus[m], part, s = backward_mlp(
                    l, l == layers - 1, m, length, paired, gs[m], after[l][m], tau, vectors, saved[l][m][9],
                    w_up, w_down, step(),
                )
                ran(s)
                if l < layers - 1:
                    small.append((l + 1, (0, 2), share, s))
                    small.append((l, (None, None, 4), share, s))
                sums[m] = links.start_sum(part)
            groups = [keep(l, 8), gms, keep(l, 7), dus]
            streams.append(kind(links, "mlp", l, layers, groups, step([sums[0][1]]), written))
            ran(streams[-1].token)
            gas, dps = [None] * parts, [None] * parts
            for m in range(parts):
                x, n1, q, k, v, att, x1 = saved[l][m][:7]
                g1, gas[m], dq, dk, dv, part, s = backward_attention(
                    l, length, paired, g2s[m], x1, *sums[m], vectors, q, k, v, wq, w_out, tables, step()
                )
                ran(s)
                small.append((l, (1, 3), share, s))
                dps[m] = (dq, dk, dv)
                gs[m] = (g1, x, *links.start_sum(part))
            groups = [keep(l, 5), gas, keep(l, 1)] + [[d[j] for d in dps] for j in range(3)]
            streams.append(kind(links, "attention", l, layers, groups, step([gs[0][3]]), written))
            ran(streams[-1].token)
        tiny, ends, due = [], {}, {}

        def by(round_number, array):
            due.setdefault(round_number, []).append(array)

        def send_last(r):
            if paired:
                for m in range(parts):
                    x1, mine_part, theirs = heads[m]
                    heads[m] = (x1, mine_part, links.swap_tensor(hold(theirs, list(last))))
                    by(r + 2 + m, heads[m][2])

        def end_layers(r):
            cot = cotangent if paired else jnp.concatenate([g[0][0] for g in gs_first])
            ends["result"], s = last_layer(layers - 1, length, parts, tau, vectors, cot, heads, list(last))
            small.append((layers - 1, (4,), 1.0, s))
            by(r + 1, s)

        def end_input(r):
            rows_here = own if paired else gs[0][1].shape[0]
            ends["inputs"], s = input_gradient(0, paired, rows_here, vectors, gs, list(last))
            small.append((0, (0, 2), share, s))
            by(r + 1, s)

        def add_up(r):
            tiny.append(totals(small, layers, width, list(last)))
            by(r + 1, tiny[-1])

        def exchange(axis, pairs, r):
            got = lax.ppermute(tiny[-1], axis, pairs)
            by(r + 2, got)
            tiny.append((tiny[-1], got))

        def take(r):
            tiny.append(tiny[-1][0] + tiny[-1][1])

        nothing = lambda r: None
        errands = [nothing, nothing, end_input, send_last, nothing, nothing, end_layers, add_up]
        for j in range(links.dp.bit_length() - 1):
            pairs = [(i, i ^ (1 << j)) for i in range(links.dp)]
            errands += [functools.partial(exchange, "dp", pairs), take]
        if paired:
            errands += [functools.partial(exchange, "tensor", [(0, 1), (1, 0)]), take]
        for m in range(parts):
            by(1 + m, gs[m][3])
        r = 0
        while errands or any(s.going() for s in streams):
            last[:] = step(due.pop(r, []))
            if errands:
                errands.pop(0)(r)
            r += 1
        tiny = tiny[-1]
        result, inputs = ends["result"], ends["inputs"]
        if not paired:
            t = lax.axis_index("tensor")
            cut = lambda v: jnp.concatenate(
                [
                    lax.dynamic_slice_in_dim(v, m * v.shape[0] // parts + t * own, own)
                    for m in range(parts)
                ]
            )
            result, inputs = cut(result), cut(inputs)
        gains, biases = tiny[:, 0:2], tiny[:, 2:4]
        return (
            result,
            inputs,
            gains,
            biases,
            jnp.transpose(written["attention"][1], (0, 2, 1, 3)),
            written["attention"][0],
            written["mlp"][1],
            written["mlp"][0],
            tiny[:, 4],
            jnp.stack([gains[layers - 1, 1], biases[layers - 1, 1]]),
        )

    return local


def solution(mesh):
    links = Links(mesh.shape["dp"], mesh.shape["tensor"])
    token_spec = P(("dp", "tensor"), None)
    in_specs = (
        token_spec,
        P(("dp", "tensor")),
        P(),
        P(),
        P(),
        P(None, None, None, "tensor"),
        P(None, "tensor", None),
        P(None, None, "tensor"),
        P(None, "tensor", None),
        P(),
        token_spec,
    )
    out_specs = (
        token_spec,
        token_spec,
        P(),
        P(),
        P(None, None, None, "tensor"),
        P(None, "tensor", None),
        P(None, None, "tensor"),
        P(None, "tensor", None),
        P(),
        P(),
    )
    return jax.shard_map(
        make_local(links), mesh=mesh, in_specs=in_specs, out_specs=out_specs, check_vma=False
    )
```

```python
import functools
import math

import jax
import jax.numpy as jnp
import numpy as np
from jax import lax
from jax.experimental import pallas as pl
from jax.experimental.pallas import tpu as pltpu
from jax.sharding import PartitionSpec as P

HD = 64
bf16 = jnp.bfloat16
f32 = jnp.float32
epsilon = 1e-05


def mm(a, b):
    return jnp.dot(a, b, preferred_element_type=f32)


def mm_t(a, b):
    return lax.dot_general(a, b, (((1,), (1,)), ((), ())), preferred_element_type=f32)


def across(a, b):
    return lax.dot_general(a, b, (((0,), (0,)), ((), ())), preferred_element_type=f32)


def ein(spec, a, b):
    return jnp.einsum(spec, a, b, preferred_element_type=f32)


def gelu_parts(u):
    square = u * u
    s = 0.5 + 0.5 * jnp.tanh(u * (0.7978845608 + 0.7978845608 * 0.044715 * square))
    value = u * s
    slope = s + value * (1.0 - s) * (2.0 * 0.7978845608 + 6.0 * 0.7978845608 * 0.044715 * square)
    return value, slope


def standardize(v):
    centered = v - jnp.mean(v, axis=-1, keepdims=True)
    inverse = lax.rsqrt(jnp.mean(centered * centered, axis=-1, keepdims=True) + epsilon)
    return centered * inverse, inverse


def norm_backward(grad, xhat, inverse, gain):
    e = grad * gain
    return inverse * (
        e
        - jnp.mean(e, axis=-1, keepdims=True)
        - xhat * jnp.mean(e * xhat, axis=-1, keepdims=True)
    )


CHUNK = 32
BLOCK = 256


def rope_tables(length, width):
    half = HD // 2
    freqs = np.exp(-math.log(10000.0) * np.arange(half) * 2.0 / HD)
    angles = np.arange(length)[:, None] * freqs[None, :]
    heads = width // HD
    cos = np.tile(np.cos(angles), (1, 2 * heads))
    sin = np.tile(np.concatenate([-np.sin(angles), np.sin(angles)], axis=1), (1, heads))
    return jnp.asarray(cos, f32), jnp.asarray(sin, f32)


def partner(u):
    width = u.shape[1]
    lane = lax.broadcasted_iota(jnp.int32, u.shape, 1)
    low = (lane & (HD - 1)) < HD // 2
    return jnp.where(low, pltpu.roll(u, width - HD // 2, 1), pltpu.roll(u, HD // 2, 1))


GAIN, BIAS, TIME = 0, 1, 2


def vector(ref, group, row):
    at = group * (ref.shape[0] // 3) + row
    return ref[at : at + 1, :]


def chunks(rows, body, start=0):
    def step(i, carry):
        body(pl.multiple_of(i * CHUNK, CHUNK))
        return carry

    lax.fori_loop(start // CHUNK, rows // CHUNK, step, 0, unroll=4)


def rows_at(at):
    return pl.ds(at, CHUNK)


def other_rows(at, rows, swapped):
    if not swapped:
        return rows_at(at)
    half = rows // 2
    return rows_at(pl.multiple_of(jnp.where(at < half, at + half, at - half), CHUNK))


def fold(v):
    return jnp.sum(v.reshape(-1, 8, v.shape[-1]), axis=0)


LIMIT = 17 * 2**20
SMALL = 12 * 2**20


def call(kernel, ins, outs, scratch, flops, name, aliases={}, after=(), limit=LIMIT):
    count, late = len(ins), len(after)
    specs, args = [], []
    for a, away in ins:
        space = pltpu.SMEM if a.dtype == jnp.int32 else pltpu.HBM if away else pltpu.VMEM
        specs.append(pl.BlockSpec(memory_space=space))
        args.append(a if space == pltpu.SMEM else pltpu.with_memory_space_constraint(a, space))

    def run(*refs):
        kernel(*refs[:count], *refs[count + late :])

    return pl.pallas_call(
        run,
        out_shape=[(pltpu.HBM if away else pltpu.VMEM)(s, d) for s, d, away in outs],
        in_specs=specs + [pl.BlockSpec(memory_space=pl.ANY)] * late,
        out_specs=[pl.BlockSpec(memory_space=pltpu.HBM if away else pltpu.VMEM) for _, _, away in outs],
        scratch_shapes=scratch,
        input_output_aliases=aliases,
        compiler_params=pltpu.CompilerParams(vmem_limit_bytes=limit),
        cost_estimate=pl.CostEstimate(flops=20 * flops, bytes_accessed=2**20, transcendentals=0),
        name=name,
    )(*args, *after)


class Saver:
    def __init__(self, sems):
        self.sems, self.copies = sems, []

    def save(self, held, out):
        c = pltpu.make_async_copy(held, out, self.sems.at[len(self.copies)])
        c.start()
        self.copies.append(c)

    def wait(self):
        for c in self.copies:
            c.wait()


def masks():
    lane = lax.broadcasted_iota(jnp.int32, (1, 2 * HD), 1)
    return lane < HD


def both_heads(v, low):
    zero = jnp.zeros_like(v)
    return jnp.concatenate([jnp.where(low, v, zero), jnp.where(low, zero, v)], axis=0)


def halves(v):
    n = v.shape[1] // 2
    return v[:, :n], v[:, n:]


def softmax(scores):
    out = []
    for s in halves(scores):
        e = jnp.exp(s - jnp.max(s, axis=-1, keepdims=True))
        out.append(e * (1.0 / jnp.sum(e, axis=-1, keepdims=True)))
    return out


def beside(a, b):
    return jnp.concatenate([a, b], axis=1)


def forward_attention(layer, part_index, length, swapped, head, tau, vectors, w_qkv, w_out, tables):
    first = layer == 0
    rows = sum(n for _, _, n in head) if first else head[0].shape[0]
    width = w_out.shape[2]
    local = w_out.shape[1]
    block = min(BLOCK, local)
    scale = HD ** (-0.5)
    seqs = rows // length

    def kernel(*refs):
        it = iter(refs)
        take = lambda n: [next(it) for _ in range(n)]
        head_refs = take(len(head))
        tau_ref = None if first else take(1)[0]
        vec_ref, wq_any, wo_any, cos_any, sin_any = take(5)
        x_ref, part_ref = take(2)
        outs = take(6 if first else 7)
        wq, wo, cos_ref, sin_ref, sems, out_sems = take(6)
        n_ref, q_ref, k_ref, v_ref, att_ref = take(5)
        if first:
            held, = take(1)
        else:
            x2_ref, = take(1)
        saver = Saver(out_sems)
        if first:
            own = head_refs[0].at[pl.ds(head[0][1], head[0][2]), :]
            fetch = pltpu.make_async_copy(own, held, sems.at[4])
            fetch.start()
        ropes = [pltpu.make_async_copy(a, b, sems.at[5 + j]) for j, (a, b) in
                 enumerate(((cos_any, cos_ref), (sin_any, sin_ref)))]
        copies = [pltpu.make_async_copy(wq_any.at[layer, j], wq.at[j], sems.at[j]) for j in range(3)]
        copies.append(pltpu.make_async_copy(wo_any.at[layer], wo, sems.at[3]))
        for c in copies[:1] + ropes + copies[1:]:
            c.start()
        gain, bias = vector(vec_ref, GAIN, 2 * layer), vector(vec_ref, BIAS, 2 * layer)

        def norm(at, x):
            x_ref[rows_at(at), :] = x
            xhat, _ = standardize(x)
            n_ref[rows_at(at), :] = (xhat * gain + bias).astype(bf16)

        if first:
            count = head[0][2]
            if len(head) > 1:
                ref = head_refs[1]
                chunks(rows, lambda at: norm(at, ref[rows_at(at - count), :].astype(f32)), count)
            fetch.wait()
            chunks(count, lambda at: norm(at, held[rows_at(at), :].astype(f32)))
        else:
            x1, own, got = head_refs

            def scaled(at):
                here = rows_at(at)
                there = other_rows(at, rows, swapped)
                x2 = x1[here, :] + own[here, :].astype(f32) + got[there, :].astype(f32)
                x2_ref[here, :] = x2
                t = tau_ref[pl.ds(at // length * (tau.shape[0] // seqs) + part_index, 1), :]
                norm(at, x2 * (1.0 + t * vector(vec_ref, TIME, layer - 1)))

            chunks(rows, scaled)
            saver.save(x2_ref, outs[6])
        saver.save(x_ref, outs[0])
        saver.save(n_ref, outs[1])
        for c in ropes:
            c.wait()
        for j, out in enumerate((q_ref, k_ref, v_ref)):
            copies[j].wait()
            for b in range(0, local, block):
                u = mm(n_ref[...], wq[j, :, b : b + block])
                if j < 2:
                    for s in range(0, rows, length):
                        us = u[s : s + length]
                        us = us * cos_ref[:, b : b + block] + partner(us) * sin_ref[:, b : b + block]
                        out[s : s + length, b : b + block] = us.astype(bf16)
                else:
                    out[:, b : b + block] = u.astype(bf16)
            saver.save(out, outs[2 + j])
        low = masks()
        for s in range(0, rows, length):
            for b in range(0, local, 2 * HD):
                here = (slice(s, s + length), slice(b, b + 2 * HD))
                keys = both_heads(k_ref[here], low)
                probs = beside(*softmax(mm_t(q_ref[here], keys) * scale)).astype(bf16)
                att_ref[here] = mm(probs, both_heads(v_ref[here], low)).astype(bf16)
        saver.save(att_ref, outs[5])
        copies[3].wait()
        for b in range(0, width, BLOCK):
            part_ref[:, b : b + BLOCK] = mm(att_ref[...], wo[:, b : b + BLOCK]).astype(bf16)
        saver.wait()

    ins = [(a[0], j == 0) for j, a in enumerate(head)] if first else [(a, False) for a in head]
    ins += [] if first else [(tau, False)]
    ins += [(vectors, False), (w_qkv, True), (w_out, True)] + [(t, True) for t in tables]
    near = lambda n, d: ((rows, n), d, False)
    far = lambda n, d: ((rows, n), d, True)
    outs = [near(width, f32), near(width, bf16)]
    outs += [far(width, f32), far(width, bf16)] + [far(local, bf16)] * 4
    outs += [] if first else [far(width, f32)]
    scratch = [
        pltpu.VMEM((3, width, local), bf16),
        pltpu.VMEM((local, width), bf16),
        pltpu.VMEM((length, local), f32),
        pltpu.VMEM((length, local), f32),
        pltpu.SemaphoreType.DMA((7,)),
        pltpu.SemaphoreType.DMA((7,)),
        pltpu.VMEM((rows, width), bf16),
    ]
    scratch += [pltpu.VMEM((rows, local), bf16)] * 4
    scratch.append(pltpu.VMEM((head[0][2], width), bf16) if first else pltpu.VMEM((rows, width), f32))
    return call(kernel, ins, outs, scratch, 4 * 10**9, "forward_attention")


def forward_mlp(layer, swapped, x, own, got, vectors, w_up, w_down, after):
    rows, width = x.shape
    hidden = w_up.shape[2]
    tiles = hidden // BLOCK

    def kernel(x_ref, own_ref, got_ref, vec_ref, wu_any, wd_any, x1_ref, *refs):
        part_ref, x1_out, n_out, h_out, slope_out, n_ref, h_ref, slope_ref, wu, wd, sems, out_sems = refs
        saver = Saver(out_sems)
        gain, bias = vector(vec_ref, GAIN, 2 * layer + 1), vector(vec_ref, BIAS, 2 * layer + 1)
        ups = [
            pltpu.make_async_copy(
                wu_any.at[layer, :, pl.ds(t * BLOCK, BLOCK)], wu.at[t], sems.at[t]
            )
            for t in range(tiles)
        ]
        down = pltpu.make_async_copy(wd_any.at[layer], wd, sems.at[tiles])
        for c in ups:
            c.start()
        down.start()

        def norm(at):
            here = rows_at(at)
            there = other_rows(at, rows, swapped)
            x1 = x_ref[here, :] + own_ref[here, :].astype(f32) + got_ref[there, :].astype(f32)
            x1_ref[here, :] = x1
            xhat, _ = standardize(x1)
            n_ref[here, :] = (xhat * gain + bias).astype(bf16)

        chunks(rows, norm)
        saver.save(x1_ref, x1_out)
        saver.save(n_ref, n_out)
        for t in range(tiles):
            ups[t].wait()
            value, slope = gelu_parts(mm(n_ref[...], wu[t]))
            h_ref[:, t * BLOCK : (t + 1) * BLOCK] = value.astype(bf16)
            slope_ref[:, t * BLOCK : (t + 1) * BLOCK] = slope.astype(bf16)
        saver.save(h_ref, h_out)
        saver.save(slope_ref, slope_out)
        down.wait()
        for b in range(0, width, BLOCK):
            part_ref[:, b : b + BLOCK] = mm(h_ref[...], wd[:, b : b + BLOCK]).astype(bf16)
        saver.wait()

    ins = [(a, False) for a in (x, own, got, vectors)] + [(w_up, True), (w_down, True)]
    near = lambda n, d: ((rows, n), d, False)
    far = lambda n, d: ((rows, n), d, True)
    outs = [near(width, f32), near(width, bf16)]
    outs += [far(width, f32), far(width, bf16), far(hidden, bf16), far(hidden, bf16)]
    scratch = [
        pltpu.VMEM((rows, width), bf16),
        pltpu.VMEM((rows, hidden), bf16),
        pltpu.VMEM((rows, hidden), bf16),
        pltpu.VMEM((tiles, width, BLOCK), bf16),
        pltpu.VMEM((hidden, width), bf16),
        pltpu.SemaphoreType.DMA((tiles + 1,)),
        pltpu.SemaphoreType.DMA((4,)),
    ]
    return call(kernel, ins, outs, scratch, 6 * 10**9, "forward_mlp", after=after)


def last_layer(layer, length, swapped, own_rows, tau, vectors, rows_of, after):
    rows, width = rows_of[0][0].shape
    parts = len(rows_of)
    pieces = rows_of[0][3]

    def kernel(tau_ref, vec_ref, *refs):
        result_out, sums_ref, result_ref, sem = refs[-4:]
        sums_ref[...] = jnp.zeros_like(sums_ref)
        for m in range(parts):
            n = 3 + len(pieces)
            x1_ref, own_ref, got_ref, *cot_refs = refs[n * m : n * m + n]
            low = 0
            for ref, (_, start, count) in zip(cot_refs, rows_of[m][3]):

                def body(at, ref=ref, shift=start - low, mine=low < own_rows):
                    here = rows_at(at)
                    x2 = x1_ref[here, :] + own_ref[here, :].astype(f32)
                    x2 = x2 + got_ref[other_rows(at, rows, swapped), :].astype(f32)
                    t = tau_ref[pl.ds(at // length * parts + m, 1), :]
                    g = ref[rows_at(pl.multiple_of(at + shift, CHUNK)), :].astype(f32)
                    sums_ref[...] += fold(g * x2) * t
                    if mine:
                        result_ref[rows_at(pl.multiple_of(at + m * own_rows, CHUNK)), :] = x2 * (
                            1.0 + t * vector(vec_ref, TIME, layer)
                        )

                chunks(low + count, body, low)
                low += count
        c = pltpu.make_async_copy(result_ref, result_out, sem)
        c.start()
        c.wait()

    ins = [(tau, False), (vectors, False)]
    for x1, mine, got, cot in rows_of:
        ins += [(v, False) for v in (x1, mine, got)] + [(v, False) for v, _, _ in cot]
    shape = (own_rows * parts, width)
    outs = [(shape, f32, True), ((8, width), f32, False)]
    scratch = [pltpu.VMEM(shape, f32), pltpu.SemaphoreType.DMA]
    return call(kernel, ins, outs, scratch, 10**8, "last_layer", after=after, limit=SMALL)


def backward_mlp(layer, last, part_index, length, swapped, head, x2, tau, vectors, slope, w_up, w_down, after):
    rows = slope.shape[0]
    width = vectors.shape[1]
    hidden = w_up.shape[2]
    tiles = hidden // BLOCK
    seqs = rows // length
    parts = tau.shape[0] // seqs

    def kernel(*refs):
        it = iter(refs)
        take = lambda n: [next(it) for _ in range(n)]
        head_refs = take(len(head))
        x2_ref = None if last else take(1)[0]
        tau_ref, vec_ref, slope_ref, wu_any, wd_any = take(5)
        g2_ref, gm_ref, du_ref, part_ref, sums_ref = take(5)
        wu, wd, sems = take(3)
        downs = [
            pltpu.make_async_copy(
                wd_any.at[layer, pl.ds(t * BLOCK, BLOCK), :], wd.at[t], sems.at[t]
            )
            for t in range(tiles)
        ]
        up = pltpu.make_async_copy(wu_any.at[layer], wu, sems.at[tiles])
        for c in downs:
            c.start()
        up.start()
        sums_ref[...] = jnp.zeros_like(sums_ref)

        def begin(at, g):
            here = rows_at(at)
            t = tau_ref[pl.ds(at // length * parts + part_index, 1), :]
            if not last:
                sums_ref[16:24, :] += fold(g * x2_ref[here, :]) * t
            g2 = g * (1.0 + t * vector(vec_ref, TIME, layer))
            g2_ref[here, :] = g2
            gm_ref[here, :] = g2.astype(bf16)

        if last:
            low = 0
            for ref, (_, start, count) in zip(head_refs, head):
                chunks(
                    low + count,
                    lambda at, ref=ref, shift=start - low: begin(
                        at, ref[rows_at(pl.multiple_of(at + shift, CHUNK)), :].astype(f32)
                    ),
                    low,
                )
                low += count
        else:
            g1, x, own, got = head_refs

            def through_norm(at):
                here = rows_at(at)
                dn = own[here, :].astype(f32) + got[other_rows(at, rows, swapped), :].astype(f32)
                xhat, inverse = standardize(x[here, :])
                sums_ref[0:8, :] += fold(dn * xhat)
                sums_ref[8:16, :] += fold(dn)
                begin(at, g1[here, :] + norm_backward(dn, xhat, inverse, vector(vec_ref, GAIN, 2 * layer + 2)))

            chunks(rows, through_norm)
        for t in range(tiles):
            downs[t].wait()
            at = slice(t * BLOCK, (t + 1) * BLOCK)
            dh = mm_t(gm_ref[...], wd[t])
            du_ref[:, at] = (dh * slope_ref[:, at].astype(f32)).astype(bf16)
        up.wait()
        for b in range(0, width, BLOCK):
            part_ref[:, b : b + BLOCK] = mm_t(du_ref[...], wu[b : b + BLOCK, :]).astype(bf16)

    ins = [(a[0] if last else a, False) for a in head]
    ins += [] if last else [(x2, False)]
    ins += [(a, False) for a in (tau, vectors, slope)]
    ins += [(w_up, True), (w_down, True)]
    near = lambda n, d: ((rows, n), d, False)
    outs = [near(width, f32), near(width, bf16), near(hidden, bf16), near(width, bf16)]
    outs += [((24, width), f32, False)]
    scratch = [
        pltpu.VMEM((width, hidden), bf16),
        pltpu.VMEM((tiles, BLOCK, width), bf16),
        pltpu.SemaphoreType.DMA((tiles + 1,)),
    ]
    return call(kernel, ins, outs, scratch, 6 * 10**9, "backward_mlp", after=after)


def input_gradient(layer, swapped, own_rows, vectors, rows_of, after):
    rows, width = rows_of[0][1].shape

    def kernel(vec_ref, *refs):
        out_far, sums_ref, out_ref, sem = refs[-4:]
        sums_ref[...] = jnp.zeros_like(sums_ref)
        for m in range(len(rows_of)):
            g1_ref, x_ref, own_ref, got_ref = refs[4 * m : 4 * m + 4]

            def body(at, mine):
                here = rows_at(at)
                dn = own_ref[here, :].astype(f32) + got_ref[other_rows(at, rows, swapped), :].astype(f32)
                xhat, inverse = standardize(x_ref[here, :])
                sums_ref[0:8, :] += fold(dn * xhat)
                sums_ref[8:16, :] += fold(dn)
                if mine:
                    out_ref[rows_at(pl.multiple_of(at + m * own_rows, CHUNK)), :] = g1_ref[here, :] + norm_backward(
                        dn, xhat, inverse, vector(vec_ref, GAIN, 2 * layer)
                    )

            chunks(own_rows, lambda at: body(at, True))
            chunks(rows, lambda at: body(at, False), own_rows)
        c = pltpu.make_async_copy(out_ref, out_far, sem)
        c.start()
        c.wait()

    ins = [(vectors, False)] + [(v, False) for part in rows_of for v in part]
    shape = (own_rows * len(rows_of), width)
    outs = [(shape, f32, True), ((16, width), f32, False)]
    scratch = [pltpu.VMEM(shape, f32), pltpu.SemaphoreType.DMA]
    return call(kernel, ins, outs, scratch, 10**8, "input_gradient", after=after, limit=SMALL)


def totals(sums, layers, width, core, place, after):
    half_width = width // 2
    shape = (8, 16, half_width)

    def kernel(s_ref, *refs):
        send_ref, keep_ref, all_ref = refs[-3:]
        all_ref[...] = jnp.zeros_like(all_ref)
        for ref, (layer, rows, _) in zip(refs, sums):
            for j, row in enumerate(rows):
                if row is not None:
                    all_ref[layer, row : row + 1, :] += jnp.sum(ref[8 * j : 8 * j + 8, :], axis=0, keepdims=True)
        rows = lax.broadcasted_iota(jnp.int32, (16, half_width), 0)
        for target, half, p in (
            (send_ref, 1 - s_ref[0], lax.rem(8 - s_ref[1], 8)),
            (keep_ref, s_ref[0], s_ref[1]),
        ):
            for b in range(8):
                v = all_ref[half, b : b + 1, :]
                block = jnp.where(rows == 0, v[:, :half_width], jnp.where(rows == 1, v[:, half_width:], 0.0))
                target[lax.rem(p - b + 8, 8)] = block.astype(bf16)

    ins = [(jnp.stack([core, place]).astype(jnp.int32), False)] + [(v, False) for _, _, v in sums]
    outs = [(shape, bf16, False)] * 2
    scratch = [pltpu.VMEM((2, 8, width), f32)]
    return call(kernel, ins, outs, scratch, 10**8, "totals", after=after, limit=SMALL)


def backward_attention(layer, length, swapped, g2, x1, own, got, vectors, q, k, v, w_qkv, w_out, tables, after):
    rows, width = x1.shape
    local = w_out.shape[1]
    block = min(BLOCK, local)
    scale = HD ** (-0.5)

    def kernel(g2_ref, x1_ref, own_ref, got_ref, vec_ref, q_ref, k_ref, v_ref, wq_any, wo_any, cos_any, sin_any,
               g1_ref, ga_ref, dq_ref, dk_ref, dv_ref, part_ref, sums_ref, wq, wo, do_ref, cos_ref, sin_ref, sems):
        copies = [pltpu.make_async_copy(wo_any.at[layer], wo, sems.at[3])]
        copies += [pltpu.make_async_copy(cos_any, cos_ref, sems.at[4])]
        copies += [pltpu.make_async_copy(sin_any, sin_ref, sems.at[5])]
        copies += [pltpu.make_async_copy(wq_any.at[layer, j], wq.at[j], sems.at[j]) for j in range(3)]
        for c in copies:
            c.start()
        sums_ref[...] = jnp.zeros_like(sums_ref)

        def begin(at):
            here = rows_at(at)
            dn = own_ref[here, :].astype(f32) + got_ref[other_rows(at, rows, swapped), :].astype(f32)
            xhat, inverse = standardize(x1_ref[here, :])
            sums_ref[0:8, :] += fold(dn * xhat)
            sums_ref[8:16, :] += fold(dn)
            g1 = g2_ref[here, :] + norm_backward(dn, xhat, inverse, vector(vec_ref, GAIN, 2 * layer + 1))
            g1_ref[here, :] = g1
            ga_ref[here, :] = g1.astype(bf16)

        chunks(rows, begin)
        for c in copies[:3]:
            c.wait()
        for b in range(0, local, block):
            do_ref[:, b : b + block] = mm_t(ga_ref[...], wo[b : b + block, :]).astype(bf16)
        low = masks()
        for s in range(0, rows, length):
            for b in range(0, local, 2 * HD):
                here = (slice(s, s + length), slice(b, b + 2 * HD))
                lanes = slice(b, b + 2 * HD)
                keys = both_heads(k_ref[here], low)
                grad = do_ref[here]
                probs = softmax(mm_t(q_ref[here], keys) * scale)
                dps = halves(mm_t(grad, both_heads(v_ref[here], low)))
                ds = [p * (d - jnp.sum(p * d, axis=-1, keepdims=True)) for p, d in zip(probs, dps)]
                across_heads = lambda v, w: mm(beside(v[0].T, v[1].T).astype(bf16), both_heads(w, low))
                dv_ref[here] = across_heads(probs, grad).astype(bf16)
                dq = mm(beside(*ds).astype(bf16), keys) * scale
                dk = across_heads(ds, q_ref[here]) * scale
                for d, out in ((dq, dq_ref), (dk, dk_ref)):
                    out[here] = (d * cos_ref[:, lanes] + partner(d * sin_ref[:, lanes])).astype(bf16)
        for c in copies[3:]:
            c.wait()
        for b in range(0, width, BLOCK):
            at = slice(b, b + BLOCK)
            part = mm_t(dq_ref[...], wq[0, at, :]) + mm_t(dk_ref[...], wq[1, at, :])
            part_ref[:, at] = (part + mm_t(dv_ref[...], wq[2, at, :])).astype(bf16)

    ins = [(a, False) for a in (g2, x1, own, got, vectors, q, k, v)] + [(w_qkv, True), (w_out, True)]
    ins += [(t, True) for t in tables]
    near = lambda n, d: ((rows, n), d, False)
    outs = [near(width, f32), near(width, bf16)] + [near(local, bf16)] * 3
    outs += [near(width, bf16), ((16, width), f32, False)]
    scratch = [
        pltpu.VMEM((3, width, local), bf16),
        pltpu.VMEM((local, width), bf16),
        pltpu.VMEM((rows, local), bf16),
        pltpu.VMEM((length, local), f32),
        pltpu.VMEM((length, local), f32),
        pltpu.SemaphoreType.DMA((6,)),
    ]
    return call(kernel, ins, outs, scratch, 7 * 10**9, "backward_attention", after=after)


class Links:
    def __init__(self, dp, tensor):
        self.dp, self.tensor = dp, tensor
        self.chips = dp // 2
        self.ring = dp == 16
        self.walk = [0, 2, 4, 6, 7, 5, 3, 1]
        self.ring_pairs = []
        for k in range(8):
            here, there = self.walk[k], self.walk[(k + 1) % 8]
            self.ring_pairs.append((2 * here, 2 * there))
            self.ring_pairs.append((2 * there + 1, 2 * here + 1))
        self.core_pairs = [(i, i ^ 1) for i in range(dp)]

    def ring_place(self):
        i = lax.axis_index("dp")
        z, x = i >> 2, (i >> 1) & 1
        p = jnp.where(x == 0, z, 7 - z)
        return jnp.where(i & 1 == 0, p, (8 - p) & 7)

    def swap_tensor(self, v):
        return lax.ppermute(v, "tensor", [(0, 1), (1, 0)])

    def gather_tensor(self, v):
        if self.tensor != 2:
            return lax.all_gather(v, "tensor", axis=0, tiled=True)
        other = self.swap_tensor(v)
        first = lax.axis_index("tensor") == 0
        return jnp.concatenate([jnp.where(first, v, other), jnp.where(first, other, v)])

    def start_sum(self, part):
        part = part.astype(bf16)
        if self.tensor != 2:
            summed = lax.psum(part, "tensor")
            return (summed, jnp.zeros_like(summed))
        return (part, self.swap_tensor(part))

def total(parts):
    out = parts[0].astype(f32)
    for p in parts[1:]:
        out = out + p.astype(f32)
    return out


def over_rows(lefts, rights):
    return across(jnp.concatenate(lefts), jnp.concatenate(rights))


def mlp_gradients(h, gm, n2, du, core, place, after):
    n = len(h)
    hidden, width = h[0].shape[1], gm[0].shape[1]
    half_hidden = hidden // 2
    tall = half_hidden // 8
    wide = width // 8

    def kernel(s_ref, *refs):
        hs, gms, ns, dus = [refs[n * j : n * j + n] for j in range(4)]
        send_out, keep_ref, send_ref, sems = refs[4 * n :]

        def make(target, half, p, ended):
            gm_all = jnp.concatenate([r[...] for r in gms])
            columns = slice(half * half_hidden, (half + 1) * half_hidden)
            du_all = jnp.concatenate([r[:, columns] for r in dus])
            for j in range(4):
                first = half * half_hidden + j * 2 * tall
                down = across(jnp.concatenate([r[:, first : first + 2 * tall] for r in hs]), gm_all)
                up = across(jnp.concatenate([r[:, j * 2 * wide : (j + 1) * 2 * wide] for r in ns]), du_all)
                for i in range(2):
                    slot = lax.rem(p - (2 * j + i) + 8, 8)
                    target[slot, 0:tall, :] = down[i * tall : (i + 1) * tall].astype(bf16)
                    target[slot, tall : tall + wide, :] = up[i * wide : (i + 1) * wide].astype(bf16)
                    ended(slot, 2 * j + i)

        def away(slot, i):
            pltpu.make_async_copy(send_ref.at[slot], send_out.at[slot], sems.at[i]).start()

        for c in range(2):

            @pl.when(s_ref[0] == c)
            def _():
                make(send_ref, 1 - c, lax.rem(8 - s_ref[1], 8), away)
                make(keep_ref, c, s_ref[1], lambda slot, i: None)

        for i in range(8):
            slot = lax.rem(lax.rem(8 - s_ref[1], 8) - i + 8, 8)
            pltpu.make_async_copy(send_ref.at[slot], send_out.at[slot], sems.at[i]).wait()

    ins = [(jnp.stack([core, place]).astype(jnp.int32), False)]
    ins += [(v, False) for group in (h, gm, n2, du) for v in group]
    shape = (8, tall + wide, width)
    scratch = [pltpu.VMEM(shape, bf16), pltpu.SemaphoreType.DMA((8,))]
    outs = [(shape, bf16, True), (shape, bf16, False)]
    return call(kernel, ins, outs, scratch, 9 * 10**9, "mlp_gradients", after=after, limit=SMALL)


def attention_gradients(att, ga, n1, dq, dk, dv, core, place, after):
    n = len(att)
    local, width = att[0].shape[1], ga[0].shape[1]
    heads, wide = local // 2, width // 2

    def kernel(s_ref, *refs):
        atts, gas, ns = [refs[n * j : n * j + n] for j in range(3)]
        dps = [refs[n * j : n * j + n] for j in range(3, 6)]

        def make(target, half, p):
            def put(value, low, size):
                for b in range(8):
                    slot = lax.rem(p - b + 8, 8)
                    target[slot, low : low + size, :] = value[b * size : (b + 1) * size].astype(bf16)

            lefts = [r[:, half * heads : (half + 1) * heads] for r in atts]
            for j in range(2):
                put(over_rows(lefts, [r[:, j * wide : (j + 1) * wide] for r in gas]), heads // 8 * j, heads // 8)
            lefts = [r[:, half * wide : (half + 1) * wide] for r in ns]
            for j in range(3):
                put(over_rows(lefts, [r[...] for r in dps[j]]), heads // 4 + wide // 8 * j, wide // 8)

        for c in range(2):

            @pl.when(s_ref[0] == c)
            def _():
                make(refs[6 * n], 1 - c, lax.rem(8 - s_ref[1], 8))
                make(refs[6 * n + 1], c, s_ref[1])

    ins = [(jnp.stack([core, place]).astype(jnp.int32), False)]
    ins += [(v, False) for group in (att, ga, n1, dq, dk, dv) for v in group]
    out = ((8, heads // 4 + 3 * wide // 8, local), bf16, False)
    return call(kernel, ins, [out, out], [], 5 * 10**9, "attention_gradients", after=after, limit=SMALL)


def pack(lanes, after):
    depths = [lane[0].shape[0] for lane in lanes]
    count, width = len(lanes[0]), lanes[0][0].shape[1]

    def kernel(*refs):
        low = 0
        for j, depth in enumerate(depths):
            for i in range(count):
                refs[-1][i, low : low + depth, :] = refs[j * count + i][...]
            low += depth

    out = ((count, sum(depths), width), bf16, False)
    ins = [(v, False) for lane in lanes for v in lane]
    return call(kernel, ins, [out], [], 10**8, "pack", after=after, limit=SMALL)[0]


def merge(pairs, lanes, after):
    count, _, width = pairs[0][0].shape
    depths = [a.shape[1] for a, _ in pairs]
    depth = sum(depths) // lanes

    def kernel(*refs):
        ins, outs = refs[: 2 * len(pairs)], refs[2 * len(pairs) :]

        def total(i, j):
            if lanes == 1:
                return jnp.concatenate(
                    [
                        (ins[2 * n][i].astype(f32) + ins[2 * n + 1][i].astype(f32)).astype(bf16)
                        for n in range(len(pairs))
                    ]
                )
            at = slice(j * depth, (j + 1) * depth)
            return (ins[0][i, at, :].astype(f32) + ins[1][i, at, :].astype(f32)).astype(bf16)

        for j in range(lanes):
            outs[2 * j][...] = total(0, j)

        def body(i, carry):
            for j in range(lanes):
                outs[2 * j + 1][i] = total(i, j)
            return carry

        lax.fori_loop(1, count, body, 0)

    outs = [((depth, width), bf16, False), ((count, depth, width), bf16, False)] * lanes
    ins = [(v, False) for pair in pairs for v in pair]
    out = call(kernel, ins, outs, [], 10**8, "merge", after=after, limit=SMALL)
    return out[0::2], out[1::2]


def add(a, blocks, i, after):
    def kernel(a_ref, b_ref, out_ref):
        out_ref[...] = (a_ref[...].astype(f32) + b_ref[i].astype(f32)).astype(bf16)

    outs = [(a.shape, bf16, False)]
    return call(kernel, [(a, False), (blocks, False)], outs, [], 10**8, "add", after=after, limit=SMALL)[0]


def hold(a, after):
    def kernel(a_ref, out_ref):
        out_ref[...] = a_ref[...]

    return call(kernel, [(a, False)], [(a.shape, a.dtype, False)], [], 10**8, "hold", after=after, limit=SMALL)[0]


DEEP = 4


def spread(pieces, shapes, blocks, begin, own, core, place, before, after):
    count, depth, width = blocks.shape
    deep = min(DEEP, count)

    def kernel(s_ref, block_ref, *refs):
        token_ref, held, sems = refs[-3:]
        outs = refs[len(refs) - 3 - len(shapes) : -3]
        token_ref[...] = jnp.zeros_like(token_ref)

        def copies(i):
            half, p = (s_ref[0], s_ref[1]) if own else (1 - s_ref[0], lax.rem(8 - s_ref[1], 8))
            b = lax.rem(p + 1 - begin - i + 16, 8)
            return [
                pltpu.make_async_copy(
                    held.at[(i % deep,) + source], outs[o].at[place], sems.at[i % deep, j]
                )
                for j, (source, o, place) in enumerate(pieces(half, b))
            ]

        for i in range(count):
            if i >= deep:
                for c in copies(i - deep):
                    c.wait()
            held[i % deep] = block_ref[i].astype(f32)
            for c in copies(i):
                c.start()
        for i in range(count - deep, count):
            for c in copies(i):
                c.wait()

    ins = [(jnp.stack([core, place]).astype(jnp.int32), False), (blocks, False)]
    aliases = {}
    for j, v in enumerate(before):
        aliases[len(ins)] = j
        ins.append((v, True))
    scratch = [
        pltpu.VMEM((deep, depth, width), f32),
        pltpu.SemaphoreType.DMA((deep, len(pieces(0, 0)))),
    ]
    outs = [(s, f32, True) for s in shapes] + [((8, 128), f32, False)]
    *outs, token = call(kernel, ins, outs, scratch, 10**8, "spread", aliases, after=after, limit=SMALL)
    return outs, token


def mlp_pieces(layer, layers, hidden, width):
    tall, wide = hidden // 16, width // 8

    def pieces(half, b):
        rows = pl.ds(pl.multiple_of(half * (hidden // 2) + b * tall, tall), tall)
        across_rows = pl.ds(pl.multiple_of(b * wide, wide), wide)
        columns = pl.ds(pl.multiple_of(half * (hidden // 2), hidden // 2), hidden // 2)
        return [
            ((slice(0, tall), slice(None)), 0, (layer, rows, slice(None))),
            ((slice(tall, tall + wide), slice(None)), 1, (layer, across_rows, columns)),
        ]

    return pieces, [(layers, hidden, width), (layers, width, hidden)]


def attention_pieces(layer, layers, local, width):
    tall, wide = local // 16, width // 16

    def pieces(half, b):
        rows = pl.ds(pl.multiple_of(half * (local // 2) + b * tall, tall), tall)
        deep = pl.ds(pl.multiple_of(half * (width // 2) + b * wide, wide), wide)
        out = []
        for j in range(2):
            columns = slice(j * width // 2, (j + 1) * width // 2)
            out.append(((slice(tall * j, tall * (j + 1)), slice(None)), 0, (layer, rows, columns)))
        for j in range(3):
            low = 2 * tall + wide * j
            out.append(((slice(low, low + wide), slice(None)), 1, (layer, j, deep, slice(None))))
        return out

    return pieces, [(layers, local, width), (layers, 3, width, local)]


def small_outputs(ends, begins, layers, width, core, place):
    row = ends[0][0].shape[1] - 16
    half_width = width // 2

    def kernel(s_ref, *refs):
        outs, held = refs[2 * len(ends) : 2 * len(ends) + 4], refs[2 * len(ends) + 4 : -1]
        gains, biases, times, norms = held

        def put(source, half, p):
            for b in range(5):
                slot = lax.rem(p + 1 - b + 16, 8)
                for n, begin in enumerate(begins):
                    ref = refs[2 * n + source]

                    @pl.when((slot >= begin) & (slot < begin + ref.shape[0]))
                    def _():
                        for j in range(2):
                            v = ref[slot - begin, row : row + 16, :].astype(f32)[j : j + 1, :]
                            at = slice(j * half_width, (j + 1) * half_width)
                            if b == 4:
                                times[half : half + 1, at] = v
                            else:
                                (gains, biases)[b // 2][half, b % 2 : b % 2 + 1, at] = v

        for c in range(2):

            @pl.when(s_ref[0] == c)
            def _():
                put(0, c, s_ref[1])
                put(1, 1 - c, 8 - s_ref[1])

        norms[0:1, :] = gains[layers - 1, 1:2, :]
        norms[1:2, :] = biases[layers - 1, 1:2, :]
        copies = [pltpu.make_async_copy(a, b, refs[-1].at[j]) for j, (a, b) in enumerate(zip(held, outs))]
        for c in copies:
            c.start()
        for c in copies:
            c.wait()

    shapes = [(layers, 2, width), (layers, 2, width), (layers, width), (2, width)]
    ins = [(jnp.stack([core, place]).astype(jnp.int32), False)] + [(v, False) for pair in ends for v in pair]
    scratch = [pltpu.VMEM(s, f32) for s in shapes] + [pltpu.SemaphoreType.DMA((4,))]
    return call(kernel, ins, [(s, f32, True) for s in shapes], scratch, 10**8, "small_outputs", limit=SMALL)


class Stream:
    def __init__(self, links, kind, layer, layers, groups, after, written):
        self.links, self.kind, self.written = links, kind, written
        self.steps = -2
        self.extra = []
        self.cuts = [(0, 5), (5, 8)] if kind == "attention" and layer == 0 else [(0, 8)]
        self.packed = []
        self.lanes = LANES[kind][min(layer, 1)]
        self.core = lax.axis_index("dp") & 1
        self.p = links.ring_place()
        if kind == "mlp":
            send, self.blocks = mlp_gradients(*groups, self.core, self.p, after)
            self.layout = mlp_pieces(layer, layers, groups[0][0].shape[1], groups[1][0].shape[1])
        else:
            send, self.blocks = attention_gradients(*groups, self.core, self.p, after)
            self.layout = attention_pieces(layer, layers, groups[0][0].shape[1], groups[1][0].shape[1])
        self.raw = lax.ppermute(send, "dp", links.core_pairs)
        self.done = [[] for _ in range(self.lanes)]
        self.token = self.blocks

    def step(self, after):
        self.steps += 1
        if self.steps < 0:
            return []
        out = []
        if self.steps == 14:
            for lane, v in zip(self.done, self.raw):
                lane.append(v)
        if self.packed and len(self.packed[-1]) == 2 and not self.packed[-1][-1][1]:
            (_, peer), state = self.packed[-1][0], self.packed[-1][-1]
            state[1] = True
            out.append(self.write(peer, state[0], False, after))
        if self.steps == 15:
            return out
        for low, high in self.cuts:
            if self.steps == min(high + 7, 14):
                mine = pack([lane[low:high] for lane in self.done], after)
                peer = lax.ppermute(mine, "dp", self.links.core_pairs)
                out.append(self.write(mine, low, True, []))
                self.packed.append(((mine, peer), [low, False]))
        if self.steps == 14:
            return out
        if self.steps == 0:
            now, self.blocks = merge([(self.blocks, self.raw)] + self.extra, self.lanes, after)
        elif self.steps < 8:
            now = [add(r, b, self.steps, after) for r, b in zip(self.raw, self.blocks)]
        else:
            now = [hold(r, after) for r in self.raw]
        if self.steps >= 7:
            for lane, v in zip(self.done, now):
                lane.append(v)
        self.raw = [lax.ppermute(v, "dp", self.links.ring_pairs) for v in now]
        return out + list(now)

    def write(self, blocks, begin, own, after):
        before = self.written.get(self.kind, [])
        self.written[self.kind], token = spread(
            *self.layout, blocks, begin, own, self.core, self.p, before, after
        )
        return token

    def going(self):
        return self.steps < 15


LANES = {"mlp": (2, 1), "attention": (1, 1)}


class Plain:
    def __init__(self, links, kind, layer, layers, groups, after, written):
        left, right, deep, *dps = [jnp.concatenate(g) for g in groups]
        out = [ein("ra,rb->ab", left, right)]
        if kind == "mlp":
            out.append(ein("ra,rb->ab", deep, dps[0]))
        else:
            out.append(jnp.stack([ein("ra,rb->ab", deep, d) for d in dps]))
        out = [lax.psum(v.astype(bf16), "dp").astype(f32) for v in out]
        if kind not in written:
            written[kind] = [jnp.zeros((layers,) + v.shape, f32) for v in out]
        written[kind] = [b.at[layer].set(v) for b, v in zip(written[kind], out)]
        self.token = after[0]

    def going(self):
        return False

def make_local(links):
    def local(
        tokens,
        time_index,
        time_table,
        norm_gain,
        norm_bias,
        w_qkv,
        w_out,
        w_up,
        w_down,
        time_weight,
        cotangent,
    ):
        rows, width = tokens.shape
        seq_here = time_index.shape[0]
        length = rows // seq_here
        layers = norm_gain.shape[0]
        local_width = w_out.shape[1]
        tables = rope_tables(length, local_width)
        parts = 2 if seq_here % 2 == 0 else 1
        own = rows // parts
        paired = links.tensor == 2
        wq = jnp.transpose(w_qkv, (0, 2, 1, 3))

        def group_rows(v, m, after=()):
            if paired:
                mine = v[m * own : (m + 1) * own]
                got = links.swap_tensor(hold(mine, after) if after else mine)
                return [(v, m * own, own), (got, 0, own)]
            v = links.gather_tensor(v[m * own : (m + 1) * own])
            return [(v, 0, v.shape[0])]

        heads = [group_rows(tokens, 0)]
        heads += [group_rows(tokens, m, [heads[-1][-1][0]]) for m in range(1, parts)]
        gs = [group_rows(cotangent, m, [heads[-1][-1][0]]) for m in range(parts)]
        arrived = [g[-1][0] for g in gs]
        vectors = [norm_gain.reshape(2 * layers, width), norm_bias.reshape(2 * layers, width)]
        vectors += [time_weight, jnp.zeros((layers, width), f32)]
        vectors = jnp.concatenate(vectors)
        if paired:
            index = jnp.concatenate([time_index, links.swap_tensor(time_index)])
        else:
            index = links.gather_tensor(time_index)
        onehot = (index[:, None] == jnp.arange(time_table.shape[0], dtype=jnp.int32)[None, :]).astype(f32)
        tau = jnp.dot(onehot, time_table, precision=lax.Precision.HIGHEST)
        saved = [[None] * parts for _ in range(layers)]
        after = [[None] * parts for _ in range(layers)]
        for l in range(layers):
            for m in range(parts):
                x_near, part, *out = forward_attention(
                    l, m, length, paired, heads[m], tau, vectors, wq, w_out, tables
                )
                if l > 0:
                    after[l - 1][m] = out.pop()
                saved[l][m] = out
                heads[m] = (x_near, *links.start_sum(part))
            for m in range(parts):
                x1, part, *out = forward_mlp(l, paired, *heads[m], vectors, w_up, w_down, arrived)
                heads[m] = (x1, part) if l == layers - 1 else (x1, *links.start_sum(part))
                saved[l][m] += out
                arrived = []

        kind = Stream if links.ring else Plain
        streams = []
        small = []
        keep = lambda l, i: [s[i] for s in saved[l]]

        last, written = [], {}

        def step(also=()):
            before = list(also)
            for s in streams:
                if s.going():
                    before += s.step(list(last))
            return before

        def ran(out):
            last[:] = [out]

        gs_first = gs
        gs = list(gs)
        for l in reversed(range(layers)):
            g2s, gms, dus, sums = [None] * parts, [None] * parts, [None] * parts, [None] * parts
            gas, dps = [None] * parts, [None] * parts
            for m in range(parts):
                g2s[m], gms[m], dus[m], part, s = backward_mlp(
                    l, l == layers - 1, m, length, paired, gs[m], after[l][m], tau, vectors, saved[l][m][9],
                    w_up, w_down, step(),
                )
                ran(s)
                if l < layers - 1:
                    small.append((l + 1, (0, 2), s))
                    small.append((l, (None, None, 4), s))
                sums[m] = links.start_sum(part)

            def mlp_stream(also):
                groups = [keep(l, 8), gms, keep(l, 7), dus]
                streams.append(kind(links, "mlp", l, layers, groups, step(also), written))
                ran(streams[-1].token)

            if l > 0:
                mlp_stream([sums[0][1]])
            for m in range(parts):
                x, n1, q, k, v, att, x1 = saved[l][m][:7]
                g1, gas[m], dq, dk, dv, part, s = backward_attention(
                    l, length, paired, g2s[m], x1, *sums[m], vectors, q, k, v, wq, w_out, tables, step()
                )
                ran(s)
                small.append((l, (1, 3), s))
                dps[m] = (dq, dk, dv)
                gs[m] = (g1, x, *links.start_sum(part))
                if m == 0 and l == 0:
                    mlp_stream([sums[-1][1]])
            groups = [keep(l, 5), gas, keep(l, 1)] + [[d[j] for d in dps] for j in range(3)]
            streams.append(kind(links, "attention", l, layers, groups, step([gs[0][3]]), written))
            ran(streams[-1].token)
        final = streams[-1]
        own_here = own if paired else gs[0][1].shape[0]

        def send_last():
            for m in range(parts):
                x1, part = heads[m]
                held = hold(part, list(last)) if links.ring else part
                heads[m] = (x1, *links.start_sum(held), gs_first[m])
                heads[m] = (x1, part, heads[m][2], gs_first[m]) if paired else heads[m]

        def end_layers():
            inputs, s = input_gradient(0, paired, own_here, vectors, gs, list(last))
            small.append((0, (0, 2), s))
            result, s = last_layer(layers - 1, length, paired, own_here, tau, vectors, heads, list(last) + [s])
            small.append((layers - 1, (4,), s))
            return inputs, result

        send_last()
        if links.ring:
            last[:] = step()
            inputs, result = end_layers()
            send, kept = totals(small, layers, width, final.core, final.p, list(last))
            final.extra = [(kept, lax.ppermute(send, "dp", links.core_pairs))]
            final.steps -= 1
            while any(s.going() for s in streams):
                last[:] = step()
            ends = [pair for pair, _ in final.packed]
            begins = [low for low, _ in final.cuts]
            gains, biases, times, norms = small_outputs(ends, begins, layers, width, final.core, final.p)
        else:
            inputs, result = end_layers()
            tiny = jnp.zeros((layers, 8, width), f32)
            for l, rows_of, s in small:
                for j, row in enumerate(rows_of):
                    if row is not None:
                        tiny = tiny.at[l, row].add(jnp.sum(s[8 * j : 8 * j + 8], axis=0))
            tiny = lax.psum(tiny, "dp")
            gains, biases, times = tiny[:, 0:2], tiny[:, 2:4], tiny[:, 4]
            norms = jnp.stack([gains[layers - 1, 1], biases[layers - 1, 1]])
        if not paired:
            t = lax.axis_index("tensor")
            cut = lambda v: jnp.concatenate(
                [
                    lax.dynamic_slice_in_dim(v, m * v.shape[0] // parts + t * own, own)
                    for m in range(parts)
                ]
            )
            result, inputs = cut(result), cut(inputs)
        return (
            result,
            inputs,
            gains,
            biases,
            jnp.transpose(written["attention"][1], (0, 2, 1, 3)),
            written["attention"][0],
            written["mlp"][1],
            written["mlp"][0],
            times,
            norms,
        )

    return local


def solution(mesh):
    links = Links(mesh.shape["dp"], mesh.shape["tensor"])
    token_spec = P(("dp", "tensor"), None)
    in_specs = (
        token_spec,
        P(("dp", "tensor")),
        P(),
        P(),
        P(),
        P(None, None, None, "tensor"),
        P(None, "tensor", None),
        P(None, None, "tensor"),
        P(None, "tensor", None),
        P(),
        token_spec,
    )
    out_specs = (
        token_spec,
        token_spec,
        P(),
        P(),
        P(None, None, None, "tensor"),
        P(None, "tensor", None),
        P(None, None, "tensor"),
        P(None, "tensor", None),
        P(),
        P(),
    )
    return jax.shard_map(
        make_local(links), mesh=mesh, in_specs=in_specs, out_specs=out_specs, check_vma=False
    )
```

```python
import functools
import math

import jax
import jax.numpy as jnp
import numpy as np
from jax import lax
from jax.experimental import pallas as pl
from jax.experimental.pallas import tpu as pltpu
from jax.sharding import PartitionSpec as P

HD = 64
bf16 = jnp.bfloat16
f32 = jnp.float32
epsilon = 1e-05


def mm(a, b):
    return jnp.dot(a, b, preferred_element_type=f32)


def mm_t(a, b):
    return lax.dot_general(a, b, (((1,), (1,)), ((), ())), preferred_element_type=f32)


def across(a, b):
    return lax.dot_general(a, b, (((0,), (0,)), ((), ())), preferred_element_type=f32)


def ein(spec, a, b):
    return jnp.einsum(spec, a, b, preferred_element_type=f32)


def gelu_parts(u):
    square = u * u
    s = 0.5 + 0.5 * jnp.tanh(u * (0.7978845608 + 0.7978845608 * 0.044715 * square))
    value = u * s
    slope = s + value * (1.0 - s) * (2.0 * 0.7978845608 + 6.0 * 0.7978845608 * 0.044715 * square)
    return value, slope


def standardize(v):
    centered = v - jnp.mean(v, axis=-1, keepdims=True)
    inverse = lax.rsqrt(jnp.mean(centered * centered, axis=-1, keepdims=True) + epsilon)
    return centered * inverse, inverse


def norm_backward(grad, xhat, inverse, gain):
    e = grad * gain
    return inverse * (
        e
        - jnp.mean(e, axis=-1, keepdims=True)
        - xhat * jnp.mean(e * xhat, axis=-1, keepdims=True)
    )


CHUNK = 32
BLOCK = 256


def rope_tables(length, width):
    half = HD // 2
    freqs = np.exp(-math.log(10000.0) * np.arange(half) * 2.0 / HD)
    angles = np.arange(length)[:, None] * freqs[None, :]
    heads = width // HD
    cos = np.tile(np.cos(angles), (1, 2 * heads))
    sin = np.tile(np.concatenate([-np.sin(angles), np.sin(angles)], axis=1), (1, heads))
    return jnp.asarray(cos, f32), jnp.asarray(sin, f32)


def partner(u):
    width = u.shape[1]
    lane = lax.broadcasted_iota(jnp.int32, u.shape, 1)
    low = (lane & (HD - 1)) < HD // 2
    return jnp.where(low, pltpu.roll(u, width - HD // 2, 1), pltpu.roll(u, HD // 2, 1))


GAIN, BIAS, TIME = 0, 1, 2


def vector(ref, group, row):
    at = group * (ref.shape[0] // 3) + row
    return ref[at : at + 1, :]


def chunks(rows, body, start=0):
    def step(i, carry):
        body(pl.multiple_of(i * CHUNK, CHUNK))
        return carry

    lax.fori_loop(start // CHUNK, rows // CHUNK, step, 0, unroll=4)


def rows_at(at):
    return pl.ds(at, CHUNK)


def other_rows(at, rows, swapped):
    if not swapped:
        return rows_at(at)
    half = rows // 2
    return rows_at(pl.multiple_of(jnp.where(at < half, at + half, at - half), CHUNK))


def fold(v):
    return jnp.sum(v.reshape(-1, 8, v.shape[-1]), axis=0)


LIMIT = 17 * 2**20
SMALL = 12 * 2**20


def call(kernel, ins, outs, scratch, flops, name, aliases={}, after=(), limit=LIMIT):
    count, late = len(ins), len(after)
    specs, args = [], []
    for a, away in ins:
        space = pltpu.SMEM if a.dtype == jnp.int32 else pltpu.HBM if away else pltpu.VMEM
        specs.append(pl.BlockSpec(memory_space=space))
        args.append(a if space == pltpu.SMEM else pltpu.with_memory_space_constraint(a, space))

    def run(*refs):
        kernel(*refs[:count], *refs[count + late :])

    return pl.pallas_call(
        run,
        out_shape=[(pltpu.HBM if away else pltpu.VMEM)(s, d) for s, d, away in outs],
        in_specs=specs + [pl.BlockSpec(memory_space=pl.ANY)] * late,
        out_specs=[pl.BlockSpec(memory_space=pltpu.HBM if away else pltpu.VMEM) for _, _, away in outs],
        scratch_shapes=scratch,
        input_output_aliases=aliases,
        compiler_params=pltpu.CompilerParams(vmem_limit_bytes=limit),
        cost_estimate=pl.CostEstimate(flops=20 * flops, bytes_accessed=2**20, transcendentals=0),
        name=name,
    )(*args, *after)


class Saver:
    def __init__(self, sems):
        self.sems, self.copies = sems, []

    def save(self, held, out):
        c = pltpu.make_async_copy(held, out, self.sems.at[len(self.copies)])
        c.start()
        self.copies.append(c)

    def wait(self):
        for c in self.copies:
            c.wait()


def masks():
    lane = lax.broadcasted_iota(jnp.int32, (1, 2 * HD), 1)
    return lane < HD


def both_heads(v, low):
    zero = jnp.zeros_like(v)
    return jnp.concatenate([jnp.where(low, v, zero), jnp.where(low, zero, v)], axis=0)


def halves(v):
    n = v.shape[1] // 2
    return v[:, :n], v[:, n:]


def softmax(scores):
    out = []
    for s in halves(scores):
        e = jnp.exp(s - jnp.max(s, axis=-1, keepdims=True))
        out.append(e * (1.0 / jnp.sum(e, axis=-1, keepdims=True)))
    return out


def beside(a, b):
    return jnp.concatenate([a, b], axis=1)


def forward_attention(layer, part_index, length, swapped, head, tau, vectors, w_qkv, w_out, tables, after):
    first = layer == 0
    rows = sum(n for _, _, n in head) if first else head[0].shape[0]
    width = w_out.shape[2]
    local = w_out.shape[1]
    block = min(BLOCK, local)
    scale = HD ** (-0.5)
    seqs = rows // length

    def kernel(*refs):
        it = iter(refs)
        take = lambda n: [next(it) for _ in range(n)]
        head_refs = take(len(head))
        tau_ref = None if first else take(1)[0]
        vec_ref, wq_any, wo_any, cos_any, sin_any = take(5)
        x_ref, part_ref = take(2)
        outs = take(6 if first else 7)
        wq, wo, cos_ref, sin_ref, sems, out_sems = take(6)
        n_ref, q_ref, k_ref, v_ref, att_ref = take(5)
        if first:
            held, = take(1)
        else:
            x2_ref, = take(1)
        saver = Saver(out_sems)
        if first:
            own = head_refs[0].at[pl.ds(head[0][1], head[0][2]), :]
            fetch = pltpu.make_async_copy(own, held, sems.at[4])
            fetch.start()
        ropes = [pltpu.make_async_copy(a, b, sems.at[5 + j]) for j, (a, b) in
                 enumerate(((cos_any, cos_ref), (sin_any, sin_ref)))]
        copies = [pltpu.make_async_copy(wq_any.at[layer, j], wq.at[j], sems.at[j]) for j in range(3)]
        copies.append(pltpu.make_async_copy(wo_any.at[layer], wo, sems.at[3]))
        for c in copies[:1] + ropes + copies[1:]:
            c.start()
        gain, bias = vector(vec_ref, GAIN, 2 * layer), vector(vec_ref, BIAS, 2 * layer)

        def norm(at, x):
            x_ref[rows_at(at), :] = x
            xhat, _ = standardize(x)
            n_ref[rows_at(at), :] = (xhat * gain + bias).astype(bf16)

        if first:
            count = head[0][2]
            if len(head) > 1:
                ref = head_refs[1]
                chunks(rows, lambda at: norm(at, ref[rows_at(at - count), :].astype(f32)), count)
            fetch.wait()
            chunks(count, lambda at: norm(at, held[rows_at(at), :].astype(f32)))
        else:
            x1, own, got = head_refs

            def scaled(at):
                here = rows_at(at)
                there = other_rows(at, rows, swapped)
                x2 = x1[here, :] + own[here, :].astype(f32) + got[there, :].astype(f32)
                x2_ref[here, :] = x2
                t = tau_ref[pl.ds(at // length * (tau.shape[0] // seqs) + part_index, 1), :]
                norm(at, x2 * (1.0 + t * vector(vec_ref, TIME, layer - 1)))

            chunks(rows, scaled)
            saver.save(x2_ref, outs[6])
        saver.save(x_ref, outs[0])
        saver.save(n_ref, outs[1])
        for c in ropes:
            c.wait()
        for j, out in enumerate((q_ref, k_ref, v_ref)):
            copies[j].wait()
            for b in range(0, local, block):
                u = mm(n_ref[...], wq[j, :, b : b + block])
                if j < 2:
                    for s in range(0, rows, length):
                        us = u[s : s + length]
                        us = us * cos_ref[:, b : b + block] + partner(us) * sin_ref[:, b : b + block]
                        out[s : s + length, b : b + block] = us.astype(bf16)
                else:
                    out[:, b : b + block] = u.astype(bf16)
            saver.save(out, outs[2 + j])
        low = masks()
        for s in range(0, rows, length):
            for b in range(0, local, 2 * HD):
                here = (slice(s, s + length), slice(b, b + 2 * HD))
                keys = both_heads(k_ref[here], low)
                probs = beside(*softmax(mm_t(q_ref[here], keys) * scale)).astype(bf16)
                att_ref[here] = mm(probs, both_heads(v_ref[here], low)).astype(bf16)
        saver.save(att_ref, outs[5])
        copies[3].wait()
        for b in range(0, width, BLOCK):
            part_ref[:, b : b + BLOCK] = mm(att_ref[...], wo[:, b : b + BLOCK]).astype(bf16)
        saver.wait()

    ins = [(a[0], j == 0) for j, a in enumerate(head)] if first else [(a, False) for a in head]
    ins += [] if first else [(tau, False)]
    ins += [(vectors, False), (w_qkv, True), (w_out, True)] + [(t, True) for t in tables]
    near = lambda n, d: ((rows, n), d, False)
    far = lambda n, d: ((rows, n), d, True)
    outs = [near(width, f32), near(width, bf16)]
    outs += [far(width, f32), far(width, bf16)] + [far(local, bf16)] * 4
    outs += [] if first else [far(width, f32)]
    scratch = [
        pltpu.VMEM((3, width, local), bf16),
        pltpu.VMEM((local, width), bf16),
        pltpu.VMEM((length, local), f32),
        pltpu.VMEM((length, local), f32),
        pltpu.SemaphoreType.DMA((7,)),
        pltpu.SemaphoreType.DMA((7,)),
        pltpu.VMEM((rows, width), bf16),
    ]
    scratch += [pltpu.VMEM((rows, local), bf16)] * 4
    scratch.append(pltpu.VMEM((head[0][2], width), bf16) if first else pltpu.VMEM((rows, width), f32))
    return call(kernel, ins, outs, scratch, 4 * 10**9, "forward_attention", after=after)


def forward_mlp(layer, swapped, x, own, got, vectors, w_up, w_down, after):
    rows, width = x.shape
    hidden = w_up.shape[2]
    tiles = hidden // BLOCK

    def kernel(x_ref, own_ref, got_ref, vec_ref, wu_any, wd_any, x1_ref, *refs):
        part_ref, x1_out, n_out, h_out, slope_out, n_ref, h_ref, slope_ref, wu, wd, sems, out_sems = refs
        saver = Saver(out_sems)
        gain, bias = vector(vec_ref, GAIN, 2 * layer + 1), vector(vec_ref, BIAS, 2 * layer + 1)
        ups = [
            pltpu.make_async_copy(
                wu_any.at[layer, :, pl.ds(t * BLOCK, BLOCK)], wu.at[t], sems.at[t]
            )
            for t in range(tiles)
        ]
        down = pltpu.make_async_copy(wd_any.at[layer], wd, sems.at[tiles])
        for c in ups:
            c.start()
        down.start()

        def norm(at):
            here = rows_at(at)
            there = other_rows(at, rows, swapped)
            x1 = x_ref[here, :] + own_ref[here, :].astype(f32) + got_ref[there, :].astype(f32)
            x1_ref[here, :] = x1
            xhat, _ = standardize(x1)
            n_ref[here, :] = (xhat * gain + bias).astype(bf16)

        chunks(rows, norm)
        saver.save(x1_ref, x1_out)
        saver.save(n_ref, n_out)
        for t in range(tiles):
            ups[t].wait()
            value, slope = gelu_parts(mm(n_ref[...], wu[t]))
            h_ref[:, t * BLOCK : (t + 1) * BLOCK] = value.astype(bf16)
            slope_ref[:, t * BLOCK : (t + 1) * BLOCK] = slope.astype(bf16)
        saver.save(h_ref, h_out)
        saver.save(slope_ref, slope_out)
        down.wait()
        for b in range(0, width, BLOCK):
            part_ref[:, b : b + BLOCK] = mm(h_ref[...], wd[:, b : b + BLOCK]).astype(bf16)
        saver.wait()

    ins = [(a, False) for a in (x, own, got, vectors)] + [(w_up, True), (w_down, True)]
    near = lambda n, d: ((rows, n), d, False)
    far = lambda n, d: ((rows, n), d, True)
    outs = [near(width, f32), near(width, bf16)]
    outs += [far(width, f32), far(width, bf16), far(hidden, bf16), far(hidden, bf16)]
    scratch = [
        pltpu.VMEM((rows, width), bf16),
        pltpu.VMEM((rows, hidden), bf16),
        pltpu.VMEM((rows, hidden), bf16),
        pltpu.VMEM((tiles, width, BLOCK), bf16),
        pltpu.VMEM((hidden, width), bf16),
        pltpu.SemaphoreType.DMA((tiles + 1,)),
        pltpu.SemaphoreType.DMA((4,)),
    ]
    return call(kernel, ins, outs, scratch, 6 * 10**9, "forward_mlp", after=after)


def last_layer(layer, length, swapped, own_rows, tau, vectors, rows_of, after):
    rows, width = rows_of[0][0].shape
    parts = len(rows_of)
    pieces = rows_of[0][3]

    def kernel(tau_ref, vec_ref, *refs):
        result_out, sums_ref, result_ref, sem = refs[-4:]
        sums_ref[...] = jnp.zeros_like(sums_ref)
        for m in range(parts):
            n = 3 + len(pieces)
            x1_ref, own_ref, got_ref, *cot_refs = refs[n * m : n * m + n]
            low = 0
            for ref, (_, start, count) in zip(cot_refs, rows_of[m][3]):

                def body(at, ref=ref, shift=start - low, mine=low < own_rows):
                    here = rows_at(at)
                    x2 = x1_ref[here, :] + own_ref[here, :].astype(f32)
                    x2 = x2 + got_ref[other_rows(at, rows, swapped), :].astype(f32)
                    t = tau_ref[pl.ds(at // length * parts + m, 1), :]
                    g = ref[rows_at(pl.multiple_of(at + shift, CHUNK)), :].astype(f32)
                    sums_ref[...] += fold(g * x2) * t
                    if mine:
                        result_ref[rows_at(pl.multiple_of(at + m * own_rows, CHUNK)), :] = x2 * (
                            1.0 + t * vector(vec_ref, TIME, layer)
                        )

                chunks(low + count, body, low)
                low += count
        c = pltpu.make_async_copy(result_ref, result_out, sem)
        c.start()
        c.wait()

    ins = [(tau, False), (vectors, False)]
    for x1, mine, got, cot in rows_of:
        ins += [(v, False) for v in (x1, mine, got)] + [(v, False) for v, _, _ in cot]
    shape = (own_rows * parts, width)
    outs = [(shape, f32, True), ((8, width), f32, False)]
    scratch = [pltpu.VMEM(shape, f32), pltpu.SemaphoreType.DMA]
    return call(kernel, ins, outs, scratch, 10**8, "last_layer", after=after, limit=SMALL)


def backward_mlp(layer, last, part_index, length, swapped, head, x2, tau, vectors, slope, w_up, w_down, after):
    rows = slope.shape[0]
    width = vectors.shape[1]
    hidden = w_up.shape[2]
    tiles = hidden // BLOCK
    seqs = rows // length
    parts = tau.shape[0] // seqs

    def kernel(*refs):
        it = iter(refs)
        take = lambda n: [next(it) for _ in range(n)]
        head_refs = take(len(head))
        x2_ref = None if last else take(1)[0]
        tau_ref, vec_ref, slope_ref, wu_any, wd_any = take(5)
        g2_ref, gm_ref, du_ref, part_ref, sums_ref = take(5)
        wu, wd, sems = take(3)
        downs = [
            pltpu.make_async_copy(
                wd_any.at[layer, pl.ds(t * BLOCK, BLOCK), :], wd.at[t], sems.at[t]
            )
            for t in range(tiles)
        ]
        up = pltpu.make_async_copy(wu_any.at[layer], wu, sems.at[tiles])
        for c in downs:
            c.start()
        up.start()
        sums_ref[...] = jnp.zeros_like(sums_ref)

        def begin(at, g):
            here = rows_at(at)
            t = tau_ref[pl.ds(at // length * parts + part_index, 1), :]
            if not last:
                sums_ref[16:24, :] += fold(g * x2_ref[here, :]) * t
            g2 = g * (1.0 + t * vector(vec_ref, TIME, layer))
            g2_ref[here, :] = g2
            gm_ref[here, :] = g2.astype(bf16)

        if last:
            low = 0
            for ref, (_, start, count) in zip(head_refs, head):
                chunks(
                    low + count,
                    lambda at, ref=ref, shift=start - low: begin(
                        at, ref[rows_at(pl.multiple_of(at + shift, CHUNK)), :].astype(f32)
                    ),
                    low,
                )
                low += count
        else:
            g1, x, own, got = head_refs

            def through_norm(at):
                here = rows_at(at)
                dn = own[here, :].astype(f32) + got[other_rows(at, rows, swapped), :].astype(f32)
                xhat, inverse = standardize(x[here, :])
                sums_ref[0:8, :] += fold(dn * xhat)
                sums_ref[8:16, :] += fold(dn)
                begin(at, g1[here, :] + norm_backward(dn, xhat, inverse, vector(vec_ref, GAIN, 2 * layer + 2)))

            chunks(rows, through_norm)
        for t in range(tiles):
            downs[t].wait()
            at = slice(t * BLOCK, (t + 1) * BLOCK)
            dh = mm_t(gm_ref[...], wd[t])
            du_ref[:, at] = (dh * slope_ref[:, at].astype(f32)).astype(bf16)
        up.wait()
        for b in range(0, width, BLOCK):
            part_ref[:, b : b + BLOCK] = mm_t(du_ref[...], wu[b : b + BLOCK, :]).astype(bf16)

    ins = [(a[0] if last else a, False) for a in head]
    ins += [] if last else [(x2, False)]
    ins += [(a, False) for a in (tau, vectors, slope)]
    ins += [(w_up, True), (w_down, True)]
    near = lambda n, d: ((rows, n), d, False)
    outs = [near(width, f32), near(width, bf16), near(hidden, bf16), near(width, bf16)]
    outs += [((24, width), f32, False)]
    scratch = [
        pltpu.VMEM((width, hidden), bf16),
        pltpu.VMEM((tiles, BLOCK, width), bf16),
        pltpu.SemaphoreType.DMA((tiles + 1,)),
    ]
    return call(kernel, ins, outs, scratch, 6 * 10**9, "backward_mlp", after=after)


def input_gradient(layer, swapped, own_rows, vectors, rows_of, after):
    rows, width = rows_of[0][1].shape

    def kernel(vec_ref, *refs):
        out_far, sums_ref, out_ref, sem = refs[-4:]
        sums_ref[...] = jnp.zeros_like(sums_ref)
        for m in range(len(rows_of)):
            g1_ref, x_ref, own_ref, got_ref = refs[4 * m : 4 * m + 4]

            def body(at, mine):
                here = rows_at(at)
                dn = own_ref[here, :].astype(f32) + got_ref[other_rows(at, rows, swapped), :].astype(f32)
                xhat, inverse = standardize(x_ref[here, :])
                sums_ref[0:8, :] += fold(dn * xhat)
                sums_ref[8:16, :] += fold(dn)
                if mine:
                    out_ref[rows_at(pl.multiple_of(at + m * own_rows, CHUNK)), :] = g1_ref[here, :] + norm_backward(
                        dn, xhat, inverse, vector(vec_ref, GAIN, 2 * layer)
                    )

            chunks(own_rows, lambda at: body(at, True))
            chunks(rows, lambda at: body(at, False), own_rows)
        c = pltpu.make_async_copy(out_ref, out_far, sem)
        c.start()
        c.wait()

    ins = [(vectors, False)] + [(v, False) for part in rows_of for v in part]
    shape = (own_rows * len(rows_of), width)
    outs = [(shape, f32, True), ((16, width), f32, False)]
    scratch = [pltpu.VMEM(shape, f32), pltpu.SemaphoreType.DMA]
    return call(kernel, ins, outs, scratch, 10**8, "input_gradient", after=after, limit=SMALL)


def totals(sums, layers, width, core, place, after):
    half_width = width // 2
    shape = (8, 16, half_width)

    def kernel(s_ref, *refs):
        send_ref, keep_ref, all_ref = refs[-3:]
        all_ref[...] = jnp.zeros_like(all_ref)
        for ref, (layer, rows, _) in zip(refs, sums):
            for j, row in enumerate(rows):
                if row is not None:
                    all_ref[layer, row : row + 1, :] += jnp.sum(ref[8 * j : 8 * j + 8, :], axis=0, keepdims=True)
        rows = lax.broadcasted_iota(jnp.int32, (16, half_width), 0)
        for target, half, p in (
            (send_ref, 1 - s_ref[0], lax.rem(8 - s_ref[1], 8)),
            (keep_ref, s_ref[0], s_ref[1]),
        ):
            for b in range(8):
                v = all_ref[half, b : b + 1, :]
                block = jnp.where(rows == 0, v[:, :half_width], jnp.where(rows == 1, v[:, half_width:], 0.0))
                target[lax.rem(p - b + 8, 8)] = block.astype(bf16)

    ins = [(jnp.stack([core, place]).astype(jnp.int32), False)] + [(v, False) for _, _, v in sums]
    outs = [(shape, bf16, False)] * 2
    scratch = [pltpu.VMEM((2, 8, width), f32)]
    return call(kernel, ins, outs, scratch, 10**8, "totals", after=after, limit=SMALL)


def backward_attention(layer, length, swapped, g2, x1, own, got, vectors, q, k, v, w_qkv, w_out, tables, after):
    rows, width = x1.shape
    local = w_out.shape[1]
    block = min(BLOCK, local)
    scale = HD ** (-0.5)

    def kernel(g2_ref, x1_ref, own_ref, got_ref, vec_ref, q_ref, k_ref, v_ref, wq_any, wo_any, cos_any, sin_any,
               g1_ref, ga_ref, dq_ref, dk_ref, dv_ref, part_ref, sums_ref, wq, wo, do_ref, cos_ref, sin_ref, sems):
        copies = [pltpu.make_async_copy(wo_any.at[layer], wo, sems.at[3])]
        copies += [pltpu.make_async_copy(cos_any, cos_ref, sems.at[4])]
        copies += [pltpu.make_async_copy(sin_any, sin_ref, sems.at[5])]
        copies += [pltpu.make_async_copy(wq_any.at[layer, j], wq.at[j], sems.at[j]) for j in range(3)]
        for c in copies:
            c.start()
        sums_ref[...] = jnp.zeros_like(sums_ref)

        def begin(at):
            here = rows_at(at)
            dn = own_ref[here, :].astype(f32) + got_ref[other_rows(at, rows, swapped), :].astype(f32)
            xhat, inverse = standardize(x1_ref[here, :])
            sums_ref[0:8, :] += fold(dn * xhat)
            sums_ref[8:16, :] += fold(dn)
            g1 = g2_ref[here, :] + norm_backward(dn, xhat, inverse, vector(vec_ref, GAIN, 2 * layer + 1))
            g1_ref[here, :] = g1
            ga_ref[here, :] = g1.astype(bf16)

        chunks(rows, begin)
        for c in copies[:3]:
            c.wait()
        for b in range(0, local, block):
            do_ref[:, b : b + block] = mm_t(ga_ref[...], wo[b : b + block, :]).astype(bf16)
        low = masks()
        for s in range(0, rows, length):
            for b in range(0, local, 2 * HD):
                here = (slice(s, s + length), slice(b, b + 2 * HD))
                lanes = slice(b, b + 2 * HD)
                keys = both_heads(k_ref[here], low)
                grad = do_ref[here]
                probs = softmax(mm_t(q_ref[here], keys) * scale)
                dps = halves(mm_t(grad, both_heads(v_ref[here], low)))
                ds = [p * (d - jnp.sum(p * d, axis=-1, keepdims=True)) for p, d in zip(probs, dps)]
                across_heads = lambda v, w: mm(beside(v[0].T, v[1].T).astype(bf16), both_heads(w, low))
                dv_ref[here] = across_heads(probs, grad).astype(bf16)
                dq = mm(beside(*ds).astype(bf16), keys) * scale
                dk = across_heads(ds, q_ref[here]) * scale
                for d, out in ((dq, dq_ref), (dk, dk_ref)):
                    out[here] = (d * cos_ref[:, lanes] + partner(d * sin_ref[:, lanes])).astype(bf16)
        for c in copies[3:]:
            c.wait()
        for b in range(0, width, BLOCK):
            at = slice(b, b + BLOCK)
            part = mm_t(dq_ref[...], wq[0, at, :]) + mm_t(dk_ref[...], wq[1, at, :])
            part_ref[:, at] = (part + mm_t(dv_ref[...], wq[2, at, :])).astype(bf16)

    ins = [(a, False) for a in (g2, x1, own, got, vectors, q, k, v)] + [(w_qkv, True), (w_out, True)]
    ins += [(t, True) for t in tables]
    near = lambda n, d: ((rows, n), d, False)
    outs = [near(width, f32), near(width, bf16)] + [near(local, bf16)] * 3
    outs += [near(width, bf16), ((16, width), f32, False)]
    scratch = [
        pltpu.VMEM((3, width, local), bf16),
        pltpu.VMEM((local, width), bf16),
        pltpu.VMEM((rows, local), bf16),
        pltpu.VMEM((length, local), f32),
        pltpu.VMEM((length, local), f32),
        pltpu.SemaphoreType.DMA((6,)),
    ]
    return call(kernel, ins, outs, scratch, 7 * 10**9, "backward_attention", after=after)


class Links:
    def __init__(self, dp, tensor):
        self.dp, self.tensor = dp, tensor
        self.chips = dp // 2
        self.ring = dp == 16
        self.walk = [0, 2, 4, 6, 7, 5, 3, 1]
        self.ring_pairs = []
        for k in range(8):
            here, there = self.walk[k], self.walk[(k + 1) % 8]
            self.ring_pairs.append((2 * here, 2 * there))
            self.ring_pairs.append((2 * there + 1, 2 * here + 1))
        self.core_pairs = [(i, i ^ 1) for i in range(dp)]

    def ring_place(self):
        i = lax.axis_index("dp")
        z, x = i >> 2, (i >> 1) & 1
        p = jnp.where(x == 0, z, 7 - z)
        return jnp.where(i & 1 == 0, p, (8 - p) & 7)

    def swap_tensor(self, v):
        return lax.ppermute(v, "tensor", [(0, 1), (1, 0)])

    def gather_tensor(self, v):
        if self.tensor != 2:
            return lax.all_gather(v, "tensor", axis=0, tiled=True)
        other = self.swap_tensor(v)
        first = lax.axis_index("tensor") == 0
        return jnp.concatenate([jnp.where(first, v, other), jnp.where(first, other, v)])

    def start_sum(self, part):
        part = part.astype(bf16)
        if self.tensor != 2:
            summed = lax.psum(part, "tensor")
            return (summed, jnp.zeros_like(summed))
        return (part, self.swap_tensor(part))

def total(parts):
    out = parts[0].astype(f32)
    for p in parts[1:]:
        out = out + p.astype(f32)
    return out


def over_rows(lefts, rights):
    return across(jnp.concatenate(lefts), jnp.concatenate(rights))


def mlp_gradients(h, gm, n2, du, core, place, after):
    n = len(h)
    hidden, width = h[0].shape[1], gm[0].shape[1]
    half_hidden = hidden // 2
    tall = half_hidden // 8
    wide = width // 8

    def kernel(s_ref, *refs):
        hs, gms, ns, dus = [refs[n * j : n * j + n] for j in range(4)]
        send_out, keep_ref, send_ref, sems = refs[4 * n :]

        def make(target, half, p, ended):
            gm_all = jnp.concatenate([r[...] for r in gms])
            columns = slice(half * half_hidden, (half + 1) * half_hidden)
            du_all = jnp.concatenate([r[:, columns] for r in dus])
            for j in range(4):
                first = half * half_hidden + j * 2 * tall
                down = across(jnp.concatenate([r[:, first : first + 2 * tall] for r in hs]), gm_all)
                up = across(jnp.concatenate([r[:, j * 2 * wide : (j + 1) * 2 * wide] for r in ns]), du_all)
                for i in range(2):
                    slot = lax.rem(p - (2 * j + i) + 8, 8)
                    target[slot, 0:tall, :] = down[i * tall : (i + 1) * tall].astype(bf16)
                    target[slot, tall : tall + wide, :] = up[i * wide : (i + 1) * wide].astype(bf16)
                    ended(slot, 2 * j + i)

        def away(slot, i):
            pltpu.make_async_copy(send_ref.at[slot], send_out.at[slot], sems.at[i]).start()

        for c in range(2):

            @pl.when(s_ref[0] == c)
            def _():
                make(send_ref, 1 - c, lax.rem(8 - s_ref[1], 8), away)
                make(keep_ref, c, s_ref[1], lambda slot, i: None)

        for i in range(8):
            slot = lax.rem(lax.rem(8 - s_ref[1], 8) - i + 8, 8)
            pltpu.make_async_copy(send_ref.at[slot], send_out.at[slot], sems.at[i]).wait()

    ins = [(jnp.stack([core, place]).astype(jnp.int32), False)]
    ins += [(v, False) for group in (h, gm, n2, du) for v in group]
    shape = (8, tall + wide, width)
    scratch = [pltpu.VMEM(shape, bf16), pltpu.SemaphoreType.DMA((8,))]
    outs = [(shape, bf16, True), (shape, bf16, False)]
    return call(kernel, ins, outs, scratch, 9 * 10**9, "mlp_gradients", after=after, limit=SMALL)


def attention_gradients(att, ga, n1, dq, dk, dv, core, place, after):
    n = len(att)
    local, width = att[0].shape[1], ga[0].shape[1]
    heads, wide = local // 2, width // 2

    def kernel(s_ref, *refs):
        atts, gas, ns = [refs[n * j : n * j + n] for j in range(3)]
        dps = [refs[n * j : n * j + n] for j in range(3, 6)]

        def make(target, half, p):
            def put(value, low, size):
                for b in range(8):
                    slot = lax.rem(p - b + 8, 8)
                    target[slot, low : low + size, :] = value[b * size : (b + 1) * size].astype(bf16)

            lefts = [r[:, half * heads : (half + 1) * heads] for r in atts]
            for j in range(2):
                put(over_rows(lefts, [r[:, j * wide : (j + 1) * wide] for r in gas]), heads // 8 * j, heads // 8)
            lefts = [r[:, half * wide : (half + 1) * wide] for r in ns]
            for j in range(3):
                put(over_rows(lefts, [r[...] for r in dps[j]]), heads // 4 + wide // 8 * j, wide // 8)

        for c in range(2):

            @pl.when(s_ref[0] == c)
            def _():
                make(refs[6 * n], 1 - c, lax.rem(8 - s_ref[1], 8))
                make(refs[6 * n + 1], c, s_ref[1])

    ins = [(jnp.stack([core, place]).astype(jnp.int32), False)]
    ins += [(v, False) for group in (att, ga, n1, dq, dk, dv) for v in group]
    out = ((8, heads // 4 + 3 * wide // 8, local), bf16, False)
    return call(kernel, ins, [out, out], [], 5 * 10**9, "attention_gradients", after=after, limit=SMALL)


def pack(lanes, after):
    depths = [lane[0].shape[0] for lane in lanes]
    count, width = len(lanes[0]), lanes[0][0].shape[1]

    def kernel(*refs):
        low = 0
        for j, depth in enumerate(depths):
            for i in range(count):
                refs[-1][i, low : low + depth, :] = refs[j * count + i][...]
            low += depth

    out = ((count, sum(depths), width), bf16, False)
    ins = [(v, False) for lane in lanes for v in lane]
    return call(kernel, ins, [out], [], 10**8, "pack", after=after, limit=SMALL)[0]


def merge(pairs, lanes, after):
    count, _, width = pairs[0][0].shape
    depths = [a.shape[1] for a, _ in pairs]
    depth = sum(depths) // lanes

    def kernel(*refs):
        ins, outs = refs[: 2 * len(pairs)], refs[2 * len(pairs) :]

        def total(i, j):
            if lanes == 1:
                return jnp.concatenate(
                    [
                        (ins[2 * n][i].astype(f32) + ins[2 * n + 1][i].astype(f32)).astype(bf16)
                        for n in range(len(pairs))
                    ]
                )
            at = slice(j * depth, (j + 1) * depth)
            return (ins[0][i, at, :].astype(f32) + ins[1][i, at, :].astype(f32)).astype(bf16)

        for j in range(lanes):
            outs[2 * j][...] = total(0, j)

        def body(i, carry):
            for j in range(lanes):
                outs[2 * j + 1][i] = total(i, j)
            return carry

        lax.fori_loop(1, count, body, 0)

    outs = [((depth, width), bf16, False), ((count, depth, width), bf16, False)] * lanes
    ins = [(v, False) for pair in pairs for v in pair]
    out = call(kernel, ins, outs, [], 10**8, "merge", after=after, limit=SMALL)
    return out[0::2], out[1::2]


def add(a, blocks, i, after):
    def kernel(a_ref, b_ref, out_ref):
        out_ref[...] = (a_ref[...].astype(f32) + b_ref[i].astype(f32)).astype(bf16)

    outs = [(a.shape, bf16, False)]
    return call(kernel, [(a, False), (blocks, False)], outs, [], 10**8, "add", after=after, limit=SMALL)[0]


def hold(a, after):
    def kernel(a_ref, out_ref):
        out_ref[...] = a_ref[...]

    return call(kernel, [(a, False)], [(a.shape, a.dtype, False)], [], 10**8, "hold", after=after, limit=SMALL)[0]


DEEP = 4


def spread(pieces, shapes, blocks, begin, own, core, place, before, after):
    count, depth, width = blocks.shape
    deep = min(DEEP, count)

    def kernel(s_ref, block_ref, *refs):
        token_ref, held, sems = refs[-3:]
        outs = refs[len(refs) - 3 - len(shapes) : -3]
        token_ref[...] = jnp.zeros_like(token_ref)

        def copies(i):
            half, p = (s_ref[0], s_ref[1]) if own else (1 - s_ref[0], lax.rem(8 - s_ref[1], 8))
            b = lax.rem(p + 1 - begin - i + 16, 8)
            return [
                pltpu.make_async_copy(
                    held.at[(i % deep,) + source], outs[o].at[place], sems.at[i % deep, j]
                )
                for j, (source, o, place) in enumerate(pieces(half, b))
            ]

        for i in range(count):
            if i >= deep:
                for c in copies(i - deep):
                    c.wait()
            held[i % deep] = block_ref[i].astype(f32)
            for c in copies(i):
                c.start()
        for i in range(count - deep, count):
            for c in copies(i):
                c.wait()

    ins = [(jnp.stack([core, place]).astype(jnp.int32), False), (blocks, False)]
    aliases = {}
    for j, v in enumerate(before):
        aliases[len(ins)] = j
        ins.append((v, True))
    scratch = [
        pltpu.VMEM((deep, depth, width), f32),
        pltpu.SemaphoreType.DMA((deep, len(pieces(0, 0)))),
    ]
    outs = [(s, f32, True) for s in shapes] + [((8, 128), f32, False)]
    *outs, token = call(kernel, ins, outs, scratch, 10**8, "spread", aliases, after=after, limit=SMALL)
    return outs, token


def mlp_pieces(layer, layers, hidden, width):
    tall, wide = hidden // 16, width // 8

    def pieces(half, b):
        rows = pl.ds(pl.multiple_of(half * (hidden // 2) + b * tall, tall), tall)
        across_rows = pl.ds(pl.multiple_of(b * wide, wide), wide)
        columns = pl.ds(pl.multiple_of(half * (hidden // 2), hidden // 2), hidden // 2)
        return [
            ((slice(0, tall), slice(None)), 0, (layer, rows, slice(None))),
            ((slice(tall, tall + wide), slice(None)), 1, (layer, across_rows, columns)),
        ]

    return pieces, [(layers, hidden, width), (layers, width, hidden)]


def attention_pieces(layer, layers, local, width):
    tall, wide = local // 16, width // 16

    def pieces(half, b):
        rows = pl.ds(pl.multiple_of(half * (local // 2) + b * tall, tall), tall)
        deep = pl.ds(pl.multiple_of(half * (width // 2) + b * wide, wide), wide)
        out = []
        for j in range(2):
            columns = slice(j * width // 2, (j + 1) * width // 2)
            out.append(((slice(tall * j, tall * (j + 1)), slice(None)), 0, (layer, rows, columns)))
        for j in range(3):
            low = 2 * tall + wide * j
            out.append(((slice(low, low + wide), slice(None)), 1, (layer, j, deep, slice(None))))
        return out

    return pieces, [(layers, local, width), (layers, 3, width, local)]


def small_outputs(ends, begins, layers, width, core, place):
    row = ends[0][0].shape[1] - 16
    half_width = width // 2

    def kernel(s_ref, *refs):
        outs, held = refs[2 * len(ends) : 2 * len(ends) + 4], refs[2 * len(ends) + 4 : -1]
        gains, biases, times, norms = held

        def put(source, half, p):
            for b in range(5):
                slot = lax.rem(p + 1 - b + 16, 8)
                for n, begin in enumerate(begins):
                    ref = refs[2 * n + source]

                    @pl.when((slot >= begin) & (slot < begin + ref.shape[0]))
                    def _():
                        for j in range(2):
                            v = ref[slot - begin, row : row + 16, :].astype(f32)[j : j + 1, :]
                            at = slice(j * half_width, (j + 1) * half_width)
                            if b == 4:
                                times[half : half + 1, at] = v
                            else:
                                (gains, biases)[b // 2][half, b % 2 : b % 2 + 1, at] = v

        for c in range(2):

            @pl.when(s_ref[0] == c)
            def _():
                put(0, c, s_ref[1])
                put(1, 1 - c, 8 - s_ref[1])

        norms[0:1, :] = gains[layers - 1, 1:2, :]
        norms[1:2, :] = biases[layers - 1, 1:2, :]
        copies = [pltpu.make_async_copy(a, b, refs[-1].at[j]) for j, (a, b) in enumerate(zip(held, outs))]
        for c in copies:
            c.start()
        for c in copies:
            c.wait()

    shapes = [(layers, 2, width), (layers, 2, width), (layers, width), (2, width)]
    ins = [(jnp.stack([core, place]).astype(jnp.int32), False)] + [(v, False) for pair in ends for v in pair]
    scratch = [pltpu.VMEM(s, f32) for s in shapes] + [pltpu.SemaphoreType.DMA((4,))]
    return call(kernel, ins, [(s, f32, True) for s in shapes], scratch, 10**8, "small_outputs", limit=SMALL)


class Stream:
    def __init__(self, links, kind, layer, layers, groups, after, written):
        self.links, self.kind, self.written = links, kind, written
        self.steps = -2
        self.extra = []
        self.cuts = [(0, 5), (5, 8)] if kind == "attention" and layer == 0 else [(0, 8)]
        self.packed = []
        self.waits = not (kind == "attention" and layer == 0)
        self.lanes = LANES[kind][min(layer, 1)]
        self.core = lax.axis_index("dp") & 1
        self.p = links.ring_place()
        if kind == "mlp":
            send, self.blocks = mlp_gradients(*groups, self.core, self.p, after)
            self.layout = mlp_pieces(layer, layers, groups[0][0].shape[1], groups[1][0].shape[1])
        else:
            send, self.blocks = attention_gradients(*groups, self.core, self.p, after)
            self.layout = attention_pieces(layer, layers, groups[0][0].shape[1], groups[1][0].shape[1])
        self.raw = lax.ppermute(send, "dp", links.core_pairs)
        self.done = [[] for _ in range(self.lanes)]
        self.token = self.blocks

    def step(self, after):
        self.steps += 1
        if self.steps < 0:
            return []
        out = []
        if self.steps == 14:
            for lane, v in zip(self.done, self.raw):
                lane.append(v)
            if self.waits:
                return []
        if self.packed and len(self.packed[-1]) == 2 and not self.packed[-1][-1][1]:
            (_, peer), state = self.packed[-1][0], self.packed[-1][-1]
            state[1] = True
            out.append(self.write(peer, state[0], False, after))
        if self.steps == 15 + self.waits:
            return out
        for low, high in self.cuts:
            if self.steps == min(high + 7, 14 + self.waits):
                mine = pack([lane[low:high] for lane in self.done], after)
                peer = lax.ppermute(mine, "dp", self.links.core_pairs)
                out.append(self.write(mine, low, True, []))
                self.packed.append(((mine, peer), [low, False]))
        if self.steps >= 14:
            return out
        if self.steps == 0:
            now, self.blocks = merge([(self.blocks, self.raw)] + self.extra, self.lanes, after)
        elif self.steps < 8:
            now = [add(r, b, self.steps, after) for r, b in zip(self.raw, self.blocks)]
        else:
            now = [hold(r, after) for r in self.raw]
        if self.steps >= 7:
            for lane, v in zip(self.done, now):
                lane.append(v)
        self.raw = [lax.ppermute(v, "dp", self.links.ring_pairs) for v in now]
        return out + list(now)

    def write(self, blocks, begin, own, after):
        before = self.written.get(self.kind, [])
        self.written[self.kind], token = spread(
            *self.layout, blocks, begin, own, self.core, self.p, before, after
        )
        return token

    def going(self):
        return self.steps < 15 + self.waits


LANES = {"mlp": (2, 1), "attention": (1, 1)}


class Plain:
    def __init__(self, links, kind, layer, layers, groups, after, written):
        left, right, deep, *dps = [jnp.concatenate(g) for g in groups]
        out = [ein("ra,rb->ab", left, right)]
        if kind == "mlp":
            out.append(ein("ra,rb->ab", deep, dps[0]))
        else:
            out.append(jnp.stack([ein("ra,rb->ab", deep, d) for d in dps]))
        out = [lax.psum(v.astype(bf16), "dp").astype(f32) for v in out]
        if kind not in written:
            written[kind] = [jnp.zeros((layers,) + v.shape, f32) for v in out]
        written[kind] = [b.at[layer].set(v) for b, v in zip(written[kind], out)]
        self.token = after[0]

    def going(self):
        return False

def make_local(links):
    def local(
        tokens,
        time_index,
        time_table,
        norm_gain,
        norm_bias,
        w_qkv,
        w_out,
        w_up,
        w_down,
        time_weight,
        cotangent,
    ):
        rows, width = tokens.shape
        seq_here = time_index.shape[0]
        length = rows // seq_here
        layers = norm_gain.shape[0]
        local_width = w_out.shape[1]
        tables = rope_tables(length, local_width)
        parts = 2 if seq_here % 2 == 0 else 1
        own = rows // parts
        paired = links.tensor == 2
        wq = jnp.transpose(w_qkv, (0, 2, 1, 3))

        def group_rows(v, m, after=()):
            if paired:
                mine = v[m * own : (m + 1) * own]
                got = links.swap_tensor(hold(mine, after) if after else mine)
                return [(v, m * own, own), (got, 0, own)]
            v = links.gather_tensor(v[m * own : (m + 1) * own])
            return [(v, 0, v.shape[0])]

        heads = [group_rows(tokens, 0)]
        heads += [group_rows(tokens, m, [heads[-1][-1][0]]) for m in range(1, parts)]
        gs = []
        vectors = [norm_gain.reshape(2 * layers, width), norm_bias.reshape(2 * layers, width)]
        vectors += [time_weight, jnp.zeros((layers, width), f32)]
        vectors = jnp.concatenate(vectors)
        if paired:
            index = jnp.concatenate([time_index, links.swap_tensor(time_index)])
        else:
            index = links.gather_tensor(time_index)
        onehot = (index[:, None] == jnp.arange(time_table.shape[0], dtype=jnp.int32)[None, :]).astype(f32)
        tau = jnp.dot(onehot, time_table, precision=lax.Precision.HIGHEST)
        latest = []
        saved = [[None] * parts for _ in range(layers)]
        after = [[None] * parts for _ in range(layers)]
        for l in range(layers):
            for m in range(parts):
                x_near, part, *out = forward_attention(
                    l, m, length, paired, heads[m], tau, vectors, wq, w_out, tables, latest
                )
                latest = [part]
                if l > 0:
                    after[l - 1][m] = out.pop()
                saved[l][m] = out
                heads[m] = (x_near, *links.start_sum(part))
            for m in range(parts):
                x1, part, *out = forward_mlp(l, paired, *heads[m], vectors, w_up, w_down, latest)
                latest = [part]
                heads[m] = (x1, part) if l == layers - 1 else (x1, *links.start_sum(part))
                saved[l][m] += out
                if l == layers - 1:
                    gs.append(group_rows(cotangent, m, [part] + [g[-1][0] for g in gs]))

        kind = Stream if links.ring else Plain
        streams = []
        small = []
        keep = lambda l, i: [s[i] for s in saved[l]]

        last, written = [], {}

        def step(also=()):
            before = list(also)
            for s in streams:
                if s.going():
                    before += s.step(list(last))
            return before

        def ran(out):
            last[:] = [out]

        gs_first = gs
        gs = list(gs)
        for l in reversed(range(layers)):
            g2s, gms, dus, sums = [None] * parts, [None] * parts, [None] * parts, [None] * parts
            gas, dps = [None] * parts, [None] * parts
            for m in range(parts):
                g2s[m], gms[m], dus[m], part, s = backward_mlp(
                    l, l == layers - 1, m, length, paired, gs[m], after[l][m], tau, vectors, saved[l][m][9],
                    w_up, w_down, step(latest),
                )
                latest = []
                ran(s)
                if l < layers - 1:
                    small.append((l + 1, (0, 2), s))
                    small.append((l, (None, None, 4), s))
                sums[m] = links.start_sum(part)

            def mlp_stream(also):
                groups = [keep(l, 8), gms, keep(l, 7), dus]
                streams.append(kind(links, "mlp", l, layers, groups, step(also), written))
                ran(streams[-1].token)

            if l > 0:
                mlp_stream([sums[0][1]])
            for m in range(parts):
                x, n1, q, k, v, att, x1 = saved[l][m][:7]
                g1, gas[m], dq, dk, dv, part, s = backward_attention(
                    l, length, paired, g2s[m], x1, *sums[m], vectors, q, k, v, wq, w_out, tables, step()
                )
                ran(s)
                small.append((l, (1, 3), s))
                dps[m] = (dq, dk, dv)
                gs[m] = (g1, x, *links.start_sum(part))
                if m == 0 and l == 0:
                    mlp_stream([sums[-1][1]])
            groups = [keep(l, 5), gas, keep(l, 1)] + [[d[j] for d in dps] for j in range(3)]
            streams.append(kind(links, "attention", l, layers, groups, step([gs[0][3]]), written))
            ran(streams[-1].token)
        final = streams[-1]
        own_here = own if paired else gs[0][1].shape[0]

        def send_last():
            for m in range(parts):
                x1, part = heads[m]
                held = hold(part, list(last)) if links.ring else part
                heads[m] = (x1, *links.start_sum(held), gs_first[m])
                heads[m] = (x1, part, heads[m][2], gs_first[m]) if paired else heads[m]

        def end_layers():
            inputs, s = input_gradient(0, paired, own_here, vectors, gs, list(last))
            small.append((0, (0, 2), s))
            result, s = last_layer(layers - 1, length, paired, own_here, tau, vectors, heads, list(last) + [s])
            small.append((layers - 1, (4,), s))
            return inputs, result

        send_last()
        if links.ring:
            last[:] = step()
            inputs, result = end_layers()
            send, kept = totals(small, layers, width, final.core, final.p, list(last))
            final.extra = [(kept, lax.ppermute(send, "dp", links.core_pairs))]
            final.steps -= 1
            while any(s.going() for s in streams):
                moving = [s for s in streams if s.steps < 13]
                ending = [s for s in streams if s.steps >= 13 and s.going()]
                now = []
                for s in moving:
                    now += s.step(list(last))
                rest = []
                for s in ending:
                    rest += s.step(now or list(last))
                last[:] = now + rest
            ends = [pair for pair, _ in final.packed]
            begins = [low for low, _ in final.cuts]
            gains, biases, times, norms = small_outputs(ends, begins, layers, width, final.core, final.p)
        else:
            inputs, result = end_layers()
            tiny = jnp.zeros((layers, 8, width), f32)
            for l, rows_of, s in small:
                for j, row in enumerate(rows_of):
                    if row is not None:
                        tiny = tiny.at[l, row].add(jnp.sum(s[8 * j : 8 * j + 8], axis=0))
            tiny = lax.psum(tiny, "dp")
            gains, biases, times = tiny[:, 0:2], tiny[:, 2:4], tiny[:, 4]
            norms = jnp.stack([gains[layers - 1, 1], biases[layers - 1, 1]])
        if not paired:
            t = lax.axis_index("tensor")
            cut = lambda v: jnp.concatenate(
                [
                    lax.dynamic_slice_in_dim(v, m * v.shape[0] // parts + t * own, own)
                    for m in range(parts)
                ]
            )
            result, inputs = cut(result), cut(inputs)
        return (
            result,
            inputs,
            gains,
            biases,
            jnp.transpose(written["attention"][1], (0, 2, 1, 3)),
            written["attention"][0],
            written["mlp"][1],
            written["mlp"][0],
            times,
            norms,
        )

    return local


def solution(mesh):
    links = Links(mesh.shape["dp"], mesh.shape["tensor"])
    token_spec = P(("dp", "tensor"), None)
    in_specs = (
        token_spec,
        P(("dp", "tensor")),
        P(),
        P(),
        P(),
        P(None, None, None, "tensor"),
        P(None, "tensor", None),
        P(None, None, "tensor"),
        P(None, "tensor", None),
        P(),
        token_spec,
    )
    out_specs = (
        token_spec,
        token_spec,
        P(),
        P(),
        P(None, None, None, "tensor"),
        P(None, "tensor", None),
        P(None, None, "tensor"),
        P(None, "tensor", None),
        P(),
        P(),
    )
    return jax.shard_map(
        make_local(links), mesh=mesh, in_specs=in_specs, out_specs=out_specs, check_vma=False
    )
```

```python
import functools
import math

import jax
import jax.numpy as jnp
import numpy as np
from jax import lax
from jax.experimental import pallas as pl
from jax.experimental.pallas import tpu as pltpu
from jax.sharding import PartitionSpec as P

HD = 64
bf16 = jnp.bfloat16
f32 = jnp.float32
epsilon = 1e-05


def mm(a, b):
    return jnp.dot(a, b, preferred_element_type=f32)


def mm_t(a, b):
    return lax.dot_general(a, b, (((1,), (1,)), ((), ())), preferred_element_type=f32)


def across(a, b):
    return lax.dot_general(a, b, (((0,), (0,)), ((), ())), preferred_element_type=f32)


def ein(spec, a, b):
    return jnp.einsum(spec, a, b, preferred_element_type=f32)


def gelu_parts(u):
    square = u * u
    s = 0.5 + 0.5 * jnp.tanh(u * (0.7978845608 + 0.7978845608 * 0.044715 * square))
    value = u * s
    slope = s + value * (1.0 - s) * (2.0 * 0.7978845608 + 6.0 * 0.7978845608 * 0.044715 * square)
    return value, slope


def standardize(v):
    centered = v - jnp.mean(v, axis=-1, keepdims=True)
    inverse = lax.rsqrt(jnp.mean(centered * centered, axis=-1, keepdims=True) + epsilon)
    return centered * inverse, inverse


def norm_backward(grad, xhat, inverse, gain):
    e = grad * gain
    return inverse * (
        e
        - jnp.mean(e, axis=-1, keepdims=True)
        - xhat * jnp.mean(e * xhat, axis=-1, keepdims=True)
    )


CHUNK = 32
BLOCK = 256


def rope_tables(length, width):
    half = HD // 2
    freqs = np.exp(-math.log(10000.0) * np.arange(half) * 2.0 / HD)
    angles = np.arange(length)[:, None] * freqs[None, :]
    heads = width // HD
    cos = np.tile(np.cos(angles), (1, 2 * heads))
    sin = np.tile(np.concatenate([-np.sin(angles), np.sin(angles)], axis=1), (1, heads))
    return jnp.asarray(cos, f32), jnp.asarray(sin, f32)


def partner(u):
    width = u.shape[1]
    lane = lax.broadcasted_iota(jnp.int32, u.shape, 1)
    low = (lane & (HD - 1)) < HD // 2
    return jnp.where(low, pltpu.roll(u, width - HD // 2, 1), pltpu.roll(u, HD // 2, 1))


GAIN, BIAS, TIME = 0, 1, 2


def vector(ref, group, row):
    at = group * (ref.shape[0] // 3) + row
    return ref[at : at + 1, :]


def chunks(rows, body, start=0):
    def step(i, carry):
        body(pl.multiple_of(i * CHUNK, CHUNK))
        return carry

    lax.fori_loop(start // CHUNK, rows // CHUNK, step, 0, unroll=4)


def rows_at(at):
    return pl.ds(at, CHUNK)


def other_rows(at, rows, swapped):
    if not swapped:
        return rows_at(at)
    half = rows // 2
    return rows_at(pl.multiple_of(jnp.where(at < half, at + half, at - half), CHUNK))


def fold(v):
    return jnp.sum(v.reshape(-1, 8, v.shape[-1]), axis=0)


LIMIT = 17 * 2**20
SMALL = 12 * 2**20


def call(kernel, ins, outs, scratch, flops, name, aliases={}, after=(), limit=LIMIT):
    count, late = len(ins), len(after)
    specs, args = [], []
    for a, away in ins:
        space = pltpu.SMEM if a.dtype == jnp.int32 else pltpu.HBM if away else pltpu.VMEM
        specs.append(pl.BlockSpec(memory_space=space))
        args.append(a if space == pltpu.SMEM else pltpu.with_memory_space_constraint(a, space))

    def run(*refs):
        kernel(*refs[:count], *refs[count + late :])

    return pl.pallas_call(
        run,
        out_shape=[(pltpu.HBM if away else pltpu.VMEM)(s, d) for s, d, away in outs],
        in_specs=specs + [pl.BlockSpec(memory_space=pl.ANY)] * late,
        out_specs=[pl.BlockSpec(memory_space=pltpu.HBM if away else pltpu.VMEM) for _, _, away in outs],
        scratch_shapes=scratch,
        input_output_aliases=aliases,
        compiler_params=pltpu.CompilerParams(vmem_limit_bytes=limit),
        cost_estimate=pl.CostEstimate(flops=20 * flops, bytes_accessed=2**20, transcendentals=0),
        name=name,
    )(*args, *after)


class Saver:
    def __init__(self, sems):
        self.sems, self.copies = sems, []

    def save(self, held, out):
        c = pltpu.make_async_copy(held, out, self.sems.at[len(self.copies)])
        c.start()
        self.copies.append(c)

    def wait(self):
        for c in self.copies:
            c.wait()


def masks():
    lane = lax.broadcasted_iota(jnp.int32, (1, 2 * HD), 1)
    return lane < HD


def both_heads(v, low):
    zero = jnp.zeros_like(v)
    return jnp.concatenate([jnp.where(low, v, zero), jnp.where(low, zero, v)], axis=0)


def halves(v):
    n = v.shape[1] // 2
    return v[:, :n], v[:, n:]


def softmax(scores):
    out = []
    for s in halves(scores):
        e = jnp.exp(s - jnp.max(s, axis=-1, keepdims=True))
        out.append(e * (1.0 / jnp.sum(e, axis=-1, keepdims=True)))
    return out


def beside(a, b):
    return jnp.concatenate([a, b], axis=1)


def forward_attention(layer, part_index, length, swapped, head, tau, vectors, w_qkv, w_out, tables, after):
    first = layer == 0
    rows = sum(n for _, _, n in head) if first else head[0].shape[0]
    width = w_out.shape[2]
    local = w_out.shape[1]
    block = min(BLOCK, local)
    scale = HD ** (-0.5)
    seqs = rows // length

    def kernel(*refs):
        it = iter(refs)
        take = lambda n: [next(it) for _ in range(n)]
        head_refs = take(len(head))
        tau_ref = None if first else take(1)[0]
        vec_ref, wq_any, wo_any, cos_any, sin_any = take(5)
        x_ref, part_ref = take(2)
        outs = take(6 if first else 7)
        wq, wo, cos_ref, sin_ref, sems, out_sems = take(6)
        n_ref, q_ref, k_ref, v_ref, att_ref = take(5)
        if first:
            held, = take(1)
        else:
            x2_ref, = take(1)
        saver = Saver(out_sems)
        if first:
            own = head_refs[0].at[pl.ds(head[0][1], head[0][2]), :]
            fetch = pltpu.make_async_copy(own, held, sems.at[4])
            fetch.start()
        ropes = [pltpu.make_async_copy(a, b, sems.at[5 + j]) for j, (a, b) in
                 enumerate(((cos_any, cos_ref), (sin_any, sin_ref)))]
        copies = [pltpu.make_async_copy(wq_any.at[layer, j], wq.at[j], sems.at[j]) for j in range(3)]
        copies.append(pltpu.make_async_copy(wo_any.at[layer], wo, sems.at[3]))
        for c in copies[:1] + ropes + copies[1:]:
            c.start()
        gain, bias = vector(vec_ref, GAIN, 2 * layer), vector(vec_ref, BIAS, 2 * layer)

        def norm(at, x):
            x_ref[rows_at(at), :] = x
            xhat, _ = standardize(x)
            n_ref[rows_at(at), :] = (xhat * gain + bias).astype(bf16)

        if first:
            count = head[0][2]
            if len(head) > 1:
                ref = head_refs[1]
                chunks(rows, lambda at: norm(at, ref[rows_at(at - count), :].astype(f32)), count)
            fetch.wait()
            chunks(count, lambda at: norm(at, held[rows_at(at), :].astype(f32)))
        else:
            x1, own, got = head_refs

            def scaled(at):
                here = rows_at(at)
                there = other_rows(at, rows, swapped)
                x2 = x1[here, :] + own[here, :].astype(f32) + got[there, :].astype(f32)
                x2_ref[here, :] = x2
                t = tau_ref[pl.ds(at // length * (tau.shape[0] // seqs) + part_index, 1), :]
                norm(at, x2 * (1.0 + t * vector(vec_ref, TIME, layer - 1)))

            chunks(rows, scaled)
            saver.save(x2_ref, outs[6])
        saver.save(x_ref, outs[0])
        saver.save(n_ref, outs[1])
        for c in ropes:
            c.wait()
        for j, out in enumerate((q_ref, k_ref, v_ref)):
            copies[j].wait()
            for b in range(0, local, block):
                u = mm(n_ref[...], wq[j, :, b : b + block])
                if j < 2:
                    for s in range(0, rows, length):
                        us = u[s : s + length]
                        us = us * cos_ref[:, b : b + block] + partner(us) * sin_ref[:, b : b + block]
                        out[s : s + length, b : b + block] = us.astype(bf16)
                else:
                    out[:, b : b + block] = u.astype(bf16)
            saver.save(out, outs[2 + j])
        low = masks()
        for s in range(0, rows, length):
            for b in range(0, local, 2 * HD):
                here = (slice(s, s + length), slice(b, b + 2 * HD))
                keys = both_heads(k_ref[here], low)
                probs = beside(*softmax(mm_t(q_ref[here], keys) * scale)).astype(bf16)
                att_ref[here] = mm(probs, both_heads(v_ref[here], low)).astype(bf16)
        saver.save(att_ref, outs[5])
        copies[3].wait()
        for b in range(0, width, BLOCK):
            part_ref[:, b : b + BLOCK] = mm(att_ref[...], wo[:, b : b + BLOCK]).astype(bf16)
        saver.wait()

    ins = [(a[0], j == 0) for j, a in enumerate(head)] if first else [(a, False) for a in head]
    ins += [] if first else [(tau, False)]
    ins += [(vectors, False), (w_qkv, True), (w_out, True)] + [(t, True) for t in tables]
    near = lambda n, d: ((rows, n), d, False)
    far = lambda n, d: ((rows, n), d, True)
    outs = [near(width, f32), near(width, bf16)]
    outs += [far(width, f32), far(width, bf16)] + [far(local, bf16)] * 4
    outs += [] if first else [far(width, f32)]
    scratch = [
        pltpu.VMEM((3, width, local), bf16),
        pltpu.VMEM((local, width), bf16),
        pltpu.VMEM((length, local), f32),
        pltpu.VMEM((length, local), f32),
        pltpu.SemaphoreType.DMA((7,)),
        pltpu.SemaphoreType.DMA((7,)),
        pltpu.VMEM((rows, width), bf16),
    ]
    scratch += [pltpu.VMEM((rows, local), bf16)] * 4
    scratch.append(pltpu.VMEM((head[0][2], width), bf16) if first else pltpu.VMEM((rows, width), f32))
    return call(kernel, ins, outs, scratch, 4 * 10**9, "forward_attention", after=after)


def forward_mlp(layer, swapped, x, own, got, vectors, w_up, w_down, after):
    rows, width = x.shape
    hidden = w_up.shape[2]
    tiles = hidden // BLOCK

    def kernel(x_ref, own_ref, got_ref, vec_ref, wu_any, wd_any, x1_ref, *refs):
        part_ref, x1_out, n_out, h_out, slope_out, n_ref, h_ref, slope_ref, wu, wd, sems, out_sems = refs
        saver = Saver(out_sems)
        gain, bias = vector(vec_ref, GAIN, 2 * layer + 1), vector(vec_ref, BIAS, 2 * layer + 1)
        ups = [
            pltpu.make_async_copy(
                wu_any.at[layer, :, pl.ds(t * BLOCK, BLOCK)], wu.at[t], sems.at[t]
            )
            for t in range(tiles)
        ]
        down = pltpu.make_async_copy(wd_any.at[layer], wd, sems.at[tiles])
        for c in ups:
            c.start()
        down.start()

        def norm(at):
            here = rows_at(at)
            there = other_rows(at, rows, swapped)
            x1 = x_ref[here, :] + own_ref[here, :].astype(f32) + got_ref[there, :].astype(f32)
            x1_ref[here, :] = x1
            xhat, _ = standardize(x1)
            n_ref[here, :] = (xhat * gain + bias).astype(bf16)

        chunks(rows, norm)
        saver.save(x1_ref, x1_out)
        saver.save(n_ref, n_out)
        for t in range(tiles):
            ups[t].wait()
            value, slope = gelu_parts(mm(n_ref[...], wu[t]))
            h_ref[:, t * BLOCK : (t + 1) * BLOCK] = value.astype(bf16)
            slope_ref[:, t * BLOCK : (t + 1) * BLOCK] = slope.astype(bf16)
        saver.save(h_ref, h_out)
        saver.save(slope_ref, slope_out)
        down.wait()
        for b in range(0, width, BLOCK):
            part_ref[:, b : b + BLOCK] = mm(h_ref[...], wd[:, b : b + BLOCK]).astype(bf16)
        saver.wait()

    ins = [(a, False) for a in (x, own, got, vectors)] + [(w_up, True), (w_down, True)]
    near = lambda n, d: ((rows, n), d, False)
    far = lambda n, d: ((rows, n), d, True)
    outs = [near(width, f32), near(width, bf16)]
    outs += [far(width, f32), far(width, bf16), far(hidden, bf16), far(hidden, bf16)]
    scratch = [
        pltpu.VMEM((rows, width), bf16),
        pltpu.VMEM((rows, hidden), bf16),
        pltpu.VMEM((rows, hidden), bf16),
        pltpu.VMEM((tiles, width, BLOCK), bf16),
        pltpu.VMEM((hidden, width), bf16),
        pltpu.SemaphoreType.DMA((tiles + 1,)),
        pltpu.SemaphoreType.DMA((4,)),
    ]
    return call(kernel, ins, outs, scratch, 6 * 10**9, "forward_mlp", after=after)


def last_layer(layer, length, swapped, own_rows, tau, vectors, rows_of, after):
    rows, width = rows_of[0][0].shape
    parts = len(rows_of)
    pieces = rows_of[0][3]

    def kernel(tau_ref, vec_ref, *refs):
        result_out, sums_ref, result_ref, sem = refs[-4:]
        sums_ref[...] = jnp.zeros_like(sums_ref)
        for m in range(parts):
            n = 3 + len(pieces)
            x1_ref, own_ref, got_ref, *cot_refs = refs[n * m : n * m + n]
            low = 0
            for ref, (_, start, count) in zip(cot_refs, rows_of[m][3]):

                def body(at, ref=ref, shift=start - low, mine=low < own_rows):
                    here = rows_at(at)
                    x2 = x1_ref[here, :] + own_ref[here, :].astype(f32)
                    x2 = x2 + got_ref[other_rows(at, rows, swapped), :].astype(f32)
                    t = tau_ref[pl.ds(at // length * parts + m, 1), :]
                    g = ref[rows_at(pl.multiple_of(at + shift, CHUNK)), :].astype(f32)
                    sums_ref[...] += fold(g * x2) * t
                    if mine:
                        result_ref[rows_at(pl.multiple_of(at + m * own_rows, CHUNK)), :] = x2 * (
                            1.0 + t * vector(vec_ref, TIME, layer)
                        )

                chunks(low + count, body, low)
                low += count
        c = pltpu.make_async_copy(result_ref, result_out, sem)
        c.start()
        c.wait()

    ins = [(tau, False), (vectors, False)]
    for x1, mine, got, cot in rows_of:
        ins += [(v, False) for v in (x1, mine, got)] + [(v, False) for v, _, _ in cot]
    shape = (own_rows * parts, width)
    outs = [(shape, f32, True), ((8, width), f32, False)]
    scratch = [pltpu.VMEM(shape, f32), pltpu.SemaphoreType.DMA]
    return call(kernel, ins, outs, scratch, 10**8, "last_layer", after=after, limit=SMALL)


def backward_mlp(layer, last, part_index, length, swapped, head, x2, tau, vectors, slope, w_up, w_down, after):
    rows = slope.shape[0]
    width = vectors.shape[1]
    hidden = w_up.shape[2]
    tiles = hidden // BLOCK
    seqs = rows // length
    parts = tau.shape[0] // seqs

    def kernel(*refs):
        it = iter(refs)
        take = lambda n: [next(it) for _ in range(n)]
        head_refs = take(len(head))
        x2_ref = None if last else take(1)[0]
        tau_ref, vec_ref, slope_ref, wu_any, wd_any = take(5)
        g2_ref, gm_ref, du_ref, part_ref, sums_ref = take(5)
        wu, wd, sems = take(3)
        downs = [
            pltpu.make_async_copy(
                wd_any.at[layer, pl.ds(t * BLOCK, BLOCK), :], wd.at[t], sems.at[t]
            )
            for t in range(tiles)
        ]
        up = pltpu.make_async_copy(wu_any.at[layer], wu, sems.at[tiles])
        for c in downs:
            c.start()
        up.start()
        sums_ref[...] = jnp.zeros_like(sums_ref)

        def begin(at, g):
            here = rows_at(at)
            t = tau_ref[pl.ds(at // length * parts + part_index, 1), :]
            if not last:
                sums_ref[16:24, :] += fold(g * x2_ref[here, :]) * t
            g2 = g * (1.0 + t * vector(vec_ref, TIME, layer))
            g2_ref[here, :] = g2
            gm_ref[here, :] = g2.astype(bf16)

        if last:
            low = 0
            for ref, (_, start, count) in zip(head_refs, head):
                chunks(
                    low + count,
                    lambda at, ref=ref, shift=start - low: begin(
                        at, ref[rows_at(pl.multiple_of(at + shift, CHUNK)), :].astype(f32)
                    ),
                    low,
                )
                low += count
        else:
            g1, x, own, got = head_refs

            def through_norm(at):
                here = rows_at(at)
                dn = own[here, :].astype(f32) + got[other_rows(at, rows, swapped), :].astype(f32)
                xhat, inverse = standardize(x[here, :])
                sums_ref[0:8, :] += fold(dn * xhat)
                sums_ref[8:16, :] += fold(dn)
                begin(at, g1[here, :] + norm_backward(dn, xhat, inverse, vector(vec_ref, GAIN, 2 * layer + 2)))

            chunks(rows, through_norm)
        for t in range(tiles):
            downs[t].wait()
            at = slice(t * BLOCK, (t + 1) * BLOCK)
            dh = mm_t(gm_ref[...], wd[t])
            du_ref[:, at] = (dh * slope_ref[:, at].astype(f32)).astype(bf16)
        up.wait()
        for b in range(0, width, BLOCK):
            part_ref[:, b : b + BLOCK] = mm_t(du_ref[...], wu[b : b + BLOCK, :]).astype(bf16)

    ins = [(a[0] if last else a, False) for a in head]
    ins += [] if last else [(x2, False)]
    ins += [(a, False) for a in (tau, vectors, slope)]
    ins += [(w_up, True), (w_down, True)]
    near = lambda n, d: ((rows, n), d, False)
    outs = [near(width, f32), near(width, bf16), near(hidden, bf16), near(width, bf16)]
    outs += [((24, width), f32, False)]
    scratch = [
        pltpu.VMEM((width, hidden), bf16),
        pltpu.VMEM((tiles, BLOCK, width), bf16),
        pltpu.SemaphoreType.DMA((tiles + 1,)),
    ]
    return call(kernel, ins, outs, scratch, 6 * 10**9, "backward_mlp", after=after)


def input_gradient(layer, swapped, own_rows, vectors, rows_of, after):
    rows, width = rows_of[0][1].shape

    def kernel(vec_ref, *refs):
        out_far, sums_ref, out_ref, sem = refs[-4:]
        sums_ref[...] = jnp.zeros_like(sums_ref)
        for m in range(len(rows_of)):
            g1_ref, x_ref, own_ref, got_ref = refs[4 * m : 4 * m + 4]

            def body(at, mine):
                here = rows_at(at)
                dn = own_ref[here, :].astype(f32) + got_ref[other_rows(at, rows, swapped), :].astype(f32)
                xhat, inverse = standardize(x_ref[here, :])
                sums_ref[0:8, :] += fold(dn * xhat)
                sums_ref[8:16, :] += fold(dn)
                if mine:
                    out_ref[rows_at(pl.multiple_of(at + m * own_rows, CHUNK)), :] = g1_ref[here, :] + norm_backward(
                        dn, xhat, inverse, vector(vec_ref, GAIN, 2 * layer)
                    )

            chunks(own_rows, lambda at: body(at, True))
            chunks(rows, lambda at: body(at, False), own_rows)
        c = pltpu.make_async_copy(out_ref, out_far, sem)
        c.start()
        c.wait()

    ins = [(vectors, False)] + [(v, False) for part in rows_of for v in part]
    shape = (own_rows * len(rows_of), width)
    outs = [(shape, f32, True), ((16, width), f32, False)]
    scratch = [pltpu.VMEM(shape, f32), pltpu.SemaphoreType.DMA]
    return call(kernel, ins, outs, scratch, 10**8, "input_gradient", after=after, limit=SMALL)


def totals(sums, layers, width, core, place, after):
    half_width = width // 2
    shape = (8, 16, half_width)

    def kernel(s_ref, *refs):
        send_ref, keep_ref, all_ref = refs[-3:]
        all_ref[...] = jnp.zeros_like(all_ref)
        for ref, (layer, rows, _) in zip(refs, sums):
            for j, row in enumerate(rows):
                if row is not None:
                    all_ref[layer, row : row + 1, :] += jnp.sum(ref[8 * j : 8 * j + 8, :], axis=0, keepdims=True)
        rows = lax.broadcasted_iota(jnp.int32, (16, half_width), 0)
        for target, half, p in (
            (send_ref, 1 - s_ref[0], lax.rem(8 - s_ref[1], 8)),
            (keep_ref, s_ref[0], s_ref[1]),
        ):
            for b in range(8):
                v = all_ref[half, b : b + 1, :]
                block = jnp.where(rows == 0, v[:, :half_width], jnp.where(rows == 1, v[:, half_width:], 0.0))
                target[lax.rem(p - b + 8, 8)] = block.astype(bf16)

    ins = [(jnp.stack([core, place]).astype(jnp.int32), False)] + [(v, False) for _, _, v in sums]
    outs = [(shape, bf16, False)] * 2
    scratch = [pltpu.VMEM((2, 8, width), f32)]
    return call(kernel, ins, outs, scratch, 10**8, "totals", after=after, limit=SMALL)


def backward_attention(layer, length, swapped, g2, x1, own, got, vectors, q, k, v, w_qkv, w_out, tables, after):
    rows, width = x1.shape
    local = w_out.shape[1]
    block = min(BLOCK, local)
    scale = HD ** (-0.5)

    def kernel(g2_ref, x1_ref, own_ref, got_ref, vec_ref, q_ref, k_ref, v_ref, wq_any, wo_any, cos_any, sin_any,
               g1_ref, ga_ref, dq_ref, dk_ref, dv_ref, part_ref, sums_ref, wq, wo, do_ref, cos_ref, sin_ref, sems):
        copies = [pltpu.make_async_copy(wo_any.at[layer], wo, sems.at[3])]
        copies += [pltpu.make_async_copy(cos_any, cos_ref, sems.at[4])]
        copies += [pltpu.make_async_copy(sin_any, sin_ref, sems.at[5])]
        copies += [pltpu.make_async_copy(wq_any.at[layer, j], wq.at[j], sems.at[j]) for j in range(3)]
        for c in copies:
            c.start()
        sums_ref[...] = jnp.zeros_like(sums_ref)

        def begin(at):
            here = rows_at(at)
            dn = own_ref[here, :].astype(f32) + got_ref[other_rows(at, rows, swapped), :].astype(f32)
            xhat, inverse = standardize(x1_ref[here, :])
            sums_ref[0:8, :] += fold(dn * xhat)
            sums_ref[8:16, :] += fold(dn)
            g1 = g2_ref[here, :] + norm_backward(dn, xhat, inverse, vector(vec_ref, GAIN, 2 * layer + 1))
            g1_ref[here, :] = g1
            ga_ref[here, :] = g1.astype(bf16)

        chunks(rows, begin)
        for c in copies[:3]:
            c.wait()
        for b in range(0, local, block):
            do_ref[:, b : b + block] = mm_t(ga_ref[...], wo[b : b + block, :]).astype(bf16)
        low = masks()
        for s in range(0, rows, length):
            for b in range(0, local, 2 * HD):
                here = (slice(s, s + length), slice(b, b + 2 * HD))
                lanes = slice(b, b + 2 * HD)
                keys = both_heads(k_ref[here], low)
                grad = do_ref[here]
                probs = softmax(mm_t(q_ref[here], keys) * scale)
                dps = halves(mm_t(grad, both_heads(v_ref[here], low)))
                ds = [p * (d - jnp.sum(p * d, axis=-1, keepdims=True)) for p, d in zip(probs, dps)]
                across_heads = lambda v, w: mm(beside(v[0].T, v[1].T).astype(bf16), both_heads(w, low))
                dv_ref[here] = across_heads(probs, grad).astype(bf16)
                dq = mm(beside(*ds).astype(bf16), keys) * scale
                dk = across_heads(ds, q_ref[here]) * scale
                for d, out in ((dq, dq_ref), (dk, dk_ref)):
                    out[here] = (d * cos_ref[:, lanes] + partner(d * sin_ref[:, lanes])).astype(bf16)
        for c in copies[3:]:
            c.wait()
        for b in range(0, width, BLOCK):
            at = slice(b, b + BLOCK)
            part = mm_t(dq_ref[...], wq[0, at, :]) + mm_t(dk_ref[...], wq[1, at, :])
            part_ref[:, at] = (part + mm_t(dv_ref[...], wq[2, at, :])).astype(bf16)

    ins = [(a, False) for a in (g2, x1, own, got, vectors, q, k, v)] + [(w_qkv, True), (w_out, True)]
    ins += [(t, True) for t in tables]
    near = lambda n, d: ((rows, n), d, False)
    outs = [near(width, f32), near(width, bf16)] + [near(local, bf16)] * 3
    outs += [near(width, bf16), ((16, width), f32, False)]
    scratch = [
        pltpu.VMEM((3, width, local), bf16),
        pltpu.VMEM((local, width), bf16),
        pltpu.VMEM((rows, local), bf16),
        pltpu.VMEM((length, local), f32),
        pltpu.VMEM((length, local), f32),
        pltpu.SemaphoreType.DMA((6,)),
    ]
    return call(kernel, ins, outs, scratch, 7 * 10**9, "backward_attention", after=after)


class Links:
    def __init__(self, dp, tensor):
        self.dp, self.tensor = dp, tensor
        self.chips = dp // 2
        self.ring = dp == 16
        self.walk = [0, 2, 4, 6, 7, 5, 3, 1]
        self.ring_pairs = []
        for k in range(8):
            here, there = self.walk[k], self.walk[(k + 1) % 8]
            self.ring_pairs.append((2 * here, 2 * there))
            self.ring_pairs.append((2 * there + 1, 2 * here + 1))
        self.core_pairs = [(i, i ^ 1) for i in range(dp)]

    def ring_place(self):
        i = lax.axis_index("dp")
        z, x = i >> 2, (i >> 1) & 1
        p = jnp.where(x == 0, z, 7 - z)
        return jnp.where(i & 1 == 0, p, (8 - p) & 7)

    def swap_tensor(self, v):
        return lax.ppermute(v, "tensor", [(0, 1), (1, 0)])

    def gather_tensor(self, v):
        if self.tensor != 2:
            return lax.all_gather(v, "tensor", axis=0, tiled=True)
        other = self.swap_tensor(v)
        first = lax.axis_index("tensor") == 0
        return jnp.concatenate([jnp.where(first, v, other), jnp.where(first, other, v)])

    def start_sum(self, part):
        part = part.astype(bf16)
        if self.tensor != 2:
            summed = lax.psum(part, "tensor")
            return (summed, jnp.zeros_like(summed))
        return (part, self.swap_tensor(part))

def total(parts):
    out = parts[0].astype(f32)
    for p in parts[1:]:
        out = out + p.astype(f32)
    return out


def over_rows(lefts, rights):
    return across(jnp.concatenate(lefts), jnp.concatenate(rights))


def mlp_gradients(h, gm, n2, du, core, place, after):
    n = len(h)
    hidden, width = h[0].shape[1], gm[0].shape[1]
    half_hidden = hidden // 2
    tall = half_hidden // 8
    wide = width // 8

    def kernel(s_ref, *refs):
        hs, gms, ns, dus = [refs[n * j : n * j + n] for j in range(4)]
        send_out, keep_ref, send_ref, sems = refs[4 * n :]

        def make(target, half, p, ended):
            gm_all = jnp.concatenate([r[...] for r in gms])
            columns = slice(half * half_hidden, (half + 1) * half_hidden)
            du_all = jnp.concatenate([r[:, columns] for r in dus])
            for j in range(4):
                first = half * half_hidden + j * 2 * tall
                down = across(jnp.concatenate([r[:, first : first + 2 * tall] for r in hs]), gm_all)
                up = across(jnp.concatenate([r[:, j * 2 * wide : (j + 1) * 2 * wide] for r in ns]), du_all)
                for i in range(2):
                    slot = lax.rem(p - (2 * j + i) + 8, 8)
                    target[slot, 0:tall, :] = down[i * tall : (i + 1) * tall].astype(bf16)
                    target[slot, tall : tall + wide, :] = up[i * wide : (i + 1) * wide].astype(bf16)
                    ended(slot, 2 * j + i)

        def away(slot, i):
            pltpu.make_async_copy(send_ref.at[slot], send_out.at[slot], sems.at[i]).start()

        for c in range(2):

            @pl.when(s_ref[0] == c)
            def _():
                make(send_ref, 1 - c, lax.rem(8 - s_ref[1], 8), away)
                make(keep_ref, c, s_ref[1], lambda slot, i: None)

        for i in range(8):
            slot = lax.rem(lax.rem(8 - s_ref[1], 8) - i + 8, 8)
            pltpu.make_async_copy(send_ref.at[slot], send_out.at[slot], sems.at[i]).wait()

    ins = [(jnp.stack([core, place]).astype(jnp.int32), False)]
    ins += [(v, False) for group in (h, gm, n2, du) for v in group]
    shape = (8, tall + wide, width)
    scratch = [pltpu.VMEM(shape, bf16), pltpu.SemaphoreType.DMA((8,))]
    outs = [(shape, bf16, True), (shape, bf16, False)]
    return call(kernel, ins, outs, scratch, 9 * 10**9, "mlp_gradients", after=after, limit=SMALL)


def attention_gradients(att, ga, n1, dq, dk, dv, core, place, after):
    n = len(att)
    local, width = att[0].shape[1], ga[0].shape[1]
    heads, wide = local // 2, width // 2

    def kernel(s_ref, *refs):
        atts, gas, ns = [refs[n * j : n * j + n] for j in range(3)]
        dps = [refs[n * j : n * j + n] for j in range(3, 6)]

        def make(target, half, p):
            def put(value, low, size):
                for b in range(8):
                    slot = lax.rem(p - b + 8, 8)
                    target[slot, low : low + size, :] = value[b * size : (b + 1) * size].astype(bf16)

            lefts = [r[:, half * heads : (half + 1) * heads] for r in atts]
            for j in range(2):
                put(over_rows(lefts, [r[:, j * wide : (j + 1) * wide] for r in gas]), heads // 8 * j, heads // 8)
            lefts = [r[:, half * wide : (half + 1) * wide] for r in ns]
            for j in range(3):
                put(over_rows(lefts, [r[...] for r in dps[j]]), heads // 4 + wide // 8 * j, wide // 8)

        for c in range(2):

            @pl.when(s_ref[0] == c)
            def _():
                make(refs[6 * n], 1 - c, lax.rem(8 - s_ref[1], 8))
                make(refs[6 * n + 1], c, s_ref[1])

    ins = [(jnp.stack([core, place]).astype(jnp.int32), False)]
    ins += [(v, False) for group in (att, ga, n1, dq, dk, dv) for v in group]
    out = ((8, heads // 4 + 3 * wide // 8, local), bf16, False)
    return call(kernel, ins, [out, out], [], 5 * 10**9, "attention_gradients", after=after, limit=SMALL)


def pack(lanes, after):
    depths = [lane[0].shape[0] for lane in lanes]
    count, width = len(lanes[0]), lanes[0][0].shape[1]

    def kernel(*refs):
        low = 0
        for j, depth in enumerate(depths):
            for i in range(count):
                refs[-1][i, low : low + depth, :] = refs[j * count + i][...]
            low += depth

    out = ((count, sum(depths), width), bf16, False)
    ins = [(v, False) for lane in lanes for v in lane]
    return call(kernel, ins, [out], [], 10**8, "pack", after=after, limit=SMALL)[0]


def merge(pairs, lanes, after):
    count, _, width = pairs[0][0].shape
    depths = [a.shape[1] for a, _ in pairs]
    depth = sum(depths) // lanes

    def kernel(*refs):
        ins, outs = refs[: 2 * len(pairs)], refs[2 * len(pairs) :]

        def total(i, j):
            if lanes == 1:
                return jnp.concatenate(
                    [
                        (ins[2 * n][i].astype(f32) + ins[2 * n + 1][i].astype(f32)).astype(bf16)
                        for n in range(len(pairs))
                    ]
                )
            at = slice(j * depth, (j + 1) * depth)
            return (ins[0][i, at, :].astype(f32) + ins[1][i, at, :].astype(f32)).astype(bf16)

        for j in range(lanes):
            outs[2 * j][...] = total(0, j)

        def body(i, carry):
            for j in range(lanes):
                outs[2 * j + 1][i] = total(i, j)
            return carry

        lax.fori_loop(1, count, body, 0)

    outs = [((depth, width), bf16, False), ((count, depth, width), bf16, False)] * lanes
    ins = [(v, False) for pair in pairs for v in pair]
    out = call(kernel, ins, outs, [], 10**8, "merge", after=after, limit=SMALL)
    return out[0::2], out[1::2]


def add(a, blocks, i, after):
    def kernel(a_ref, b_ref, out_ref):
        out_ref[...] = (a_ref[...].astype(f32) + b_ref[i].astype(f32)).astype(bf16)

    outs = [(a.shape, bf16, False)]
    return call(kernel, [(a, False), (blocks, False)], outs, [], 10**8, "add", after=after, limit=SMALL)[0]


def hold(a, after):
    def kernel(a_ref, out_ref):
        out_ref[...] = a_ref[...]

    return call(kernel, [(a, False)], [(a.shape, a.dtype, False)], [], 10**8, "hold", after=after, limit=SMALL)[0]


DEEP = 4


def spread(pieces, shapes, blocks, begin, own, core, place, before, after):
    count, depth, width = blocks.shape
    deep = min(DEEP, count)

    def kernel(s_ref, block_ref, *refs):
        token_ref, held, sems = refs[-3:]
        outs = refs[len(refs) - 3 - len(shapes) : -3]
        token_ref[...] = jnp.zeros_like(token_ref)

        def copies(i):
            half, p = (s_ref[0], s_ref[1]) if own else (1 - s_ref[0], lax.rem(8 - s_ref[1], 8))
            b = lax.rem(p + 1 - begin - i + 16, 8)
            return [
                pltpu.make_async_copy(
                    held.at[(i % deep,) + source], outs[o].at[place], sems.at[i % deep, j]
                )
                for j, (source, o, place) in enumerate(pieces(half, b))
            ]

        for i in range(count):
            if i >= deep:
                for c in copies(i - deep):
                    c.wait()
            held[i % deep] = block_ref[i].astype(f32)
            for c in copies(i):
                c.start()
        for i in range(count - deep, count):
            for c in copies(i):
                c.wait()

    ins = [(jnp.stack([core, place]).astype(jnp.int32), False), (blocks, False)]
    aliases = {}
    for j, v in enumerate(before):
        aliases[len(ins)] = j
        ins.append((v, True))
    scratch = [
        pltpu.VMEM((deep, depth, width), f32),
        pltpu.SemaphoreType.DMA((deep, len(pieces(0, 0)))),
    ]
    outs = [(s, f32, True) for s in shapes] + [((8, 128), f32, False)]
    *outs, token = call(kernel, ins, outs, scratch, 10**8, "spread", aliases, after=after, limit=SMALL)
    return outs, token


def mlp_pieces(layer, layers, hidden, width):
    tall, wide = hidden // 16, width // 8

    def pieces(half, b):
        rows = pl.ds(pl.multiple_of(half * (hidden // 2) + b * tall, tall), tall)
        across_rows = pl.ds(pl.multiple_of(b * wide, wide), wide)
        columns = pl.ds(pl.multiple_of(half * (hidden // 2), hidden // 2), hidden // 2)
        return [
            ((slice(0, tall), slice(None)), 0, (layer, rows, slice(None))),
            ((slice(tall, tall + wide), slice(None)), 1, (layer, across_rows, columns)),
        ]

    return pieces, [(layers, hidden, width), (layers, width, hidden)]


def attention_pieces(layer, layers, local, width):
    tall, wide = local // 16, width // 16

    def pieces(half, b):
        rows = pl.ds(pl.multiple_of(half * (local // 2) + b * tall, tall), tall)
        deep = pl.ds(pl.multiple_of(half * (width // 2) + b * wide, wide), wide)
        out = []
        for j in range(2):
            columns = slice(j * width // 2, (j + 1) * width // 2)
            out.append(((slice(tall * j, tall * (j + 1)), slice(None)), 0, (layer, rows, columns)))
        for j in range(3):
            low = 2 * tall + wide * j
            out.append(((slice(low, low + wide), slice(None)), 1, (layer, j, deep, slice(None))))
        return out

    return pieces, [(layers, local, width), (layers, 3, width, local)]


def small_outputs(ends, begins, layers, width, core, place):
    row = ends[0][0].shape[1] - 16
    half_width = width // 2

    def kernel(s_ref, *refs):
        outs, held = refs[2 * len(ends) : 2 * len(ends) + 4], refs[2 * len(ends) + 4 : -1]
        gains, biases, times, norms = held

        def put(source, half, p):
            for b in range(5):
                slot = lax.rem(p + 1 - b + 16, 8)
                for n, begin in enumerate(begins):
                    ref = refs[2 * n + source]

                    @pl.when((slot >= begin) & (slot < begin + ref.shape[0]))
                    def _():
                        for j in range(2):
                            v = ref[slot - begin, row : row + 16, :].astype(f32)[j : j + 1, :]
                            at = slice(j * half_width, (j + 1) * half_width)
                            if b == 4:
                                times[half : half + 1, at] = v
                            else:
                                (gains, biases)[b // 2][half, b % 2 : b % 2 + 1, at] = v

        for c in range(2):

            @pl.when(s_ref[0] == c)
            def _():
                put(0, c, s_ref[1])
                put(1, 1 - c, 8 - s_ref[1])

        norms[0:1, :] = gains[layers - 1, 1:2, :]
        norms[1:2, :] = biases[layers - 1, 1:2, :]
        copies = [pltpu.make_async_copy(a, b, refs[-1].at[j]) for j, (a, b) in enumerate(zip(held, outs))]
        for c in copies:
            c.start()
        for c in copies:
            c.wait()

    shapes = [(layers, 2, width), (layers, 2, width), (layers, width), (2, width)]
    ins = [(jnp.stack([core, place]).astype(jnp.int32), False)] + [(v, False) for pair in ends for v in pair]
    scratch = [pltpu.VMEM(s, f32) for s in shapes] + [pltpu.SemaphoreType.DMA((4,))]
    return call(kernel, ins, [(s, f32, True) for s in shapes], scratch, 10**8, "small_outputs", limit=SMALL)


class Stream:
    def __init__(self, links, kind, layer, layers, groups, after, written):
        self.links, self.kind, self.written = links, kind, written
        self.steps = -2
        self.extra = []
        self.cuts = [(0, 5), (5, 8)] if kind == "attention" and layer == 0 else [(0, 8)]
        self.packed = []
        self.waits = not (kind == "attention" and layer == 0)
        self.lanes = LANES[kind][min(layer, 1)]
        self.core = lax.axis_index("dp") & 1
        self.p = links.ring_place()
        if kind == "mlp":
            send, self.blocks = mlp_gradients(*groups, self.core, self.p, after)
            self.layout = mlp_pieces(layer, layers, groups[0][0].shape[1], groups[1][0].shape[1])
        else:
            send, self.blocks = attention_gradients(*groups, self.core, self.p, after)
            self.layout = attention_pieces(layer, layers, groups[0][0].shape[1], groups[1][0].shape[1])
        self.raw = lax.ppermute(send, "dp", links.core_pairs)
        self.done = [[] for _ in range(self.lanes)]
        self.token = self.blocks

    def step(self, after):
        self.steps += 1
        if self.steps < 0:
            return []
        out = []
        if self.steps == 14:
            for lane, v in zip(self.done, self.raw):
                lane.append(v)
            if self.waits:
                return []
        if self.packed and len(self.packed[-1]) == 2 and not self.packed[-1][-1][1]:
            (_, peer), state = self.packed[-1][0], self.packed[-1][-1]
            state[1] = True
            out.append(self.write(peer, state[0], False, after))
        if self.steps == 15 + self.waits:
            return out
        for low, high in self.cuts:
            if self.steps == min(high + 7, 14 + self.waits):
                mine = pack([lane[low:high] for lane in self.done], after)
                peer = lax.ppermute(mine, "dp", self.links.core_pairs)
                out.append(self.write(mine, low, True, []))
                self.packed.append(((mine, peer), [low, False]))
        if self.steps >= 14:
            return out
        if self.steps == 0:
            now, self.blocks = merge([(self.blocks, self.raw)] + self.extra, self.lanes, after)
        elif self.steps < 8:
            now = [add(r, b, self.steps, after) for r, b in zip(self.raw, self.blocks)]
        else:
            now = [hold(r, after) for r in self.raw]
        if self.steps >= 7:
            for lane, v in zip(self.done, now):
                lane.append(v)
        self.raw = [lax.ppermute(v, "dp", self.links.ring_pairs) for v in now]
        return out + list(now)

    def write(self, blocks, begin, own, after):
        before = self.written.get(self.kind, [])
        self.written[self.kind], token = spread(
            *self.layout, blocks, begin, own, self.core, self.p, before, after
        )
        return token

    def going(self):
        return self.steps < 15 + self.waits


LANES = {"mlp": (2, 1), "attention": (1, 1)}


class Plain:
    def __init__(self, links, kind, layer, layers, groups, after, written):
        left, right, deep, *dps = [jnp.concatenate(g) for g in groups]
        out = [ein("ra,rb->ab", left, right)]
        if kind == "mlp":
            out.append(ein("ra,rb->ab", deep, dps[0]))
        else:
            out.append(jnp.stack([ein("ra,rb->ab", deep, d) for d in dps]))
        out = [lax.psum(v.astype(bf16), "dp").astype(f32) for v in out]
        if kind not in written:
            written[kind] = [jnp.zeros((layers,) + v.shape, f32) for v in out]
        written[kind] = [b.at[layer].set(v) for b, v in zip(written[kind], out)]
        self.token = after[0]

    def going(self):
        return False

def make_local(links):
    def local(
        tokens,
        time_index,
        time_table,
        norm_gain,
        norm_bias,
        w_qkv,
        w_out,
        w_up,
        w_down,
        time_weight,
        cotangent,
    ):
        rows, width = tokens.shape
        seq_here = time_index.shape[0]
        length = rows // seq_here
        layers = norm_gain.shape[0]
        local_width = w_out.shape[1]
        tables = rope_tables(length, local_width)
        parts = 2 if seq_here % 2 == 0 else 1
        own = rows // parts
        paired = links.tensor == 2
        wq = jnp.transpose(w_qkv, (0, 2, 1, 3))

        def group_rows(v, m, after=()):
            if paired:
                mine = v[m * own : (m + 1) * own]
                got = links.swap_tensor(hold(mine, after) if after else mine)
                return [(v, m * own, own), (got, 0, own)]
            v = links.gather_tensor(v[m * own : (m + 1) * own])
            return [(v, 0, v.shape[0])]

        heads = [group_rows(tokens, 0)]
        heads += [group_rows(tokens, m, [heads[-1][-1][0]]) for m in range(1, parts)]
        gs = []
        vectors = [norm_gain.reshape(2 * layers, width), norm_bias.reshape(2 * layers, width)]
        vectors += [time_weight, jnp.zeros((layers, width), f32)]
        vectors = jnp.concatenate(vectors)
        def times(after):
            if paired:
                held = hold(time_index.astype(f32)[None, :], after)
                index = jnp.concatenate([held, links.swap_tensor(held)], axis=1)[0].astype(jnp.int32)
            else:
                index = links.gather_tensor(time_index)
            rows_of = jnp.arange(time_table.shape[0], dtype=jnp.int32)
            onehot = (index[:, None] == rows_of[None, :]).astype(f32)
            return jnp.dot(onehot, time_table, precision=lax.Precision.HIGHEST)

        tau = None
        latest = []
        saved = [[None] * parts for _ in range(layers)]
        after = [[None] * parts for _ in range(layers)]
        for l in range(layers):
            for m in range(parts):
                x_near, part, *out = forward_attention(
                    l, m, length, paired, heads[m], tau, vectors, wq, w_out, tables, latest
                )
                latest = [part]
                if l > 0:
                    after[l - 1][m] = out.pop()
                if tau is None and m == parts - 1:
                    tau = times(latest)
                saved[l][m] = out
                heads[m] = (x_near, *links.start_sum(part))
            for m in range(parts):
                x1, part, *out = forward_mlp(l, paired, *heads[m], vectors, w_up, w_down, latest)
                latest = [part]
                heads[m] = (x1, part) if l == layers - 1 else (x1, *links.start_sum(part))
                saved[l][m] += out
                if l == layers - 1:
                    gs.append(group_rows(cotangent, m, [part] + [g[-1][0] for g in gs]))

        kind = Stream if links.ring else Plain
        streams = []
        small = []
        keep = lambda l, i: [s[i] for s in saved[l]]

        last, written = [], {}

        def step(also=()):
            before = list(also)
            for s in streams:
                if s.going():
                    before += s.step(list(last))
            return before

        def ran(out):
            last[:] = [out]

        gs_first = gs
        gs = list(gs)
        for l in reversed(range(layers)):
            g2s, gms, dus, sums = [None] * parts, [None] * parts, [None] * parts, [None] * parts
            gas, dps = [None] * parts, [None] * parts
            for m in range(parts):
                g2s[m], gms[m], dus[m], part, s = backward_mlp(
                    l, l == layers - 1, m, length, paired, gs[m], after[l][m], tau, vectors, saved[l][m][9],
                    w_up, w_down, step(latest),
                )
                latest = []
                ran(s)
                if l < layers - 1:
                    small.append((l + 1, (0, 2), s))
                    small.append((l, (None, None, 4), s))
                sums[m] = links.start_sum(part)

            def mlp_stream(also):
                groups = [keep(l, 8), gms, keep(l, 7), dus]
                streams.append(kind(links, "mlp", l, layers, groups, step(also), written))
                ran(streams[-1].token)

            if l > 0:
                mlp_stream([sums[0][1]])
            for m in range(parts):
                x, n1, q, k, v, att, x1 = saved[l][m][:7]
                g1, gas[m], dq, dk, dv, part, s = backward_attention(
                    l, length, paired, g2s[m], x1, *sums[m], vectors, q, k, v, wq, w_out, tables, step()
                )
                ran(s)
                small.append((l, (1, 3), s))
                dps[m] = (dq, dk, dv)
                gs[m] = (g1, x, *links.start_sum(part))
                if m == 0 and l == 0:
                    mlp_stream([sums[-1][1]])
            groups = [keep(l, 5), gas, keep(l, 1)] + [[d[j] for d in dps] for j in range(3)]
            streams.append(kind(links, "attention", l, layers, groups, step([gs[0][3]]), written))
            ran(streams[-1].token)
        final = streams[-1]
        own_here = own if paired else gs[0][1].shape[0]

        def send_last():
            for m in range(parts):
                x1, part = heads[m]
                held = hold(part, list(last)) if links.ring else part
                heads[m] = (x1, *links.start_sum(held), gs_first[m])
                heads[m] = (x1, part, heads[m][2], gs_first[m]) if paired else heads[m]

        def end_layers():
            inputs, s = input_gradient(0, paired, own_here, vectors, gs, list(last))
            small.append((0, (0, 2), s))
            result, s = last_layer(layers - 1, length, paired, own_here, tau, vectors, heads, list(last) + [s])
            small.append((layers - 1, (4,), s))
            return inputs, result

        send_last()
        if links.ring:
            last[:] = step()
            inputs, result = end_layers()
            send, kept = totals(small, layers, width, final.core, final.p, list(last))
            final.extra = [(kept, lax.ppermute(send, "dp", links.core_pairs))]
            final.steps -= 1
            while any(s.going() for s in streams):
                moving = [s for s in streams if s.steps < 13]
                ending = [s for s in streams if s.steps >= 13 and s.going()]
                now = []
                for s in moving:
                    now += s.step(list(last))
                rest = []
                for s in ending:
                    rest += s.step(now or list(last))
                last[:] = now + rest
            ends = [pair for pair, _ in final.packed]
            begins = [low for low, _ in final.cuts]
            gains, biases, times, norms = small_outputs(ends, begins, layers, width, final.core, final.p)
        else:
            inputs, result = end_layers()
            tiny = jnp.zeros((layers, 8, width), f32)
            for l, rows_of, s in small:
                for j, row in enumerate(rows_of):
                    if row is not None:
                        tiny = tiny.at[l, row].add(jnp.sum(s[8 * j : 8 * j + 8], axis=0))
            tiny = lax.psum(tiny, "dp")
            gains, biases, times = tiny[:, 0:2], tiny[:, 2:4], tiny[:, 4]
            norms = jnp.stack([gains[layers - 1, 1], biases[layers - 1, 1]])
        if not paired:
            t = lax.axis_index("tensor")
            cut = lambda v: jnp.concatenate(
                [
                    lax.dynamic_slice_in_dim(v, m * v.shape[0] // parts + t * own, own)
                    for m in range(parts)
                ]
            )
            result, inputs = cut(result), cut(inputs)
        return (
            result,
            inputs,
            gains,
            biases,
            jnp.transpose(written["attention"][1], (0, 2, 1, 3)),
            written["attention"][0],
            written["mlp"][1],
            written["mlp"][0],
            times,
            norms,
        )

    return local


def solution(mesh):
    links = Links(mesh.shape["dp"], mesh.shape["tensor"])
    token_spec = P(("dp", "tensor"), None)
    in_specs = (
        token_spec,
        P(("dp", "tensor")),
        P(),
        P(),
        P(),
        P(None, None, None, "tensor"),
        P(None, "tensor", None),
        P(None, None, "tensor"),
        P(None, "tensor", None),
        P(),
        token_spec,
    )
    out_specs = (
        token_spec,
        token_spec,
        P(),
        P(),
        P(None, None, None, "tensor"),
        P(None, "tensor", None),
        P(None, None, "tensor"),
        P(None, "tensor", None),
        P(),
        P(),
    )
    return jax.shard_map(
        make_local(links), mesh=mesh, in_specs=in_specs, out_specs=out_specs, check_vma=False
    )
```
